512 devices in a mesh: gz: 64 (over y_hi, x, z), af: 8 (over y_lo, core).
Axes of the slice: x: 4, y: 8 (y_hi: 2, y_lo: 4; y = y_hi * 4 + y_lo), z: 8, core: 2. Of those that a mesh axis runs over, the one named last changes fastest.
Arguments:
- inputs: bfloat16 [256, 64, 8, 128], P('af', 'gz'), may hold values from -6 to 6
- pre_acts: bfloat16 [256, 64, 8, 128], P('af', 'gz'), may hold values from -6 to 6
- out_grad: bfloat16 [256, 64, 8, 128], P('af', 'gz'), may hold values from -4 to 4
- weight_one: bfloat16 [256, 27, 256], P('af'), may hold values from -0.078125 to 0.078125
- weight_two: bfloat16 [256, 27, 256], P('af'), may hold values from -0.078125 to 0.078125
Outputs:
- input_grad: bfloat16 [256, 64, 8, 128], P('af', 'gz')
- filter_grad_one: float32 [27, 256, 256], P(None, 'gz', 'af')
- filter_grad_two: float32 [27, 256, 256], P(None, 'gz', 'af')
The draws below stay inside these ranges and needn't reach their ends.
All inputs are finite; a program needn't handle non-finite values.
Results may differ from the reference program's by a relative error of at most 0.0049.
Values may be sent and summed in bfloat16 or wider, within the bound.
A program may use at most 128 MiB of HBM per device.

```python
import jax
import jax.numpy as jnp
from jax import lax

C = 256
X = 8
Y = 128
NZ = 64


def block_scale(own_key, shape, split, low, high):
    def one(axis_at, blocks):
        steps = jax.random.uniform(jax.random.fold_in(jax.random.fold_in(own_key, 6), axis_at), (blocks,), jnp.float32, low / len(split), high / len(split))
        return jnp.repeat(jnp.exp(steps), shape[axis_at] // blocks).reshape((-1,) + (1,) * (len(shape) - axis_at - 1))

    factor_of = one(*split[0])
    for cut in split[1:]:
        factor_of = factor_of * one(*cut)
    return factor_of


def bell_draw(own_key, shape, width, limit, split=(), dtype=jnp.bfloat16):
    result = jax.random.normal(own_key, shape, jnp.float32) * width
    if len(split) > 0:
        result = block_scale(own_key, shape, split, -0.22, 0.18) * result
    return jnp.clip(result, min=-limit, max=limit).astype(dtype)


def setup_inputs(seed: int = 0) -> dict:
    key_list = jax.random.split(jax.random.key(seed), 6)
    inputs = bell_draw(key_list[0], (C, NZ, X, Y), 1.0, 6.0, ((0, 8), (1, 64)))
    pre_acts = bell_draw(key_list[1], (C, NZ, X, Y), 1.0, 6.0, ((0, 8), (1, 64)))
    out_grad = bell_draw(key_list[2], (C, NZ, X, Y), 0.5, 4.0, ((0, 8), (1, 64)))
    weight_one = bell_draw(key_list[3], (C, 27, C), (27 * C) ** -0.5, 0.078125, ((0, 8),))
    weight_two = bell_draw(key_list[4], (C, 27, C), (27 * C) ** -0.5, 0.078125, ((0, 8),))
    return dict(inputs=inputs, pre_acts=pre_acts, out_grad=out_grad, weight_one=weight_one, weight_two=weight_two)


tap_offsets = [(a, b, c) for a in (-1, 0, 1) for b in (-1, 0, 1) for c in (-1, 0, 1)]
contract_last = (((1,), (1,)), ((), ()))
contract_first = (((0,), (0,)), ((), ()))


def tap_cells(padded, offset, planes, height, across):
    return padded[:, 1 - offset[0]:1 - offset[0] + planes, 1 - offset[1]:1 - offset[1] + height, 1 - offset[2]:1 - offset[2] + across]


def pad_all(values):
    return jnp.pad(values, ((0, 0), (1, 1), (1, 1), (1, 1)))


def input_term(gradient, weight):
    channels, planes, height, across = gradient.shape
    padded = pad_all(gradient.astype(jnp.float32))
    summed = jnp.zeros((channels, planes * height * across), jnp.float32)
    for number, offset in enumerate(tap_offsets):
        shifted = tap_cells(padded, offset, planes, height, across).reshape(channels, -1)
        summed = summed + lax.dot_general(weight[:, number, :].astype(jnp.float32), shifted, contract_first, preferred_element_type=jnp.float32)
    return summed.reshape(channels, planes, height, across)


def filter_term(activation, gradient):
    channels, planes, height, across = gradient.shape
    flat_acts = activation.astype(jnp.float32).reshape(channels, -1)
    padded = pad_all(gradient.astype(jnp.float32))
    columns = []
    for offset in tap_offsets:
        shifted = tap_cells(padded, offset, planes, height, across).reshape(channels, -1)
        columns.append(lax.dot_general(flat_acts, shifted, contract_last, preferred_element_type=jnp.float32))
    return jnp.stack(columns, axis=0)


def reference(inputs, pre_acts, out_grad, weight_one, weight_two):
    pre_float = pre_acts.astype(jnp.float32)
    activation = jnp.where(pre_float > 0, pre_float, 0.3 * pre_float).astype(jnp.bfloat16)
    grad_two = filter_term(activation, out_grad)
    slopes = jnp.where(pre_float > 0, jnp.float32(1.0), jnp.float32(0.3))
    mid_grad = (input_term(out_grad, weight_two) * slopes).astype(jnp.bfloat16)
    grad_one = filter_term(inputs, mid_grad)
    return input_term(mid_grad, weight_one).astype(jnp.bfloat16), grad_one, grad_two
```

```python
import functools

import jax
import jax.numpy as jnp
from jax import lax
from jax.experimental import pallas as pl
from jax.experimental.pallas import tpu as pltpu
from jax.sharding import PartitionSpec as P

MESH = pl.DeviceIdType.MESH
BF = jnp.bfloat16
F32 = jnp.float32
ZRUN = 8
XRUN = 4
CUT = 384
TAPS = 27
ACROSS = 128
last_dims = (((1,), (1,)), ((), ()))


def kernel(
    slabs, groups, own, height, cut,
    in_hbm, pre_hbm, og_hbm, w1_hbm, w2_hbm,
    ig_ref, f1_ref, f2_ref,
    in_ref, pre_ref, og_ref, w1_ref, w2_ref,
    rel, slope, field, G, WT, U, UP, PS, PR, SB, SR,
    KF, KS, KR, QS, QR,
    XF0, XS0, XR0, ZS0, ZR0, HS0, HR0,
    XF1, XS1, XR1, ZS1, ZR1, HS1, HR1,
    load_s, halo_s, halo_r, ag_s, ag_r, px_s, px_r, y_s, y_r, k_s, k_r, q_s, q_r,
    xs, xr, zs, zr, hs, hr,
):
    cells = height * ACROSS
    chips = groups // 2
    runs = slabs // ZRUN
    halves = runs // XRUN
    rows = groups * own
    share = rows // slabs
    k = lax.axis_index("gz")
    me = lax.axis_index("af")
    chip, core = me // 2, me % 2
    run, z = k // ZRUN, k % ZRUN
    hi, xi = run // XRUN, run % XRUN
    sibling = {"af": chip * 2 + (1 - core)}
    chip_at = lambda d: {"af": lax.rem(chip + d, chips) * 2 + core}
    z_at = lambda d: {"gz": run * ZRUN + lax.rem(z + d, ZRUN)}
    run_at = lambda d: {"gz": lax.rem(run + d, runs) * ZRUN + z}
    x_at = lambda d: {"gz": (hi * XRUN + lax.rem(xi + d, XRUN)) * ZRUN + z}
    hi_at = lambda d: {"gz": (lax.rem(hi + d, halves) * XRUN + xi) * ZRUN + z}
    above = {"gz": lax.rem(k + 1, slabs)}
    below = {"gz": lax.rem(k + slabs - 1, slabs)}
    filled = TAPS * own
    wide = G.shape[0]
    inner = slice(ACROSS, ACROSS + cells)
    columns = ((0, wide), (cut, wide))
    xbufs = ((XF0, XS0, XR0, ZS0, ZR0, HS0, HR0), (XF1, XS1, XR1, ZS1, ZR1, HS1, HR1))

    peers = [sibling, above, below]
    peers += [chip_at(d) for d in range(1, chips)]
    peers += [z_at(d) for d in range(1, ZRUN)]
    peers += [run_at(d) for d in range(1, runs)]
    barrier = pltpu.get_barrier_semaphore()
    for peer in peers:
        pl.semaphore_signal(barrier, inc=1, device_id=peer, device_id_type=MESH)

    loads = []
    for i, (src, dst) in enumerate(
        ((og_hbm, og_ref), (pre_hbm, pre_ref), (w2_hbm, w2_ref), (in_hbm, in_ref), (w1_hbm, w1_ref))
    ):
        loads.append(pltpu.make_async_copy(src, dst, load_s.at[i]))
        loads[-1].start()

    started = []

    def remote(src, dst, s, r, to):
        return pltpu.make_async_remote_copy(
            src_ref=src, dst_ref=dst, send_sem=s, recv_sem=r, device_id=to, device_id_type=MESH
        )

    def send(src, dst, s, r, to):
        copy = remote(src, dst, s, r, to)
        copy.start()
        started.append(copy)
        return copy

    def planes_of(ref):
        rel[...] = ref[...].astype(F32).reshape(own * height, ACROSS)
        return [rel[pl.ds(x, own, stride=height), :] for x in range(height)]

    def at_x(x):
        return slice(x * ACROSS, (x + 1) * ACROSS)

    def halo_copies(l):
        up = remote(field.at[l, 1], field.at[l, 0], halo_s.at[l, 0], halo_r.at[l, 0], above)
        down = remote(field.at[l, 1], field.at[l, 2], halo_s.at[l, 1], halo_r.at[l, 1], below)
        return up, down

    def halo_send(l):
        up, down = halo_copies(l)
        pl.when(k < slabs - 1)(up.start)
        pl.when(k > 0)(down.start)

    def halo_wait(l):
        up, down = halo_copies(l)
        pl.when(k > 0)(up.wait_recv)
        pl.when(k < slabs - 1)(down.wait_recv)

    def halo_done(l):
        up, down = halo_copies(l)
        pl.when(k < slabs - 1)(up.wait_send)
        pl.when(k > 0)(down.wait_send)

    def gather_start(l):
        mine = U.at[l, me]
        found = [
            send(mine, mine, ag_s.at[l, d], ag_r.at[l, d], chip_at(d)) for d in range(1, chips)
        ]
        found.append(send(mine, mine, ag_s.at[l, 0], ag_r.at[l, 0], sibling))
        return found

    def gather_forward(l, found):
        onward = [found[-1]]
        for d in range(1, chips):
            found[d - 1].wait_recv()
            block = U.at[l, lax.rem(chip + chips - d, chips) * 2 + core]
            onward.append(
                send(block, block, ag_s.at[l, chips - 1 + d], ag_r.at[l, chips - 1 + d], sibling)
            )
        return onward

    def gather_finish(onward):
        for copy in onward:
            copy.wait_recv()

    def reorder(l):
        low, mid, top = share.bit_length() - 1, runs.bit_length() - 1, ZRUN.bit_length() - 1
        to_row = lax.broadcasted_iota(jnp.int32, (rows, rows), 0)
        from_row = lax.broadcasted_iota(jnp.int32, (rows, rows), 1)
        wanted = (
            (((to_row >> low) & (runs - 1)) << (low + top))
            | ((to_row >> (low + mid)) << low)
            | (to_row & (share - 1))
        )
        move = jnp.where(from_row == wanted, 1.0, 0.0).astype(BF)
        for n in range(0, cells, 256):
            block = U[l, :, :, n : n + 256].reshape(rows, 256)
            UP[:, n : n + 256] = jnp.dot(move, block, preferred_element_type=F32).astype(BF)

    def turn(l, w_ref):
        full = jnp.concatenate([w_ref[...], jnp.zeros((wide - filled, rows), BF)], axis=0).T
        for g in range(groups):
            WT[l, g % 2, (g // 2) * own : (g // 2 + 1) * own, :] = full[g * own : (g + 1) * own, :]

    lane = lax.broadcasted_iota(jnp.int32, (own, ACROSS), 1)
    number = lambda a, b, c: 9 * (a + 1) + 3 * (b + 1) + (c + 1)
    tap_rows = lambda t: slice(t * own, (t + 1) * own)

    def build(l, p):
        a = 1 - p

        def step(x, carry):
            v = field[l, p, :, pl.ds(pl.multiple_of(x * ACROSS, ACROSS), ACROSS)].astype(F32)
            for c in (-1, 0, 1):
                if c == 0:
                    s = v
                else:
                    edge = 0 if c == 1 else ACROSS - 1
                    s = jnp.where(lane == edge, 0.0, pltpu.roll(v, c % ACROSS, 1))
                s = s.astype(BF)
                for b in (-1, 0, 1):
                    at = pl.ds(pl.multiple_of((x + b + 1) * ACROSS, ACROSS), ACROSS)
                    G[tap_rows(number(a, b, c)), at] = s
            return carry

        lax.fori_loop(0, height, step, 0)

    def grad_product(l, half, which):
        for n in range(0, cells, 256):
            PS[l, half, :, n : n + 256] = jnp.dot(
                WT[l, which], G[:, ACROSS + n : ACROSS + n + 256], preferred_element_type=F32
            )

    def grad_first(l):
        grad_product(l, 0, 1 - core)
        copy = send(PS.at[l, 0], PR.at[l], px_s.at[l], px_r.at[l], sibling)
        grad_product(l, 1, core)
        return copy

    def grad_second(l, copy):
        copy.wait_recv()
        for j in range(chips):
            at = slice(j * own, (j + 1) * own)
            total = PS[l, 1, at, :] + PR[l, at, :]
            PS[l, 1, at, :] = total
            SB[l, j] = total.astype(BF)
        return [
            send(
                SB.at[l, lax.rem(chip + d, chips)], SR.at[l, d - 1],
                y_s.at[l, d - 1], y_r.at[l, d - 1], chip_at(d),
            )
            for d in range(1, chips)
        ]

    def grad_last(l, copies):
        for copy in copies:
            copy.wait_recv()
        mine = pl.ds(pl.multiple_of(chip * own, own), own)

        def at(x):
            total = PS[l, 1, mine, at_x(x)]
            for d in range(chips - 1):
                total = total + SR[l, d, :, at_x(x)].astype(F32)
            return total

        return at

    def z_first():
        for n in range(0, cut, 256):
            size = min(256, cut - n)
            block = lax.dot_general(
                UP[...], G[n : n + size, inner], last_dims, preferred_element_type=F32
            ).reshape(ZRUN, runs * share, size)
            KF[:, :, n : n + size] = block
            KS[:, :, n : n + size] = block.astype(BF)
        return [
            send(KS.at[lax.rem(z + d, ZRUN)], KR.at[d - 1], k_s.at[d - 1], k_r.at[d - 1], z_at(d))
            for d in range(1, ZRUN)
        ]

    def z_first_then(copies):
        for copy in copies:
            copy.wait_recv()
        for n in range(0, cut, 128):
            at = slice(n, n + 128)
            total = KF[z, :, at]
            for d in range(ZRUN - 1):
                total = total + KR[d, :, at].astype(F32)
            for j in range(runs):
                QS[j, :, at] = total[j * share : (j + 1) * share, :]
        return [
            send(QS.at[lax.rem(run + d, runs)], QR.at[d - 1], q_s.at[d - 1], q_r.at[d - 1], run_at(d))
            for d in range(1, runs)
        ]

    def z_first_last(copies, out_ref):
        for copy in copies:
            copy.wait_recv()
        total = QS[run]
        for d in range(runs - 1):
            total = total + QR[d]
        out_ref[:, :cut] = total

    def x_first(l):
        start, stop = columns[l]
        XF, XS, XR = xbufs[l][:3]
        for n in range(start, stop, 256):
            size = min(256, stop - n)
            at = slice(n - start, n - start + size)
            block = lax.dot_general(
                U[l].reshape(rows, cells), G[n : n + size, inner], last_dims,
                preferred_element_type=F32,
            )
            for h in range(halves):
                for x in range(XRUN):
                    j = (h * XRUN + x) * ZRUN * share
                    part = block[j : j + ZRUN * share, :]
                    XF[x, h, :, at] = part
                    XS[x, h, :, at] = part.astype(BF)
        return [
            send(
                XS.at[lax.rem(xi + d, XRUN)], XR.at[d - 1],
                xs.at[l, d - 1], xr.at[l, d - 1], x_at(d),
            )
            for d in range(1, XRUN)
        ]

    def x_first_then(l, copies):
        start, stop = columns[l]
        XF, XS, XR, ZS, ZR = xbufs[l][:5]
        for copy in copies:
            copy.wait_recv()
        for n in range(0, stop - start, 128):
            at = slice(n, n + 128)
            for h in range(halves):
                total = XF[xi, h, :, at]
                for d in range(XRUN - 1):
                    total = total + XR[d, h, :, at].astype(F32)
                for j in range(ZRUN):
                    ZS[j, h * share : (h + 1) * share, at] = total[j * share : (j + 1) * share, :]
        return [
            send(
                ZS.at[lax.rem(z + d, ZRUN)], ZR.at[d - 1],
                zs.at[l, d - 1], zr.at[l, d - 1], z_at(d),
            )
            for d in range(1, ZRUN)
        ]

    def x_first_pair(l, copies):
        ZS, ZR, HS, HR = xbufs[l][3:]
        for copy in copies:
            copy.wait_recv()
        total = ZS[z]
        for d in range(ZRUN - 1):
            total = total + ZR[d]
        for h in range(halves):
            HS[h] = total[h * share : (h + 1) * share, :]
        return [
            send(
                HS.at[lax.rem(hi + d, halves)], HR.at[d - 1],
                hs.at[l, d - 1], hr.at[l, d - 1], hi_at(d),
            )
            for d in range(1, halves)
        ]

    def x_first_last(l, copies, out_ref):
        start, stop = columns[l]
        HS, HR = xbufs[l][5:]
        for copy in copies:
            copy.wait_recv()
        total = HS[hi]
        for d in range(halves - 1):
            total = total + HR[d]
        out_ref[:, start:stop] = total

    loads[0].wait()
    for x, v in enumerate(planes_of(og_ref)):
        field[0, 1, :, at_x(x)] = v.astype(BF)
    loads[1].wait()
    for x, v in enumerate(planes_of(pre_ref)):
        slope[:, at_x(x)] = jnp.where(v > 0, jnp.float32(1.0), jnp.float32(0.3))
        U[0, me, :, at_x(x)] = jnp.where(v > 0, v, 0.3 * v).astype(BF)

    @pl.when(k == 0)
    def _():
        for l in range(2):
            field[l, 0] = jnp.zeros((own, cells), BF)

    @pl.when(k == slabs - 1)
    def _():
        for l in range(2):
            field[l, 2] = jnp.zeros((own, cells), BF)

    pl.semaphore_wait(barrier, len(peers))
    halo_send(0)
    gather_act = gather_start(0)

    none = jnp.zeros((own, ACROSS), BF)
    for a in (-1, 0, 1):
        for c in (-1, 0, 1):
            G[tap_rows(number(a, 1, c)), at_x(1)] = none
            G[tap_rows(number(a, -1, c)), at_x(height)] = none
    if wide > filled:
        G[filled:, :] = jnp.zeros((wide - filled, G.shape[1]), BF)

    build(0, 1)
    loads[2].wait()
    turn(0, w2_ref)
    halo_wait(0)
    build(0, 0)
    build(0, 2)
    pair = grad_first(0)
    loads[3].wait()
    for x, v in enumerate(planes_of(in_ref)):
        U[1, me, :, at_x(x)] = v.astype(BF)
    parts = grad_second(0, pair)
    loads[4].wait()
    turn(1, w1_ref)
    onward = gather_forward(0, gather_act)
    gather_finish(onward)
    two = x_first(0)
    total_at = grad_last(0, parts)
    for x in range(height):
        field[1, 1, :, at_x(x)] = (total_at(x) * slope[:, at_x(x)]).astype(BF)
    halo_send(1)
    gather_in = gather_start(1)
    build(1, 1)
    halo_wait(1)
    build(1, 0)
    build(1, 2)
    pair = grad_first(1)
    parts = grad_second(1, pair)
    two = x_first_then(0, two)
    onward = gather_forward(1, gather_in)
    gather_finish(onward)
    reorder(1)
    one_z = z_first()
    one_x = x_first(1)
    two = x_first_pair(0, two)
    total_at = grad_last(1, parts)
    for x in range(height):
        rel[pl.ds(x, own, stride=height), :] = total_at(x)
    ig_ref[...] = rel[...].reshape(own, height, ACROSS).astype(BF)
    one_x = x_first_then(1, one_x)
    one_z = z_first_then(one_z)
    x_first_last(0, two, f2_ref)
    one_x = x_first_pair(1, one_x)
    z_first_last(one_z, f1_ref)
    x_first_last(1, one_x, f1_ref)
    halo_done(0)
    halo_done(1)
    for copy in started:
        copy.wait_send()


def body(slabs, groups, inputs, pre_acts, out_grad, weight_one, weight_two):
    own, planes, height, across = out_grad.shape
    channels = weight_one.shape[2]
    cells = height * across
    chips = groups // 2
    runs = slabs // ZRUN
    halves = runs // XRUN
    share = channels // slabs
    wide = -(-TAPS * own // 128) * 128
    cut = CUT
    flat = lambda v: v.reshape(own, height, across)
    taps = lambda w: jnp.transpose(w, (1, 0, 2)).reshape(TAPS * own, channels)
    vmem = pl.BlockSpec(memory_space=pltpu.VMEM)
    hbm = pl.BlockSpec(memory_space=pltpu.HBM)
    scratch = [pltpu.VMEM((own, height, across), BF)] * 3
    scratch += [pltpu.VMEM((TAPS * own, channels), BF)] * 2
    scratch += [
        pltpu.VMEM((own * height, across), F32),
        pltpu.VMEM((own, cells), F32),
        pltpu.VMEM((2, 3, own, cells), BF),
        pltpu.VMEM((wide, cells + 2 * across), BF),
        pltpu.VMEM((2, 2, chips * own, wide), BF),
        pltpu.VMEM((2, groups, own, cells), BF),
        pltpu.VMEM((channels, cells), BF),
        pltpu.VMEM((2, 2, chips * own, cells), F32),
        pltpu.VMEM((2, chips * own, cells), F32),
        pltpu.VMEM((2, chips, own, cells), BF),
        pltpu.VMEM((2, chips - 1, own, cells), BF),
        pltpu.VMEM((ZRUN, runs * share, cut), F32),
        pltpu.VMEM((ZRUN, runs * share, cut), BF),
        pltpu.VMEM((ZRUN - 1, runs * share, cut), BF),
        pltpu.VMEM((runs, share, cut), F32),
        pltpu.VMEM((runs - 1, share, cut), F32),
    ]
    for width in (wide, wide - cut):
        scratch += [
            pltpu.VMEM((XRUN, halves, ZRUN * share, width), F32),
            pltpu.VMEM((XRUN, halves, ZRUN * share, width), BF),
            pltpu.VMEM((XRUN - 1, halves, ZRUN * share, width), BF),
            pltpu.VMEM((ZRUN, halves * share, width), F32),
            pltpu.VMEM((ZRUN - 1, halves * share, width), F32),
            pltpu.VMEM((halves, share, width), F32),
            pltpu.VMEM((halves - 1, share, width), F32),
        ]
    scratch.append(pltpu.SemaphoreType.DMA((5,)))
    for shape in (
        (2, 2), (2, 2 * chips - 1), (2,), (2, chips - 1), (ZRUN - 1,), (runs - 1,),
        (2, XRUN - 1), (2, ZRUN - 1), (2, halves - 1),
    ):
        scratch += [pltpu.SemaphoreType.DMA(shape), pltpu.SemaphoreType.DMA(shape)]
    input_grad, one, two = pl.pallas_call(
        functools.partial(kernel, slabs, groups, own, height, cut),
        out_shape=[
            jax.ShapeDtypeStruct((own, height, across), BF),
            jax.ShapeDtypeStruct((share, wide), F32),
            jax.ShapeDtypeStruct((share, wide), F32),
        ],
        in_specs=[hbm] * 5,
        out_specs=[vmem] * 3,
        scratch_shapes=scratch,
        compiler_params=pltpu.CompilerParams(
            collective_id=0, has_side_effects=True, vmem_limit_bytes=60 * 1024 * 1024
        ),
        name="conv_back",
    )(flat(inputs), flat(pre_acts), flat(out_grad), taps(weight_one), taps(weight_two))

    def filters(v):
        return jnp.transpose(v[:, : TAPS * own].reshape(share, TAPS, own), (1, 0, 2))

    return input_grad.reshape(own, planes, height, across), filters(one), filters(two)


def solution(mesh):
    in_specs = (
        P("af", "gz", None, None),
        P("af", "gz", None, None),
        P("af", "gz", None, None),
        P("af", None, None),
        P("af", None, None),
    )
    out_specs = (P("af", "gz", None, None), P(None, "gz", "af"), P(None, "gz", "af"))
    return jax.shard_map(
        functools.partial(body, mesh.shape["gz"], mesh.shape["af"]),
        mesh=mesh, in_specs=in_specs, out_specs=out_specs, check_vma=False,
    )
```

```python
import functools

import jax
import jax.numpy as jnp
from jax import lax
from jax.experimental import pallas as pl
from jax.experimental.pallas import tpu as pltpu
from jax.sharding import PartitionSpec as P

MESH = pl.DeviceIdType.MESH
BF = jnp.bfloat16
F32 = jnp.float32
ZRUN = 8
XRUN = 4
CUTS = (256, 512)
PIECES = 4
ORDER = (0, -1, 1)
TAPS = 27
ACROSS = 128
last_dims = (((1,), (1,)), ((), ()))


def kernel(
    slabs, groups, own, height, cuts,
    in_hbm, pre_hbm, og_hbm, w1_hbm, w2_hbm,
    ig_ref, f1_ref, f2_ref,
    in_ref, pre_ref, og_ref, w1_ref, w2_ref,
    rel, slope, field, G, WT, U, UP, PS, PR, SB, SR,
    KF0, KS0, KR0, QS0, QR0,
    KF1, KS1, KR1, QS1, QR1,
    XF0, XS0, XR0, ZF0, ZS0, ZR0, HS0, HR0,
    XF1, XS1, XR1, ZF1, ZS1, ZR1, HS1, HR1,
    load_s, halo_s, halo_r, ag_s, ag_r, px_s, px_r, y_s, y_r, k_s, k_r, q_s, q_r,
    xs, xr, zs, zr, hs, hr,
):
    cells = height * ACROSS
    chips = groups // 2
    runs = slabs // ZRUN
    halves = runs // XRUN
    rows = groups * own
    share = rows // slabs
    k = lax.axis_index("gz")
    me = lax.axis_index("af")
    chip, core = me // 2, me % 2
    run, z = k // ZRUN, k % ZRUN
    hi, xi = run // XRUN, run % XRUN
    sibling = {"af": chip * 2 + (1 - core)}
    chip_at = lambda d: {"af": lax.rem(chip + d, chips) * 2 + core}
    z_at = lambda d: {"gz": run * ZRUN + lax.rem(z + d, ZRUN)}
    run_at = lambda d: {"gz": lax.rem(run + d, runs) * ZRUN + z}
    x_at = lambda d: {"gz": (hi * XRUN + lax.rem(xi + d, XRUN)) * ZRUN + z}
    hi_at = lambda d: {"gz": (lax.rem(hi + d, halves) * XRUN + xi) * ZRUN + z}
    above = {"gz": lax.rem(k + 1, slabs)}
    below = {"gz": lax.rem(k + slabs - 1, slabs)}
    filled = TAPS * own
    wide = G.shape[0]
    inner = slice(ACROSS, ACROSS + cells)
    part = cells // PIECES
    step = height // PIECES
    place = k % (ZRUN * XRUN)
    edge = (place == 0) | (place == ZRUN * XRUN - 1)
    crossed = (place == ZRUN - 1) | (place == ZRUN * (XRUN - 1))
    columns = ((0, wide), (cuts[-1], wide))
    zbufs = ((KF0, KS0, KR0, QS0, QR0), (KF1, KS1, KR1, QS1, QR1))
    xbufs = ((XF0, XS0, XR0, ZF0, ZS0, ZR0, HS0, HR0), (XF1, XS1, XR1, ZF1, ZS1, ZR1, HS1, HR1))

    peers = [sibling, above, below]
    peers += [chip_at(d) for d in range(1, chips)]
    peers += [z_at(d) for d in range(1, ZRUN)]
    peers += [run_at(d) for d in range(1, runs)]
    barrier = pltpu.get_barrier_semaphore()
    for peer in peers:
        pl.semaphore_signal(barrier, inc=1, device_id=peer, device_id_type=MESH)

    loads = []
    for i, (src, dst) in enumerate(
        ((og_hbm, og_ref), (pre_hbm, pre_ref), (w2_hbm, w2_ref), (in_hbm, in_ref), (w1_hbm, w1_ref))
    ):
        loads.append(pltpu.make_async_copy(src, dst, load_s.at[i]))
        loads[-1].start()

    started = []

    def remote(src, dst, s, r, to):
        return pltpu.make_async_remote_copy(
            src_ref=src, dst_ref=dst, send_sem=s, recv_sem=r, device_id=to, device_id_type=MESH
        )

    def send(src, dst, s, r, to):
        copy = remote(src, dst, s, r, to)
        copy.start()
        started.append(copy)
        return copy

    def planes_of(ref):
        rel[...] = ref[...].astype(F32).reshape(own * height, ACROSS)
        return [rel[pl.ds(x, own, stride=height), :] for x in range(height)]

    def at_x(x):
        return slice(x * ACROSS, (x + 1) * ACROSS)

    def halo_copies(l, q):
        own_plane, low, high = (field.at[l, p, q] for p in (1, 0, 2))
        up = remote(own_plane, low, halo_s.at[l, q, 0], halo_r.at[l, q, 0], above)
        down = remote(own_plane, high, halo_s.at[l, q, 1], halo_r.at[l, q, 1], below)
        return up, down

    def halo_send(l, q):
        up, down = halo_copies(l, q)
        pl.when(k < slabs - 1)(up.start)
        pl.when(k > 0)(down.start)

    def halo_wait(l, q):
        up, down = halo_copies(l, q)
        pl.when(k > 0)(up.wait_recv)
        pl.when(k < slabs - 1)(down.wait_recv)

    def halo_done(l, q):
        up, down = halo_copies(l, q)
        pl.when(k < slabs - 1)(up.wait_send)
        pl.when(k > 0)(down.wait_send)

    def gather_copies(l):
        mine = U.at[l, me]
        found = [
            remote(mine, mine, ag_s.at[l, d], ag_r.at[l, d], chip_at(d)) for d in range(1, chips)
        ]
        found.append(remote(mine, mine, ag_s.at[l, 0], ag_r.at[l, 0], sibling))
        return found

    def gather_start(l, found, when):
        @pl.when(when)
        def _():
            for copy in found:
                copy.start()

    def gather_forward(l, found):
        started.extend(found)
        onward = [found[-1]]
        for d in range(1, chips):
            found[d - 1].wait_recv()
            block = U.at[l, lax.rem(chip + chips - d, chips) * 2 + core]
            onward.append(
                send(block, block, ag_s.at[l, chips - 1 + d], ag_r.at[l, chips - 1 + d], sibling)
            )
        return onward

    def gather_finish(onward):
        for copy in onward:
            copy.wait_recv()

    def reorder(l):
        low, mid, top = share.bit_length() - 1, runs.bit_length() - 1, ZRUN.bit_length() - 1
        to_row = lax.broadcasted_iota(jnp.int32, (rows, rows), 0)
        from_row = lax.broadcasted_iota(jnp.int32, (rows, rows), 1)
        wanted = (
            (((to_row >> low) & (runs - 1)) << (low + top))
            | ((to_row >> (low + mid)) << low)
            | (to_row & (share - 1))
        )
        move = jnp.where(from_row == wanted, 1.0, 0.0).astype(BF)
        for n in range(0, cells, 256):
            block = U[l, :, :, n : n + 256].reshape(rows, 256)
            UP[:, n : n + 256] = jnp.dot(move, block, preferred_element_type=F32).astype(BF)

    def turn(l, w_ref):
        third = filled // 3
        blocks = [w_ref[(a + 1) * third : (a + 2) * third, :] for a in ORDER]
        full = jnp.concatenate(blocks + [jnp.zeros((wide - filled, rows), BF)], axis=0).T
        for g in range(groups):
            WT[l, g % 2, (g // 2) * own : (g // 2 + 1) * own, :] = full[g * own : (g + 1) * own, :]

    lane = lax.broadcasted_iota(jnp.int32, (own, ACROSS), 1)
    number = lambda a, b, c: 9 * ORDER.index(a) + 3 * (b + 1) + (c + 1)
    tap_rows = lambda t: slice(t * own, (t + 1) * own)

    def build(l, p, q):
        a = 1 - p
        for x in range(q * step, (q + 1) * step):
            v = field[l, p, q, :, at_x(x - q * step)].astype(F32)
            for c in (-1, 0, 1):
                if c == 0:
                    s = v
                else:
                    edge = 0 if c == 1 else ACROSS - 1
                    s = jnp.where(lane == edge, 0.0, pltpu.roll(v, c % ACROSS, 1))
                s = s.astype(BF)
                for b in (-1, 0, 1):
                    if 0 <= x + b < height:
                        G[tap_rows(number(a, b, c)), at_x(x + b + 1)] = s

    def grad_product(l, half, which, q):
        at = slice(ACROSS + q * part, ACROSS + (q + 1) * part)
        PS[l, half, q] = jnp.dot(WT[l, which], G[:, at], preferred_element_type=F32)

    def grad_first(l, q):
        grad_product(l, 0, 1 - core, q)
        copy = send(PS.at[l, 0, q], PR.at[l, q], px_s.at[l, q], px_r.at[l, q], sibling)
        grad_product(l, 1, core, q)
        return copy

    def grad_second(l, q, copy):
        copy.wait_recv()
        for j in range(chips):
            at = slice(j * own, (j + 1) * own)
            total = PS[l, 1, q, at, :] + PR[l, q, at, :]
            PS[l, 1, q, at, :] = total
            SB[l, q, j] = total.astype(BF)
        return [
            send(
                SB.at[l, q, lax.rem(chip + d, chips)], SR.at[l, q, d - 1],
                y_s.at[l, q, d - 1], y_r.at[l, q, d - 1], chip_at(d),
            )
            for d in range(1, chips)
        ]

    def grad_last(l, q, found):
        for copy in found:
            copy.wait_recv()
        mine = pl.ds(pl.multiple_of(chip * own, own), own)
        total = PS[l, 1, q, mine, :]
        for d in range(chips - 1):
            total = total + SR[l, q, d].astype(F32)
        return total

    def by_tap(total, start, out_ref):
        for i in range(total.shape[1] // own):
            block = start // own + i
            if block < TAPS:
                out_ref[9 * (ORDER[block // 9] + 1) + block % 9] = total[:, i * own : (i + 1) * own]

    zcolumns = ((0, cuts[0]), (cuts[0], cuts[1]))

    def z_first(i):
        KF, KS, KR = zbufs[i][:3]
        start, stop = zcolumns[i]
        for n in range(start, stop, 256):
            size = min(256, stop - n)
            at = slice(n - start, n - start + size)
            block = lax.dot_general(
                UP[...], G[n : n + size, inner], last_dims, preferred_element_type=F32
            ).reshape(ZRUN, runs * share, size)
            KF[:, :, at] = block
            KS[:, :, at] = block.astype(BF)
        return [
            send(
                KS.at[lax.rem(z + d, ZRUN)], KR.at[d - 1],
                k_s.at[i, d - 1], k_r.at[i, d - 1], z_at(d),
            )
            for d in range(1, ZRUN)
        ]

    def z_first_then(i, copies):
        KF, KS, KR, QS, QR = zbufs[i]
        for copy in copies:
            copy.wait_recv()
        for n in range(0, KF.shape[2], 128):
            at = slice(n, n + 128)
            total = KF[z, :, at]
            for d in range(ZRUN - 1):
                total = total + KR[d, :, at].astype(F32)
            for j in range(runs):
                QS[j, :, at] = total[j * share : (j + 1) * share, :]
        return [
            send(
                QS.at[lax.rem(run + d, runs)], QR.at[d - 1],
                q_s.at[i, d - 1], q_r.at[i, d - 1], run_at(d),
            )
            for d in range(1, runs)
        ]

    def z_first_last(i, copies, out_ref):
        QS, QR = zbufs[i][3:]
        for copy in copies:
            copy.wait_recv()
        total = QS[run]
        for d in range(runs - 1):
            total = total + QR[d]
        by_tap(total, zcolumns[i][0], out_ref)

    def x_first(l):
        start, stop = columns[l]
        XF, XS, XR = xbufs[l][:3]
        for n in range(start, stop, 256):
            size = min(256, stop - n)
            at = slice(n - start, n - start + size)
            block = lax.dot_general(
                U[l].reshape(rows, cells), G[n : n + size, inner], last_dims,
                preferred_element_type=F32,
            )
            for h in range(halves):
                for x in range(XRUN):
                    j = (h * XRUN + x) * ZRUN * share
                    part = block[j : j + ZRUN * share, :]
                    XF[x, h, :, at] = part
                    XS[x, h, :, at] = part.astype(BF)
        return [
            send(
                XS.at[lax.rem(xi + d, XRUN)], XR.at[d - 1],
                xs.at[l, d - 1], xr.at[l, d - 1], x_at(d),
            )
            for d in range(1, XRUN)
        ]

    def x_first_then(l, copies):
        start, stop = columns[l]
        XF, XS, XR, ZF, ZS, ZR = xbufs[l][:6]
        eight = halves * share
        for copy in copies:
            copy.wait_recv()
        for n in range(0, stop - start, 128):
            at = slice(n, n + 128)
            fold, to = divmod(n, ZS.shape[2])
            to = slice(to, to + 128)
            for h in range(halves):
                total = XF[xi, h, :, at]
                for d in range(XRUN - 1):
                    total = total + XR[d, h, :, at].astype(F32)
                first = fold * eight + h * share
                for j in range(ZRUN):
                    ZF[j, first : first + share, to] = total[j * share : (j + 1) * share, :]
        for j in range(ZRUN):
            ZS[j] = ZF[j].astype(BF)
        return [
            send(
                ZS.at[lax.rem(z + d, ZRUN)], ZR.at[d - 1],
                zs.at[l, d - 1], zr.at[l, d - 1], z_at(d),
            )
            for d in range(1, ZRUN)
        ]

    def x_first_pair(l, copies):
        start, stop = columns[l]
        ZF, ZS, ZR, HS, HR = xbufs[l][3:]
        eight = halves * share
        for copy in copies:
            copy.wait_recv()
        total = ZF[z]
        for d in range(ZRUN - 1):
            total = total + ZR[d].astype(F32)
        fold = total.shape[1]
        for h in range(halves):
            HS[h, :, :fold] = total[h * share : (h + 1) * share, :]
            rest = stop - start - fold
            HS[h, :, fold:] = total[eight + h * share : eight + (h + 1) * share, :rest]
        return [
            send(
                HS.at[lax.rem(hi + d, halves)], HR.at[d - 1],
                hs.at[l, d - 1], hr.at[l, d - 1], hi_at(d),
            )
            for d in range(1, halves)
        ]

    def x_first_last(l, copies, out_ref):
        start, stop = columns[l]
        HS, HR = xbufs[l][6:]
        for copy in copies:
            copy.wait_recv()
        total = HS[hi]
        for d in range(halves - 1):
            total = total + HR[d]
        by_tap(total, start, out_ref)

    loads[0].wait()
    for x, v in enumerate(planes_of(og_ref)):
        field[0, 1, x // step, :, at_x(x % step)] = v.astype(BF)
    loads[1].wait()
    for x, v in enumerate(planes_of(pre_ref)):
        slope[x // step, :, at_x(x % step)] = jnp.where(v > 0, jnp.float32(1.0), jnp.float32(0.3))
        U[0, me, :, at_x(x)] = jnp.where(v > 0, v, 0.3 * v).astype(BF)
    loads[3].wait()
    for x, v in enumerate(planes_of(in_ref)):
        U[1, me, :, at_x(x)] = v.astype(BF)

    @pl.when(k == 0)
    def _():
        for l in range(2):
            field[l, 0] = jnp.zeros(field.shape[2:], BF)

    @pl.when(k == slabs - 1)
    def _():
        for l in range(2):
            field[l, 2] = jnp.zeros(field.shape[2:], BF)

    pl.semaphore_wait(barrier, len(peers))
    for q in range(PIECES):
        halo_send(0, q)
    gather_act, gather_in = gather_copies(0), gather_copies(1)
    gather_start(0, gather_act, jnp.logical_not(crossed))
    gather_start(1, gather_in, edge)

    none = jnp.zeros((own, ACROSS), BF)
    for a in (-1, 0, 1):
        for c in (-1, 0, 1):
            G[tap_rows(number(a, 1, c)), at_x(1)] = none
            G[tap_rows(number(a, -1, c)), at_x(height)] = none
    if wide > filled:
        G[filled:, :] = jnp.zeros((wide - filled, G.shape[1]), BF)

    def grad_pieces(l, last):
        pair, parts = [], []
        for q in range(PIECES):
            halo_wait(l, q)
            build(l, 0, q)
            build(l, 2, q)
            if q > 0:
                pair.append(grad_first(l, q - 1))
            if q > 1:
                parts.append(grad_second(l, q - 2, pair[q - 2]))
        pair.append(grad_first(l, PIECES - 1))
        last()
        for q in range(PIECES - 2, PIECES):
            parts.append(grad_second(l, q, pair[q]))
        return parts

    for q in range(PIECES):
        build(0, 1, q)
    loads[2].wait()
    turn(0, w2_ref)
    parts = grad_pieces(0, lambda: None)
    gather_start(0, gather_act, crossed)
    loads[4].wait()
    turn(1, w1_ref)
    onward = gather_forward(0, gather_act)
    gather_finish(onward)
    two = x_first(0)
    for q in range(PIECES):
        field[1, 1, q] = (grad_last(0, q, parts[q]) * slope[q]).astype(BF)
        halo_send(1, q)
        if q == 0:
            gather_start(1, gather_in, jnp.logical_not(edge))
    for q in range(PIECES):
        build(1, 1, q)
    onward = gather_forward(1, gather_in)
    gather_finish(onward)
    reorder(1)
    one_early = z_first(0)
    two = x_first_then(0, two)
    late = []

    def products():
        late.append(x_first(1))
        late.append(z_first(1))

    parts = grad_pieces(1, products)
    one_x, one_late = late
    two = x_first_pair(0, two)
    one_early = z_first_then(0, one_early)
    one_x = x_first_then(1, one_x)
    one_late = z_first_then(1, one_late)
    x_first_last(0, two, f2_ref)
    z_first_last(0, one_early, f1_ref)
    for q in range(PIECES):
        total = grad_last(1, q, parts[q])
        for x in range(step):
            rel[pl.ds(q * step + x, own, stride=height), :] = total[:, at_x(x)]
    ig_ref[...] = rel[...].reshape(own, height, ACROSS).astype(BF)
    one_x = x_first_pair(1, one_x)
    z_first_last(1, one_late, f1_ref)
    x_first_last(1, one_x, f1_ref)
    for l in range(2):
        for q in range(PIECES):
            halo_done(l, q)
    for copy in started:
        copy.wait_send()


def body(slabs, groups, inputs, pre_acts, out_grad, weight_one, weight_two):
    own, planes, height, across = out_grad.shape
    channels = weight_one.shape[2]
    cells = height * across
    chips = groups // 2
    runs = slabs // ZRUN
    halves = runs // XRUN
    share = channels // slabs
    wide = -(-TAPS * own // 128) * 128
    cuts = CUTS
    flat = lambda v: v.reshape(own, height, across)
    taps = lambda w: jnp.transpose(w, (1, 0, 2)).reshape(TAPS * own, channels)
    results = [
        jax.ShapeDtypeStruct((own, height, across), BF),
        jax.ShapeDtypeStruct((TAPS, share, own), F32),
        jax.ShapeDtypeStruct((TAPS, share, own), F32),
    ]
    piece = cells // PIECES
    fold = lambda width: -(-width // 256) * 128
    scratch = [pltpu.VMEM((own, height, across), BF)] * 3
    scratch += [pltpu.VMEM((TAPS * own, channels), BF)] * 2
    scratch += [
        pltpu.VMEM((own * height, across), F32),
        pltpu.VMEM((PIECES, own, piece), F32),
        pltpu.VMEM((2, 3, PIECES, own, piece), BF),
        pltpu.VMEM((wide, cells + 2 * across), BF),
        pltpu.VMEM((2, 2, chips * own, wide), BF),
        pltpu.VMEM((2, groups, own, cells), BF),
        pltpu.VMEM((channels, cells), BF),
        pltpu.VMEM((2, 2, PIECES, chips * own, piece), F32),
        pltpu.VMEM((2, PIECES, chips * own, piece), F32),
        pltpu.VMEM((2, PIECES, chips, own, piece), BF),
        pltpu.VMEM((2, PIECES, chips - 1, own, piece), BF),
    ]
    for width in (cuts[0], cuts[1] - cuts[0]):
        scratch += [
            pltpu.VMEM((ZRUN, runs * share, width), F32),
            pltpu.VMEM((ZRUN, runs * share, width), BF),
            pltpu.VMEM((ZRUN - 1, runs * share, width), BF),
            pltpu.VMEM((runs, share, width), F32),
            pltpu.VMEM((runs - 1, share, width), F32),
        ]
    for width in (wide, wide - cuts[1]):
        scratch += [
            pltpu.VMEM((XRUN, halves, ZRUN * share, width), F32),
            pltpu.VMEM((XRUN, halves, ZRUN * share, width), BF),
            pltpu.VMEM((XRUN - 1, halves, ZRUN * share, width), BF),
            pltpu.VMEM((ZRUN, 2 * halves * share, fold(width)), F32),
            pltpu.VMEM((ZRUN, 2 * halves * share, fold(width)), BF),
            pltpu.VMEM((ZRUN - 1, 2 * halves * share, fold(width)), BF),
            pltpu.VMEM((halves, share, width), F32),
            pltpu.VMEM((halves - 1, share, width), F32),
        ]
    scratch.append(pltpu.SemaphoreType.DMA((5,)))
    for shape in (
        (2, PIECES, 2), (2, 2 * chips - 1), (2, PIECES), (2, PIECES, chips - 1), (2, ZRUN - 1), (2, runs - 1),
        (2, XRUN - 1), (2, ZRUN - 1), (2, halves - 1),
    ):
        scratch += [pltpu.SemaphoreType.DMA(shape), pltpu.SemaphoreType.DMA(shape)]
    arrays = (flat(inputs), flat(pre_acts), flat(out_grad), taps(weight_one), taps(weight_two))
    input_grad, one, two = pl.pallas_call(
        functools.partial(kernel, slabs, groups, own, height, cuts),
        out_shape=results,
        in_specs=[pl.BlockSpec(memory_space=pltpu.HBM)] * 5,
        out_specs=[pl.BlockSpec(memory_space=pltpu.VMEM)] * 3,
        scratch_shapes=scratch,
        compiler_params=pltpu.CompilerParams(
            collective_id=0, has_side_effects=True, vmem_limit_bytes=48 * 1024 * 1024
        ),
        name="conv_back",
    )(*[pltpu.with_memory_space_constraint(v, pltpu.HBM) for v in arrays])
    return input_grad.reshape(own, planes, height, across), one, two


def solution(mesh):
    in_specs = (
        P("af", "gz", None, None),
        P("af", "gz", None, None),
        P("af", "gz", None, None),
        P("af", None, None),
        P("af", None, None),
    )
    out_specs = (P("af", "gz", None, None), P(None, "gz", "af"), P(None, "gz", "af"))
    return jax.shard_map(
        functools.partial(body, mesh.shape["gz"], mesh.shape["af"]),
        mesh=mesh, in_specs=in_specs, out_specs=out_specs, check_vma=False,
    )
```

```python
import functools

import jax
import jax.numpy as jnp
from jax import lax
from jax.experimental import pallas as pl
from jax.experimental.pallas import tpu as pltpu
from jax.sharding import PartitionSpec as P

MESH = pl.DeviceIdType.MESH
BF = jnp.bfloat16
F32 = jnp.float32
ZRUN = 8
XRUN = 4
CUT = 256
PIECES = 2
ORDER = (0, -1, 1)
TAPS = 27
ACROSS = 128
last_dims = (((1,), (1,)), ((), ()))


def kernel(
    slabs, groups, own, height, cut,
    in_hbm, pre_hbm, og_hbm, w1_hbm, w2_hbm,
    ig_ref, f1_ref, f2_ref,
    in_ref, pre_ref, og_ref, w1_ref, w2_ref,
    rel, slope, field, G, WT, U, UP, PS, PR, SB, SR,
    KF, KS, KR, QS, QR,
    XF0, XS0, XR0, ZF0, ZS0, ZR0, HS0, HR0,
    XF1, XS1, XR1, ZF1, ZS1, ZR1, HS1, HR1,
    load_s, halo_s, halo_r, ag_s, ag_r, px_s, px_r, y_s, y_r, k_s, k_r, q_s, q_r,
    xs, xr, zs, zr, hs, hr,
):
    cells = height * ACROSS
    chips = groups // 2
    runs = slabs // ZRUN
    halves = runs // XRUN
    rows = groups * own
    share = rows // slabs
    k = lax.axis_index("gz")
    me = lax.axis_index("af")
    chip, core = me // 2, me % 2
    run, z = k // ZRUN, k % ZRUN
    hi, xi = run // XRUN, run % XRUN
    sibling = {"af": chip * 2 + (1 - core)}
    chip_at = lambda d: {"af": lax.rem(chip + d, chips) * 2 + core}
    z_at = lambda d: {"gz": run * ZRUN + lax.rem(z + d, ZRUN)}
    run_at = lambda d: {"gz": lax.rem(run + d, runs) * ZRUN + z}
    x_at = lambda d: {"gz": (hi * XRUN + lax.rem(xi + d, XRUN)) * ZRUN + z}
    hi_at = lambda d: {"gz": (lax.rem(hi + d, halves) * XRUN + xi) * ZRUN + z}
    above = {"gz": lax.rem(k + 1, slabs)}
    below = {"gz": lax.rem(k + slabs - 1, slabs)}
    filled = TAPS * own
    wide = G.shape[0]
    inner = slice(ACROSS, ACROSS + cells)
    part = cells // PIECES
    step = height // PIECES
    place = k % (ZRUN * XRUN)
    crossed = (place == ZRUN - 1) | (place == ZRUN * (XRUN - 1))
    columns = ((0, wide), (cut, wide))
    xbufs = ((XF0, XS0, XR0, ZF0, ZS0, ZR0, HS0, HR0), (XF1, XS1, XR1, ZF1, ZS1, ZR1, HS1, HR1))

    peers = [sibling, above, below]
    peers += [chip_at(d) for d in range(1, chips)]
    peers += [z_at(d) for d in range(1, ZRUN)]
    peers += [run_at(d) for d in range(1, runs)]
    barrier = pltpu.get_barrier_semaphore()
    for peer in peers:
        pl.semaphore_signal(barrier, inc=1, device_id=peer, device_id_type=MESH)

    loads = []
    for i, (src, dst) in enumerate(
        ((og_hbm, og_ref), (pre_hbm, pre_ref), (w2_hbm, w2_ref), (in_hbm, in_ref), (w1_hbm, w1_ref))
    ):
        loads.append(pltpu.make_async_copy(src, dst, load_s.at[i]))
        loads[-1].start()

    started = []

    def remote(src, dst, s, r, to):
        return pltpu.make_async_remote_copy(
            src_ref=src, dst_ref=dst, send_sem=s, recv_sem=r, device_id=to, device_id_type=MESH
        )

    def send(src, dst, s, r, to):
        copy = remote(src, dst, s, r, to)
        copy.start()
        started.append(copy)
        return copy

    def planes_of(ref):
        rel[...] = ref[...].astype(F32).reshape(own * height, ACROSS)
        return [rel[pl.ds(x, own, stride=height), :] for x in range(height)]

    def at_x(x):
        return slice(x * ACROSS, (x + 1) * ACROSS)

    def halo_copies(l, q):
        own_plane, low, high = (field.at[l, p, q] for p in (1, 0, 2))
        up = remote(own_plane, low, halo_s.at[l, q, 0], halo_r.at[l, q, 0], above)
        down = remote(own_plane, high, halo_s.at[l, q, 1], halo_r.at[l, q, 1], below)
        return up, down

    def halo_send(l, q):
        up, down = halo_copies(l, q)
        pl.when(k < slabs - 1)(up.start)
        pl.when(k > 0)(down.start)

    def halo_wait(l, q):
        up, down = halo_copies(l, q)
        pl.when(k > 0)(up.wait_recv)
        pl.when(k < slabs - 1)(down.wait_recv)

    def halo_done(l, q):
        up, down = halo_copies(l, q)
        pl.when(k < slabs - 1)(up.wait_send)
        pl.when(k > 0)(down.wait_send)

    def gather_copies(l):
        mine = U.at[l, me]
        found = [
            remote(mine, mine, ag_s.at[l, d], ag_r.at[l, d], chip_at(d)) for d in range(1, chips)
        ]
        found.append(remote(mine, mine, ag_s.at[l, 0], ag_r.at[l, 0], sibling))
        return found

    def gather_start(l, found, when):
        @pl.when(when)
        def _():
            for copy in found:
                copy.start()

    def gather_forward(l, found):
        started.extend(found)
        onward = [found[-1]]
        for d in range(1, chips):
            found[d - 1].wait_recv()
            block = U.at[l, lax.rem(chip + chips - d, chips) * 2 + core]
            onward.append(
                send(block, block, ag_s.at[l, chips - 1 + d], ag_r.at[l, chips - 1 + d], sibling)
            )
        return onward

    def gather_finish(onward):
        for copy in onward:
            copy.wait_recv()

    def reorder(l):
        low, mid, top = share.bit_length() - 1, runs.bit_length() - 1, ZRUN.bit_length() - 1
        to_row = lax.broadcasted_iota(jnp.int32, (rows, rows), 0)
        from_row = lax.broadcasted_iota(jnp.int32, (rows, rows), 1)
        wanted = (
            (((to_row >> low) & (runs - 1)) << (low + top))
            | ((to_row >> (low + mid)) << low)
            | (to_row & (share - 1))
        )
        move = jnp.where(from_row == wanted, 1.0, 0.0).astype(BF)
        for n in range(0, cells, 256):
            block = U[l, :, :, n : n + 256].reshape(rows, 256)
            UP[:, n : n + 256] = jnp.dot(move, block, preferred_element_type=F32).astype(BF)

    def turn(l, w_ref):
        third = filled // 3
        blocks = [w_ref[(a + 1) * third : (a + 2) * third, :] for a in ORDER]
        full = jnp.concatenate(blocks + [jnp.zeros((wide - filled, rows), BF)], axis=0).T
        for g in range(groups):
            WT[l, g % 2, (g // 2) * own : (g // 2 + 1) * own, :] = full[g * own : (g + 1) * own, :]

    lane = lax.broadcasted_iota(jnp.int32, (own, ACROSS), 1)
    number = lambda a, b, c: 9 * ORDER.index(a) + 3 * (b + 1) + (c + 1)
    tap_rows = lambda t: slice(t * own, (t + 1) * own)

    def build(l, p, q):
        a = 1 - p
        for x in range(q * step, (q + 1) * step):
            v = field[l, p, q, :, at_x(x - q * step)].astype(F32)
            for c in (-1, 0, 1):
                if c == 0:
                    s = v
                else:
                    edge = 0 if c == 1 else ACROSS - 1
                    s = jnp.where(lane == edge, 0.0, pltpu.roll(v, c % ACROSS, 1))
                s = s.astype(BF)
                for b in (-1, 0, 1):
                    if 0 <= x + b < height:
                        G[tap_rows(number(a, b, c)), at_x(x + b + 1)] = s

    def grad_product(l, half, which, q):
        for n in range(0, part, 256):
            at = slice(ACROSS + q * part + n, ACROSS + q * part + n + 256)
            PS[l, half, q, :, n : n + 256] = jnp.dot(
                WT[l, which], G[:, at], preferred_element_type=F32
            )

    def grad_first(l, q):
        grad_product(l, 0, 1 - core, q)
        copy = send(PS.at[l, 0, q], PR.at[l, q], px_s.at[l, q], px_r.at[l, q], sibling)
        grad_product(l, 1, core, q)
        return copy

    def grad_second(l, q, copy):
        copy.wait_recv()
        for j in range(chips):
            at = slice(j * own, (j + 1) * own)
            total = PS[l, 1, q, at, :] + PR[l, q, at, :]
            PS[l, 1, q, at, :] = total
            SB[l, q, j] = total.astype(BF)
        return [
            send(
                SB.at[l, q, lax.rem(chip + d, chips)], SR.at[l, q, d - 1],
                y_s.at[l, q, d - 1], y_r.at[l, q, d - 1], chip_at(d),
            )
            for d in range(1, chips)
        ]

    def grad_last(l, q, found):
        for copy in found:
            copy.wait_recv()
        mine = pl.ds(pl.multiple_of(chip * own, own), own)
        total = PS[l, 1, q, mine, :]
        for d in range(chips - 1):
            total = total + SR[l, q, d].astype(F32)
        return total

    def by_tap(total, start, out_ref):
        for i in range(total.shape[1] // own):
            block = start // own + i
            if block < TAPS:
                out_ref[9 * (ORDER[block // 9] + 1) + block % 9] = total[:, i * own : (i + 1) * own]

    def z_first():
        for n in range(0, cut, 256):
            size = min(256, cut - n)
            at = slice(n, n + size)
            block = lax.dot_general(
                UP[...], G[n : n + size, inner], last_dims, preferred_element_type=F32
            ).reshape(ZRUN, runs * share, size)
            KF[:, :, at] = block
            KS[:, :, at] = block.astype(BF)
        return [
            send(
                KS.at[lax.rem(z + d, ZRUN)], KR.at[d - 1],
                k_s.at[d - 1], k_r.at[d - 1], z_at(d),
            )
            for d in range(1, ZRUN)
        ]

    def z_first_then(copies):
        for copy in copies:
            copy.wait_recv()
        for n in range(0, KF.shape[2], 128):
            at = slice(n, n + 128)
            total = KF[z, :, at]
            for d in range(ZRUN - 1):
                total = total + KR[d, :, at].astype(F32)
            for j in range(runs):
                QS[j, :, at] = total[j * share : (j + 1) * share, :]
        return [
            send(
                QS.at[lax.rem(run + d, runs)], QR.at[d - 1],
                q_s.at[d - 1], q_r.at[d - 1], run_at(d),
            )
            for d in range(1, runs)
        ]

    def z_first_last(copies, out_ref):
        for copy in copies:
            copy.wait_recv()
        total = QS[run]
        for d in range(runs - 1):
            total = total + QR[d]
        by_tap(total, 0, out_ref)

    def x_first(l):
        start, stop = columns[l]
        XF, XS, XR = xbufs[l][:3]
        for n in range(start, stop, 256):
            size = min(256, stop - n)
            at = slice(n - start, n - start + size)
            block = lax.dot_general(
                U[l].reshape(rows, cells), G[n : n + size, inner], last_dims,
                preferred_element_type=F32,
            )
            for h in range(halves):
                for x in range(XRUN):
                    j = (h * XRUN + x) * ZRUN * share
                    part = block[j : j + ZRUN * share, :]
                    XF[x, h, :, at] = part
                    XS[x, h, :, at] = part.astype(BF)
        return [
            send(
                XS.at[lax.rem(xi + d, XRUN)], XR.at[d - 1],
                xs.at[l, d - 1], xr.at[l, d - 1], x_at(d),
            )
            for d in range(1, XRUN)
        ]

    def x_first_then(l, copies):
        start, stop = columns[l]
        XF, XS, XR, ZF, ZS, ZR = xbufs[l][:6]
        eight = halves * share
        for copy in copies:
            copy.wait_recv()
        for n in range(0, stop - start, 128):
            at = slice(n, n + 128)
            fold, to = divmod(n, ZS.shape[2])
            to = slice(to, to + 128)
            for h in range(halves):
                total = XF[xi, h, :, at]
                for d in range(XRUN - 1):
                    total = total + XR[d, h, :, at].astype(F32)
                first = fold * eight + h * share
                for j in range(ZRUN):
                    ZF[j, first : first + share, to] = total[j * share : (j + 1) * share, :]
        for j in range(ZRUN):
            ZS[j] = ZF[j].astype(BF)
        return [
            send(
                ZS.at[lax.rem(z + d, ZRUN)], ZR.at[d - 1],
                zs.at[l, d - 1], zr.at[l, d - 1], z_at(d),
            )
            for d in range(1, ZRUN)
        ]

    def x_first_pair(l, copies):
        start, stop = columns[l]
        ZF, ZS, ZR, HS, HR = xbufs[l][3:]
        eight = halves * share
        for copy in copies:
            copy.wait_recv()
        total = ZF[z]
        for d in range(ZRUN - 1):
            total = total + ZR[d].astype(F32)
        fold = total.shape[1]
        for h in range(halves):
            HS[h, :, :fold] = total[h * share : (h + 1) * share, :]
            rest = stop - start - fold
            HS[h, :, fold:] = total[eight + h * share : eight + (h + 1) * share, :rest]
        return [
            send(
                HS.at[lax.rem(hi + d, halves)], HR.at[d - 1],
                hs.at[l, d - 1], hr.at[l, d - 1], hi_at(d),
            )
            for d in range(1, halves)
        ]

    def x_first_last(l, copies, out_ref):
        start, stop = columns[l]
        HS, HR = xbufs[l][6:]
        for copy in copies:
            copy.wait_recv()
        total = HS[hi]
        for d in range(halves - 1):
            total = total + HR[d]
        by_tap(total, start, out_ref)

    loads[0].wait()
    for x, v in enumerate(planes_of(og_ref)):
        field[0, 1, x // step, :, at_x(x % step)] = v.astype(BF)
    loads[1].wait()
    for x, v in enumerate(planes_of(pre_ref)):
        slope[x // step, :, at_x(x % step)] = jnp.where(v > 0, jnp.float32(1.0), jnp.float32(0.3))
        U[0, me, :, at_x(x)] = jnp.where(v > 0, v, 0.3 * v).astype(BF)
    loads[3].wait()
    for x, v in enumerate(planes_of(in_ref)):
        U[1, me, :, at_x(x)] = v.astype(BF)

    @pl.when(k == 0)
    def _():
        for l in range(2):
            field[l, 0] = jnp.zeros(field.shape[2:], BF)

    @pl.when(k == slabs - 1)
    def _():
        for l in range(2):
            field[l, 2] = jnp.zeros(field.shape[2:], BF)

    pl.semaphore_wait(barrier, len(peers))
    for q in range(PIECES):
        halo_send(0, q)
    gather_act, gather_in = gather_copies(0), gather_copies(1)
    gather_start(0, gather_act, jnp.logical_not(crossed))
    gather_start(1, gather_in, jnp.logical_not(crossed))

    none = jnp.zeros((own, ACROSS), BF)
    for a in (-1, 0, 1):
        for c in (-1, 0, 1):
            G[tap_rows(number(a, 1, c)), at_x(1)] = none
            G[tap_rows(number(a, -1, c)), at_x(height)] = none
    if wide > filled:
        G[filled:, :] = jnp.zeros((wide - filled, G.shape[1]), BF)

    def grad_pieces(l, last):
        pair, parts = [], []
        for q in range(PIECES):
            halo_wait(l, q)
            build(l, 0, q)
            build(l, 2, q)
            if q > 0:
                pair.append(grad_first(l, q - 1))
            if q > 1:
                parts.append(grad_second(l, q - 2, pair[q - 2]))
        pair.append(grad_first(l, PIECES - 1))
        last()
        for q in range(PIECES - 2, PIECES):
            parts.append(grad_second(l, q, pair[q]))
        return parts

    for q in range(PIECES):
        build(0, 1, q)
    loads[2].wait()
    turn(0, w2_ref)
    parts = grad_pieces(0, lambda: None)
    gather_start(0, gather_act, crossed)
    gather_start(1, gather_in, crossed)
    loads[4].wait()
    turn(1, w1_ref)
    onward = gather_forward(0, gather_act)
    gather_finish(onward)
    two = x_first(0)
    onward = gather_forward(1, gather_in)
    gather_finish(onward)
    reorder(1)
    for q in range(PIECES):
        field[1, 1, q] = (grad_last(0, q, parts[q]) * slope[q]).astype(BF)
        halo_send(1, q)
    for q in range(PIECES):
        build(1, 1, q)
    one_z = z_first()
    two = x_first_then(0, two)
    late = []
    parts = grad_pieces(1, lambda: late.append(x_first(1)))
    two = x_first_pair(0, two)
    one_z = z_first_then(one_z)
    one_x = x_first_then(1, late[0])
    x_first_last(0, two, f2_ref)
    z_first_last(one_z, f1_ref)
    for q in range(PIECES):
        total = grad_last(1, q, parts[q])
        for x in range(step):
            rel[pl.ds(q * step + x, own, stride=height), :] = total[:, at_x(x)]
    ig_ref[...] = rel[...].reshape(own, height, ACROSS).astype(BF)
    one_x = x_first_pair(1, one_x)
    x_first_last(1, one_x, f1_ref)
    for l in range(2):
        for q in range(PIECES):
            halo_done(l, q)
    for copy in started:
        copy.wait_send()


def body(slabs, groups, inputs, pre_acts, out_grad, weight_one, weight_two):
    own, planes, height, across = out_grad.shape
    channels = weight_one.shape[2]
    cells = height * across
    chips = groups // 2
    runs = slabs // ZRUN
    halves = runs // XRUN
    share = channels // slabs
    wide = -(-TAPS * own // 128) * 128
    cut = CUT
    flat = lambda v: v.reshape(own, height, across)
    taps = lambda w: jnp.transpose(w, (1, 0, 2)).reshape(TAPS * own, channels)
    results = [
        jax.ShapeDtypeStruct((own, height, across), BF),
        jax.ShapeDtypeStruct((TAPS, share, own), F32),
        jax.ShapeDtypeStruct((TAPS, share, own), F32),
    ]
    piece = cells // PIECES
    fold = lambda width: -(-width // 256) * 128
    scratch = [pltpu.VMEM((own, height, across), BF)] * 3
    scratch += [pltpu.VMEM((TAPS * own, channels), BF)] * 2
    scratch += [
        pltpu.VMEM((own * height, across), F32),
        pltpu.VMEM((PIECES, own, piece), F32),
        pltpu.VMEM((2, 3, PIECES, own, piece), BF),
        pltpu.VMEM((wide, cells + 2 * across), BF),
        pltpu.VMEM((2, 2, chips * own, wide), BF),
        pltpu.VMEM((2, groups, own, cells), BF),
        pltpu.VMEM((channels, cells), BF),
        pltpu.VMEM((2, 2, PIECES, chips * own, piece), F32),
        pltpu.VMEM((2, PIECES, chips * own, piece), F32),
        pltpu.VMEM((2, PIECES, chips, own, piece), BF),
        pltpu.VMEM((2, PIECES, chips - 1, own, piece), BF),
    ]
    scratch += [
        pltpu.VMEM((ZRUN, runs * share, cut), F32),
        pltpu.VMEM((ZRUN, runs * share, cut), BF),
        pltpu.VMEM((ZRUN - 1, runs * share, cut), BF),
        pltpu.VMEM((runs, share, cut), F32),
        pltpu.VMEM((runs - 1, share, cut), F32),
    ]
    for width in (wide, wide - cut):
        scratch += [
            pltpu.VMEM((XRUN, halves, ZRUN * share, width), F32),
            pltpu.VMEM((XRUN, halves, ZRUN * share, width), BF),
            pltpu.VMEM((XRUN - 1, halves, ZRUN * share, width), BF),
            pltpu.VMEM((ZRUN, 2 * halves * share, fold(width)), F32),
            pltpu.VMEM((ZRUN, 2 * halves * share, fold(width)), BF),
            pltpu.VMEM((ZRUN - 1, 2 * halves * share, fold(width)), BF),
            pltpu.VMEM((halves, share, width), F32),
            pltpu.VMEM((halves - 1, share, width), F32),
        ]
    scratch.append(pltpu.SemaphoreType.DMA((5,)))
    for shape in (
        (2, PIECES, 2), (2, 2 * chips - 1), (2, PIECES), (2, PIECES, chips - 1), (ZRUN - 1,), (runs - 1,),
        (2, XRUN - 1), (2, ZRUN - 1), (2, halves - 1),
    ):
        scratch += [pltpu.SemaphoreType.DMA(shape), pltpu.SemaphoreType.DMA(shape)]
    arrays = (flat(inputs), flat(pre_acts), flat(out_grad), taps(weight_one), taps(weight_two))
    input_grad, one, two = pl.pallas_call(
        functools.partial(kernel, slabs, groups, own, height, cut),
        out_shape=results,
        in_specs=[pl.BlockSpec(memory_space=pltpu.HBM)] * 5,
        out_specs=[pl.BlockSpec(memory_space=pltpu.VMEM)] * 3,
        scratch_shapes=scratch,
        compiler_params=pltpu.CompilerParams(
            collective_id=0, has_side_effects=True, vmem_limit_bytes=48 * 1024 * 1024
        ),
        name="conv_back",
    )(*[pltpu.with_memory_space_constraint(v, pltpu.HBM) for v in arrays])
    return input_grad.reshape(own, planes, height, across), one, two


def solution(mesh):
    in_specs = (
        P("af", "gz", None, None),
        P("af", "gz", None, None),
        P("af", "gz", None, None),
        P("af", None, None),
        P("af", None, None),
    )
    out_specs = (P("af", "gz", None, None), P(None, "gz", "af"), P(None, "gz", "af"))
    return jax.shard_map(
        functools.partial(body, mesh.shape["gz"], mesh.shape["af"]),
        mesh=mesh, in_specs=in_specs, out_specs=out_specs, check_vma=False,
    )
```

```python
import functools

import jax
import jax.numpy as jnp
from jax import lax
from jax.experimental import pallas as pl
from jax.experimental.pallas import tpu as pltpu
from jax.sharding import PartitionSpec as P

MESH = pl.DeviceIdType.MESH
BF = jnp.bfloat16
F32 = jnp.float32
ZRUN = 8
XRUN = 4
CUT = 384
PIECES = 2
ORDER = (0, -1, 1)
TAPS = 27
ACROSS = 128
last_dims = (((1,), (1,)), ((), ()))


def kernel(
    slabs, groups, own, height, cut,
    in_hbm, pre_hbm, og_hbm, w1_hbm, w2_hbm,
    ig_ref, f1_ref, f2_ref,
    in_ref, pre_ref, og_ref, w1_ref, w2_ref,
    rel, slope, field, G, WT, U, UP, PS, PR, SB, SR,
    KF, KS, KR, QS, QR,
    XF0, XS0, XR0, ZF0, ZS0, ZR0, HS0, HR0,
    XF1, XS1, XR1, ZF1, ZS1, ZR1, HS1, HR1,
    load_s, halo_s, halo_r, ag_s, ag_r, px_s, px_r, y_s, y_r, k_s, k_r, q_s, q_r,
    xs, xr, zs, zr, hs, hr,
):
    cells = height * ACROSS
    chips = groups // 2
    runs = slabs // ZRUN
    halves = runs // XRUN
    rows = groups * own
    share = rows // slabs
    k = lax.axis_index("gz")
    me = lax.axis_index("af")
    chip, core = me // 2, me % 2
    run, z = k // ZRUN, k % ZRUN
    hi, xi = run // XRUN, run % XRUN
    sibling = {"af": chip * 2 + (1 - core)}
    chip_at = lambda d: {"af": lax.rem(chip + d, chips) * 2 + core}
    z_at = lambda d: {"gz": run * ZRUN + lax.rem(z + d, ZRUN)}
    run_at = lambda d: {"gz": lax.rem(run + d, runs) * ZRUN + z}
    x_at = lambda d: {"gz": (hi * XRUN + lax.rem(xi + d, XRUN)) * ZRUN + z}
    hi_at = lambda d: {"gz": (lax.rem(hi + d, halves) * XRUN + xi) * ZRUN + z}
    above = {"gz": lax.rem(k + 1, slabs)}
    below = {"gz": lax.rem(k + slabs - 1, slabs)}
    filled = TAPS * own
    wide = G.shape[0]
    inner = slice(ACROSS, ACROSS + cells)
    part = cells // PIECES
    step = height // PIECES
    sibling = {"af": chip * 2 + (1 - core)}
    chip_at = lambda d: {"af": lax.rem(chip + d, chips) * 2 + core}
    z_at = lambda d: {"gz": run * ZRUN + lax.rem(z + d, ZRUN)}
    run_at = lambda d: {"gz": lax.rem(run + d, runs) * ZRUN + z}
    x_at = lambda d: {"gz": (hi * XRUN + lax.rem(xi + d, XRUN)) * ZRUN + z}
    hi_at = lambda d: {"gz": (lax.rem(hi + d, halves) * XRUN + xi) * ZRUN + z}
    above = {"gz": lax.rem(k + 1, slabs)}
    below = {"gz": lax.rem(k + slabs - 1, slabs)}
    filled = TAPS * own
    wide = G.shape[0]
    inner = slice(ACROSS, ACROSS + cells)
    part = cells // PIECES
    step = height // PIECES
    place = k % (ZRUN * XRUN)
    crossed = (place == ZRUN - 1) | (place == ZRUN * (XRUN - 1))
    columns = ((0, wide), (cut, wide))
    xbufs = ((XF0, XS0, XR0, ZF0, ZS0, ZR0, HS0, HR0), (XF1, XS1, XR1, ZF1, ZS1, ZR1, HS1, HR1))

    peers = [sibling, above, below]
    peers += [chip_at(d) for d in range(1, chips)]
    peers += [z_at(d) for d in range(1, ZRUN)]
    peers += [run_at(d) for d in range(1, runs)]
    barrier = pltpu.get_barrier_semaphore()
    for peer in peers:
        pl.semaphore_signal(barrier, inc=1, device_id=peer, device_id_type=MESH)

    loads = []
    for i, (src, dst) in enumerate(
        ((og_hbm, og_ref), (pre_hbm, pre_ref), (w2_hbm, w2_ref), (in_hbm, in_ref), (w1_hbm, w1_ref))
    ):
        loads.append(pltpu.make_async_copy(src, dst, load_s.at[i]))
        loads[-1].start()

    started = []

    def remote(src, dst, s, r, to):
        return pltpu.make_async_remote_copy(
            src_ref=src, dst_ref=dst, send_sem=s, recv_sem=r, device_id=to, device_id_type=MESH
        )

    def send(src, dst, s, r, to):
        copy = remote(src, dst, s, r, to)
        copy.start()
        started.append(copy)
        return copy

    def planes_of(ref):
        rel[...] = ref[...].astype(F32).reshape(own * height, ACROSS)
        return [rel[pl.ds(x, own, stride=height), :] for x in range(height)]

    def at_x(x):
        return slice(x * ACROSS, (x + 1) * ACROSS)

    def halo_copies(l, q):
        own_plane, low, high = (field.at[l, p, q] for p in (1, 0, 2))
        up = remote(own_plane, low, halo_s.at[l, q, 0], halo_r.at[l, q, 0], above)
        down = remote(own_plane, high, halo_s.at[l, q, 1], halo_r.at[l, q, 1], below)
        return up, down

    def halo_send(l, q):
        up, down = halo_copies(l, q)
        pl.when(k < slabs - 1)(up.start)
        pl.when(k > 0)(down.start)

    def halo_wait(l, q):
        up, down = halo_copies(l, q)
        pl.when(k > 0)(up.wait_recv)
        pl.when(k < slabs - 1)(down.wait_recv)

    def halo_done(l, q):
        up, down = halo_copies(l, q)
        pl.when(k < slabs - 1)(up.wait_send)
        pl.when(k > 0)(down.wait_send)

    def gather_start(l, low, high):
        mine = U.at[l, me, pl.ds(low, high - low)]
        i = l if low == 0 else 2
        return [
            send(mine, mine, ag_s.at[i, d], ag_r.at[i, d], chip_at(d)) for d in range(1, chips)
        ]

    def gather_sibling(l):
        mine = U.at[l, me]
        return send(mine, mine, ag_s.at[l, 0], ag_r.at[l, 0], sibling)

    def gather_forward(l, *found):
        onward = []
        for d in range(1, chips):
            for copies in found:
                copies[d - 1].wait_recv()
            block = U.at[l, lax.rem(chip + chips - d, chips) * 2 + core]
            onward.append(
                send(block, block, ag_s.at[l, chips - 1 + d], ag_r.at[l, chips - 1 + d], sibling)
            )
        return onward

    def gather_finish(onward):
        for copy in onward:
            copy.wait_recv()

    def reorder(l):
        low, mid, top = share.bit_length() - 1, runs.bit_length() - 1, ZRUN.bit_length() - 1
        to_row = lax.broadcasted_iota(jnp.int32, (rows, rows), 0)
        from_row = lax.broadcasted_iota(jnp.int32, (rows, rows), 1)
        wanted = (
            (((to_row >> low) & (runs - 1)) << (low + top))
            | ((to_row >> (low + mid)) << low)
            | (to_row & (share - 1))
        )
        move = jnp.where(from_row == wanted, 1.0, 0.0).astype(BF)
        for n in range(0, cells, 256):
            block = U[l, :, :, n : n + 256].reshape(rows, 256)
            UP[:, n : n + 256] = jnp.dot(move, block, preferred_element_type=F32).astype(BF)

    def turn(l, w_ref):
        third = filled // 3
        blocks = [w_ref[(a + 1) * third : (a + 2) * third, :] for a in ORDER]
        full = jnp.concatenate(blocks + [jnp.zeros((wide - filled, rows), BF)], axis=0).T
        for g in range(groups):
            WT[l, g % 2, (g // 2) * own : (g // 2 + 1) * own, :] = full[g * own : (g + 1) * own, :]

    lane = lax.broadcasted_iota(jnp.int32, (own, ACROSS), 1)
    number = lambda a, b, c: 9 * ORDER.index(a) + 3 * (b + 1) + (c + 1)
    tap_rows = lambda t: slice(t * own, (t + 1) * own)

    def build(l, p, q):
        a = 1 - p
        for x in range(q * step, (q + 1) * step):
            v = field[l, p, q, :, at_x(x - q * step)].astype(F32)
            for c in (-1, 0, 1):
                if c == 0:
                    s = v
                else:
                    edge = 0 if c == 1 else ACROSS - 1
                    s = jnp.where(lane == edge, 0.0, pltpu.roll(v, c % ACROSS, 1))
                s = s.astype(BF)
                for b in (-1, 0, 1):
                    if 0 <= x + b < height:
                        G[tap_rows(number(a, b, c)), at_x(x + b + 1)] = s

    def grad_product(l, half, which, q):
        for n in range(0, part, 256):
            at = slice(ACROSS + q * part + n, ACROSS + q * part + n + 256)
            PS[l, half, q, :, n : n + 256] = jnp.dot(
                WT[l, which], G[:, at], preferred_element_type=F32
            )

    def grad_first(l):
        copies = []
        for q in range(PIECES):
            grad_product(l, 0, 1 - core, q)
            copies.append(send(PS.at[l, 0, q], PR.at[l, q], px_s.at[l, q], px_r.at[l, q], sibling))
        for q in range(PIECES):
            grad_product(l, 1, core, q)
        return copies

    def grad_second(l, q, copy):
        copy.wait_recv()
        for j in range(chips):
            at = slice(j * own, (j + 1) * own)
            total = PS[l, 1, q, at, :] + PR[l, q, at, :]
            PS[l, 1, q, at, :] = total
            SB[l, q, j] = total.astype(BF)
        return [
            send(
                SB.at[l, q, lax.rem(chip + d, chips)], SR.at[l, q, d - 1],
                y_s.at[l, q, d - 1], y_r.at[l, q, d - 1], chip_at(d),
            )
            for d in range(1, chips)
        ]

    def grad_last(l, q, found):
        for copy in found:
            copy.wait_recv()
        mine = pl.ds(pl.multiple_of(chip * own, own), own)
        total = PS[l, 1, q, mine, :]
        for d in range(chips - 1):
            total = total + SR[l, q, d].astype(F32)
        return total

    def by_tap(total, start, out_ref):
        for i in range(total.shape[1] // own):
            block = start // own + i
            if block < TAPS:
                out_ref[9 * (ORDER[block // 9] + 1) + block % 9] = total[:, i * own : (i + 1) * own]

    def z_first():
        for n in range(0, cut, 256):
            size = min(256, cut - n)
            at = slice(n, n + size)
            block = lax.dot_general(
                UP[...], G[n : n + size, inner], last_dims, preferred_element_type=F32
            ).reshape(ZRUN, runs * share, size)
            KF[:, :, at] = block
            KS[:, :, at] = block.astype(BF)
        return [
            send(
                KS.at[lax.rem(z + d, ZRUN)], KR.at[d - 1],
                k_s.at[d - 1], k_r.at[d - 1], z_at(d),
            )
            for d in range(1, ZRUN)
        ]

    def z_first_then(copies):
        for copy in copies:
            copy.wait_recv()
        for n in range(0, KF.shape[2], 128):
            at = slice(n, n + 128)
            total = KF[z, :, at]
            for d in range(ZRUN - 1):
                total = total + KR[d, :, at].astype(F32)
            for j in range(runs):
                QS[j, :, at] = total[j * share : (j + 1) * share, :]
        return [
            send(
                QS.at[lax.rem(run + d, runs)], QR.at[d - 1],
                q_s.at[d - 1], q_r.at[d - 1], run_at(d),
            )
            for d in range(1, runs)
        ]

    def z_first_last(copies, out_ref):
        for copy in copies:
            copy.wait_recv()
        total = QS[run]
        for d in range(runs - 1):
            total = total + QR[d]
        by_tap(total, 0, out_ref)

    def x_first(l):
        start, stop = columns[l]
        XF, XS, XR = xbufs[l][:3]
        for n in range(start, stop, 256):
            size = min(256, stop - n)
            at = slice(n - start, n - start + size)
            block = lax.dot_general(
                U[l].reshape(rows, cells), G[n : n + size, inner], last_dims,
                preferred_element_type=F32,
            )
            for h in range(halves):
                for x in range(XRUN):
                    j = (h * XRUN + x) * ZRUN * share
                    part = block[j : j + ZRUN * share, :]
                    XF[x, h, :, at] = part
                    XS[x, h, :, at] = part.astype(BF)
        return [
            send(
                XS.at[lax.rem(xi + d, XRUN)], XR.at[d - 1],
                xs.at[l, d - 1], xr.at[l, d - 1], x_at(d),
            )
            for d in range(1, XRUN)
        ]

    def x_first_then(l, copies):
        start, stop = columns[l]
        XF, XS, XR, ZF, ZS, ZR = xbufs[l][:6]
        eight = halves * share
        for copy in copies:
            copy.wait_recv()
        for n in range(0, stop - start, 128):
            at = slice(n, n + 128)
            fold, to = divmod(n, ZS.shape[2])
            to = slice(to, to + 128)
            for h in range(halves):
                total = XF[xi, h, :, at]
                for d in range(XRUN - 1):
                    total = total + XR[d, h, :, at].astype(F32)
                first = fold * eight + h * share
                for j in range(ZRUN):
                    ZF[j, first : first + share, to] = total[j * share : (j + 1) * share, :]
        for j in range(ZRUN):
            ZS[j] = ZF[j].astype(BF)
        return [
            send(
                ZS.at[lax.rem(z + d, ZRUN)], ZR.at[d - 1],
                zs.at[l, d - 1], zr.at[l, d - 1], z_at(d),
            )
            for d in range(1, ZRUN)
        ]

    def x_first_pair(l, copies):
        start, stop = columns[l]
        ZF, ZS, ZR, HS, HR = xbufs[l][3:]
        eight = halves * share
        for copy in copies:
            copy.wait_recv()
        total = ZF[z]
        for d in range(ZRUN - 1):
            total = total + ZR[d].astype(F32)
        fold = total.shape[1]
        for h in range(halves):
            HS[h, :, :fold] = total[h * share : (h + 1) * share, :]
            rest = stop - start - fold
            HS[h, :, fold:] = total[eight + h * share : eight + (h + 1) * share, :rest]
        return [
            send(
                HS.at[lax.rem(hi + d, halves)], HR.at[d - 1],
                hs.at[l, d - 1], hr.at[l, d - 1], hi_at(d),
            )
            for d in range(1, halves)
        ]

    def x_first_last(l, copies, out_ref):
        start, stop = columns[l]
        HS, HR = xbufs[l][6:]
        for copy in copies:
            copy.wait_recv()
        total = HS[hi]
        for d in range(halves - 1):
            total = total + HR[d]
        by_tap(total, start, out_ref)

    loads[0].wait()
    for x, v in enumerate(planes_of(og_ref)):
        field[0, 1, x // step, :, at_x(x % step)] = v.astype(BF)
    loads[1].wait()
    for x, v in enumerate(planes_of(pre_ref)):
        slope[x // step, :, at_x(x % step)] = jnp.where(v > 0, jnp.float32(1.0), jnp.float32(0.3))
        U[0, me, :, at_x(x)] = jnp.where(v > 0, v, 0.3 * v).astype(BF)
    loads[3].wait()
    for x, v in enumerate(planes_of(in_ref)):
        U[1, me, :, at_x(x)] = v.astype(BF)

    @pl.when(k == 0)
    def _():
        for l in range(2):
            field[l, 0] = jnp.zeros(field.shape[2:], BF)

    @pl.when(k == slabs - 1)
    def _():
        for l in range(2):
            field[l, 2] = jnp.zeros(field.shape[2:], BF)

    pl.semaphore_wait(barrier, len(peers))
    for q in range(PIECES):
        halo_send(0, q)
    gather_act = gather_start(0, 0, own)
    near_act = gather_sibling(0)
    gather_in = gather_start(1, 0, own // 2)

    none = jnp.zeros((own, ACROSS), BF)
    for a in (-1, 0, 1):
        for c in (-1, 0, 1):
            G[tap_rows(number(a, 1, c)), at_x(1)] = none
            G[tap_rows(number(a, -1, c)), at_x(height)] = none
    if wide > filled:
        G[filled:, :] = jnp.zeros((wide - filled, G.shape[1]), BF)

    def finish_taps(l):
        for q in range(PIECES):
            halo_wait(l, q)
            build(l, 0, q)
            build(l, 2, q)

    for q in range(PIECES):
        build(0, 1, q)
    loads[2].wait()
    turn(0, w2_ref)
    finish_taps(0)
    pair = grad_first(0)
    parts = [grad_second(0, q, pair[q]) for q in range(PIECES)]
    onward = gather_forward(0, gather_act)
    loads[4].wait()
    turn(1, w1_ref)
    gather_finish(onward + [near_act])
    two = x_first(0)
    for q in range(PIECES):
        field[1, 1, q] = (grad_last(0, q, parts[q]) * slope[q]).astype(BF)
        halo_send(1, q)
    gather_rest = gather_start(1, own // 2, own)
    near_in = gather_sibling(1)
    for q in range(PIECES):
        build(1, 1, q)
    finish_taps(1)
    pair = grad_first(1)
    onward = gather_forward(1, gather_in, gather_rest)
    gather_finish(onward + [near_in])
    one_x = x_first(1)
    reorder(1)
    one_z = z_first()
    parts = [grad_second(1, q, pair[q]) for q in range(PIECES)]
    two = x_first_then(0, two)
    one_x = x_first_then(1, one_x)
    one_z = z_first_then(one_z)
    two = x_first_pair(0, two)
    for q in range(PIECES):
        total = grad_last(1, q, parts[q])
        for x in range(step):
            rel[pl.ds(q * step + x, own, stride=height), :] = total[:, at_x(x)]
    ig_ref[...] = rel[...].reshape(own, height, ACROSS).astype(BF)
    one_x = x_first_pair(1, one_x)
    x_first_last(0, two, f2_ref)
    z_first_last(one_z, f1_ref)
    x_first_last(1, one_x, f1_ref)
    for l in range(2):
        for q in range(PIECES):
            halo_done(l, q)
    for copy in started:
        copy.wait_send()


def body(slabs, groups, inputs, pre_acts, out_grad, weight_one, weight_two):
    own, planes, height, across = out_grad.shape
    channels = weight_one.shape[2]
    cells = height * across
    chips = groups // 2
    runs = slabs // ZRUN
    halves = runs // XRUN
    share = channels // slabs
    wide = -(-TAPS * own // 128) * 128
    cut = CUT
    flat = lambda v: v.reshape(own, height, across)
    taps = lambda w: jnp.transpose(w, (1, 0, 2)).reshape(TAPS * own, channels)
    results = [
        jax.ShapeDtypeStruct((own, height, across), BF),
        jax.ShapeDtypeStruct((TAPS, share, own), F32),
        jax.ShapeDtypeStruct((TAPS, share, own), F32),
    ]
    piece = cells // PIECES
    fold = lambda width: -(-width // 256) * 128
    scratch = [pltpu.VMEM((own, height, across), BF)] * 3
    scratch += [pltpu.VMEM((TAPS * own, channels), BF)] * 2
    scratch += [
        pltpu.VMEM((own * height, across), F32),
        pltpu.VMEM((PIECES, own, piece), F32),
        pltpu.VMEM((2, 3, PIECES, own, piece), BF),
        pltpu.VMEM((wide, cells + 2 * across), BF),
        pltpu.VMEM((2, 2, chips * own, wide), BF),
        pltpu.VMEM((2, groups, own, cells), BF),
        pltpu.VMEM((channels, cells), BF),
        pltpu.VMEM((2, 2, PIECES, chips * own, piece), F32),
        pltpu.VMEM((2, PIECES, chips * own, piece), F32),
        pltpu.VMEM((2, PIECES, chips, own, piece), BF),
        pltpu.VMEM((2, PIECES, chips - 1, own, piece), BF),
    ]
    scratch += [
        pltpu.VMEM((ZRUN, runs * share, cut), F32),
        pltpu.VMEM((ZRUN, runs * share, cut), BF),
        pltpu.VMEM((ZRUN - 1, runs * share, cut), BF),
        pltpu.VMEM((runs, share, cut), F32),
        pltpu.VMEM((runs - 1, share, cut), F32),
    ]
    for width in (wide, wide - cut):
        scratch += [
            pltpu.VMEM((XRUN, halves, ZRUN * share, width), F32),
            pltpu.VMEM((XRUN, halves, ZRUN * share, width), BF),
            pltpu.VMEM((XRUN - 1, halves, ZRUN * share, width), BF),
            pltpu.VMEM((ZRUN, 2 * halves * share, fold(width)), F32),
            pltpu.VMEM((ZRUN, 2 * halves * share, fold(width)), BF),
            pltpu.VMEM((ZRUN - 1, 2 * halves * share, fold(width)), BF),
            pltpu.VMEM((halves, share, width), F32),
            pltpu.VMEM((halves - 1, share, width), F32),
        ]
    scratch.append(pltpu.SemaphoreType.DMA((5,)))
    for shape in (
        (2, PIECES, 2), (3, 2 * chips - 1), (2, PIECES), (2, PIECES, chips - 1), (ZRUN - 1,), (runs - 1,),
        (2, XRUN - 1), (2, ZRUN - 1), (2, halves - 1),
    ):
        scratch += [pltpu.SemaphoreType.DMA(shape), pltpu.SemaphoreType.DMA(shape)]
    arrays = (flat(inputs), flat(pre_acts), flat(out_grad), taps(weight_one), taps(weight_two))
    input_grad, one, two = pl.pallas_call(
        functools.partial(kernel, slabs, groups, own, height, cut),
        out_shape=results,
        in_specs=[pl.BlockSpec(memory_space=pltpu.HBM)] * 5,
        out_specs=[pl.BlockSpec(memory_space=pltpu.VMEM)] * 3,
        scratch_shapes=scratch,
        compiler_params=pltpu.CompilerParams(
            collective_id=0, has_side_effects=True, vmem_limit_bytes=48 * 1024 * 1024
        ),
        name="conv_back",
    )(*[pltpu.with_memory_space_constraint(v, pltpu.HBM) for v in arrays])
    return input_grad.reshape(own, planes, height, across), one, two


def solution(mesh):
    in_specs = (
        P("af", "gz", None, None),
        P("af", "gz", None, None),
        P("af", "gz", None, None),
        P("af", None, None),
        P("af", None, None),
    )
    out_specs = (P("af", "gz", None, None), P(None, "gz", "af"), P(None, "gz", "af"))
    return jax.shard_map(
        functools.partial(body, mesh.shape["gz"], mesh.shape["af"]),
        mesh=mesh, in_specs=in_specs, out_specs=out_specs, check_vma=False,
    )
```

```python
import functools

import jax
import jax.numpy as jnp
from jax import lax
from jax.experimental import pallas as pl
from jax.experimental.pallas import tpu as pltpu
from jax.sharding import PartitionSpec as P

MESH = pl.DeviceIdType.MESH
BF = jnp.bfloat16
F32 = jnp.float32
ZRUN = 8
XRUN = 4
CUT = 384
PIECES = 2
ORDER = (0, -1, 1)
TAPS = 27
ACROSS = 128
last_dims = (((1,), (1,)), ((), ()))


def kernel(
    slabs, groups, own, height, cut,
    in_hbm, pre_hbm, og_hbm, w1_hbm, w2_hbm,
    ig_ref, f1_ref, f2_ref,
    in_ref, pre_ref, og_ref, w1_ref, w2_ref,
    rel, slope, field, G, WT, U, UP, PS, PR, SB, SR,
    KF, KS, KR, QS, QR,
    XF0, XS0, XR0, ZF0, ZS0, ZR0, HS0, HR0,
    XF1, XS1, XR1, ZF1, ZS1, ZR1, HS1, HR1,
    load_s, halo_s, halo_r, ag_s, ag_r, px_s, px_r, y_s, y_r, k_s, k_r, q_s, q_r,
    xs, xr, zs, zr, hs, hr,
):
    cells = height * ACROSS
    chips = groups // 2
    runs = slabs // ZRUN
    halves = runs // XRUN
    rows = groups * own
    share = rows // slabs
    k = lax.axis_index("gz")
    me = lax.axis_index("af")
    chip, core = me // 2, me % 2
    run, z = k // ZRUN, k % ZRUN
    hi, xi = run // XRUN, run % XRUN
    place = k % (ZRUN * XRUN)
    ends = (k == 0) | (k == slabs - 1)
    border = ((place == 0) | (place == ZRUN * XRUN - 1)) & jnp.logical_not(ends)
    inland = jnp.logical_not(ends | border)
    sibling = {"af": chip * 2 + (1 - core)}
    chip_at = lambda d: {"af": lax.rem(chip + d, chips) * 2 + core}
    z_at = lambda d: {"gz": run * ZRUN + lax.rem(z + d, ZRUN)}
    run_at = lambda d: {"gz": lax.rem(run + d, runs) * ZRUN + z}
    x_at = lambda d: {"gz": (hi * XRUN + lax.rem(xi + d, XRUN)) * ZRUN + z}
    hi_at = lambda d: {"gz": (lax.rem(hi + d, halves) * XRUN + xi) * ZRUN + z}
    above = {"gz": lax.rem(k + 1, slabs)}
    below = {"gz": lax.rem(k + slabs - 1, slabs)}
    filled = TAPS * own
    wide = G.shape[0]
    inner = slice(ACROSS, ACROSS + cells)
    part = cells // PIECES
    step = height // PIECES
    columns = ((0, wide), (cut, wide))
    xbufs = ((XF0, XS0, XR0, ZF0, ZS0, ZR0, HS0, HR0), (XF1, XS1, XR1, ZF1, ZS1, ZR1, HS1, HR1))

    loads = []
    for i, (src, dst) in enumerate(
        ((og_hbm, og_ref), (pre_hbm, pre_ref), (w2_hbm, w2_ref), (in_hbm, in_ref), (w1_hbm, w1_ref))
    ):
        loads.append(pltpu.make_async_copy(src, dst, load_s.at[i]))
        loads[-1].start()

    peers = [sibling, above, below]
    peers += [chip_at(d) for d in range(1, chips)]
    peers += [z_at(d) for d in range(1, ZRUN)]
    peers += [run_at(d) for d in range(1, runs)]
    barrier = pltpu.get_barrier_semaphore()
    for peer in peers:
        pl.semaphore_signal(barrier, inc=1, device_id=peer, device_id_type=MESH)

    started = []

    def remote(src, dst, s, r, to):
        return pltpu.make_async_remote_copy(
            src_ref=src, dst_ref=dst, send_sem=s, recv_sem=r, device_id=to, device_id_type=MESH
        )

    def send(src, dst, s, r, to):
        copy = remote(src, dst, s, r, to)
        copy.start()
        started.append(copy)
        return copy

    def planes_of(ref):
        rel[...] = ref[...].astype(F32).reshape(own * height, ACROSS)
        return [rel[pl.ds(x, own, stride=height), :] for x in range(height)]

    def at_x(x):
        return slice(x * ACROSS, (x + 1) * ACROSS)

    def halo_copies(l, q):
        own_plane, low, high = (field.at[l, p, q] for p in (1, 0, 2))
        up = remote(own_plane, low, halo_s.at[l, q, 0], halo_r.at[l, q, 0], above)
        down = remote(own_plane, high, halo_s.at[l, q, 1], halo_r.at[l, q, 1], below)
        return up, down

    def halo_send(l, q):
        up, down = halo_copies(l, q)
        pl.when(k < slabs - 1)(up.start)
        pl.when(k > 0)(down.start)

    def halo_wait(l, q):
        up, down = halo_copies(l, q)
        pl.when(k > 0)(up.wait_recv)
        pl.when(k < slabs - 1)(down.wait_recv)

    def halo_done(l, q):
        up, down = halo_copies(l, q)
        pl.when(k < slabs - 1)(up.wait_send)
        pl.when(k > 0)(down.wait_send)

    def gather_copies(l, low, high):
        mine = U.at[l, me, pl.ds(low, high - low)]
        i = l if low == 0 else 2
        found = [
            remote(mine, mine, ag_s.at[i, d], ag_r.at[i, d], chip_at(d)) for d in range(1, chips)
        ]
        started.extend(found)
        return found

    def start_when(when, copies):
        @pl.when(when)
        def _():
            for copy in copies:
                copy.start()

    def gather_sibling(l):
        mine = U.at[l, me]
        return send(mine, mine, ag_s.at[l, 0], ag_r.at[l, 0], sibling)

    def gather_forward(l, *found):
        onward = []
        for d in range(1, chips):
            for copies in found:
                copies[d - 1].wait_recv()
            block = U.at[l, lax.rem(chip + chips - d, chips) * 2 + core]
            onward.append(
                send(block, block, ag_s.at[l, chips - 1 + d], ag_r.at[l, chips - 1 + d], sibling)
            )
        return onward

    def gather_finish(onward):
        for copy in onward:
            copy.wait_recv()

    def reorder(l):
        low, mid, top = share.bit_length() - 1, runs.bit_length() - 1, ZRUN.bit_length() - 1
        to_row = lax.broadcasted_iota(jnp.int32, (rows, rows), 0)
        from_row = lax.broadcasted_iota(jnp.int32, (rows, rows), 1)
        wanted = (
            (((to_row >> low) & (runs - 1)) << (low + top))
            | ((to_row >> (low + mid)) << low)
            | (to_row & (share - 1))
        )
        move = jnp.where(from_row == wanted, 1.0, 0.0).astype(BF)
        for n in range(0, cells, 256):
            block = U[l, :, :, n : n + 256].reshape(rows, 256)
            UP[:, n : n + 256] = jnp.dot(move, block, preferred_element_type=F32).astype(BF)

    def turn(l, w_ref):
        third = filled // 3
        blocks = [w_ref[(a + 1) * third : (a + 2) * third, :] for a in ORDER]
        full = jnp.concatenate(blocks + [jnp.zeros((wide - filled, rows), BF)], axis=0).T
        for g in range(groups):
            WT[l, g % 2, (g // 2) * own : (g // 2 + 1) * own, :] = full[g * own : (g + 1) * own, :]

    lane = lax.broadcasted_iota(jnp.int32, (own, ACROSS), 1)
    number = lambda a, b, c: 9 * ORDER.index(a) + 3 * (b + 1) + (c + 1)
    tap_rows = lambda t: slice(t * own, (t + 1) * own)

    def build(l, p, q):
        a = 1 - p
        for x in range(q * step, (q + 1) * step):
            v = field[l, p, q, :, at_x(x - q * step)].astype(F32)
            for c in (-1, 0, 1):
                if c == 0:
                    s = v
                else:
                    edge = 0 if c == 1 else ACROSS - 1
                    s = jnp.where(lane == edge, 0.0, pltpu.roll(v, c % ACROSS, 1))
                s = s.astype(BF)
                for b in (-1, 0, 1):
                    if 0 <= x + b < height:
                        G[tap_rows(number(a, b, c)), at_x(x + b + 1)] = s

    def grad_product(l, half, which, q):
        for n in range(0, part, 256):
            at = slice(ACROSS + q * part + n, ACROSS + q * part + n + 256)
            PS[l, half, q, :, n : n + 256] = jnp.dot(
                WT[l, which], G[:, at], preferred_element_type=F32
            )

    def grad_first(l):
        copies = []
        for q in range(PIECES):
            grad_product(l, 0, 1 - core, q)
            copies.append(send(PS.at[l, 0, q], PR.at[l, q], px_s.at[l, q], px_r.at[l, q], sibling))
        return copies

    def grad_own(l):
        for q in range(PIECES):
            grad_product(l, 1, core, q)

    def grad_second(l, q, copy):
        copy.wait_recv()
        for j in range(chips):
            at = slice(j * own, (j + 1) * own)
            total = PS[l, 1, q, at, :] + PR[l, q, at, :]
            PS[l, 1, q, at, :] = total
            SB[l, q, j] = total.astype(BF)
        return [
            send(
                SB.at[l, q, lax.rem(chip + d, chips)], SR.at[l, q, d - 1],
                y_s.at[l, q, d - 1], y_r.at[l, q, d - 1], chip_at(d),
            )
            for d in range(1, chips)
        ]

    def grad_last(l, q, found):
        for copy in found:
            copy.wait_recv()
        mine = pl.ds(pl.multiple_of(chip * own, own), own)
        total = PS[l, 1, q, mine, :]
        for d in range(chips - 1):
            total = total + SR[l, q, d].astype(F32)
        return total

    def by_tap(total, start, out_ref):
        for i in range(total.shape[1] // own):
            block = start // own + i
            if block < TAPS:
                out_ref[9 * (ORDER[block // 9] + 1) + block % 9] = total[:, i * own : (i + 1) * own]

    def z_first():
        for n in range(0, cut, 256):
            size = min(256, cut - n)
            at = slice(n, n + size)
            block = lax.dot_general(
                UP[...], G[n : n + size, inner], last_dims, preferred_element_type=F32
            ).reshape(ZRUN, runs * share, size)
            KF[:, :, at] = block
            KS[:, :, at] = block.astype(BF)
        return [
            send(
                KS.at[lax.rem(z + d, ZRUN)], KR.at[d - 1],
                k_s.at[d - 1], k_r.at[d - 1], z_at(d),
            )
            for d in range(1, ZRUN)
        ]

    def z_first_then(copies):
        for copy in copies:
            copy.wait_recv()
        for n in range(0, KF.shape[2], 128):
            at = slice(n, n + 128)
            total = KF[z, :, at]
            for d in range(ZRUN - 1):
                total = total + KR[d, :, at].astype(F32)
            for j in range(runs):
                QS[j, :, at] = total[j * share : (j + 1) * share, :]
        return [
            send(
                QS.at[lax.rem(run + d, runs)], QR.at[d - 1],
                q_s.at[d - 1], q_r.at[d - 1], run_at(d),
            )
            for d in range(1, runs)
        ]

    def z_first_last(copies, out_ref):
        for copy in copies:
            copy.wait_recv()
        total = QS[run]
        for d in range(runs - 1):
            total = total + QR[d]
        by_tap(total, 0, out_ref)

    def x_first(l):
        start, stop = columns[l]
        XF, XS, XR = xbufs[l][:3]
        for n in range(start, stop, 256):
            size = min(256, stop - n)
            at = slice(n - start, n - start + size)
            block = lax.dot_general(
                U[l].reshape(rows, cells), G[n : n + size, inner], last_dims,
                preferred_element_type=F32,
            )
            for h in range(halves):
                for x in range(XRUN):
                    j = (h * XRUN + x) * ZRUN * share
                    part = block[j : j + ZRUN * share, :]
                    XF[x, h, :, at] = part
                    XS[x, h, :, at] = part.astype(BF)
        return [
            send(
                XS.at[lax.rem(xi + d, XRUN)], XR.at[d - 1],
                xs.at[l, d - 1], xr.at[l, d - 1], x_at(d),
            )
            for d in range(1, XRUN)
        ]

    def x_first_then(l, copies):
        start, stop = columns[l]
        XF, XS, XR, ZF, ZS, ZR = xbufs[l][:6]
        eight = halves * share
        for copy in copies:
            copy.wait_recv()
        for n in range(0, stop - start, 128):
            at = slice(n, n + 128)
            fold, to = divmod(n, ZS.shape[2])
            to = slice(to, to + 128)
            for h in range(halves):
                total = XF[xi, h, :, at]
                for d in range(XRUN - 1):
                    total = total + XR[d, h, :, at].astype(F32)
                first = fold * eight + h * share
                for j in range(ZRUN):
                    ZF[j, first : first + share, to] = total[j * share : (j + 1) * share, :]
        for j in range(ZRUN):
            ZS[j] = ZF[j].astype(BF)
        return [
            send(
                ZS.at[lax.rem(z + d, ZRUN)], ZR.at[d - 1],
                zs.at[l, d - 1], zr.at[l, d - 1], z_at(d),
            )
            for d in range(1, ZRUN)
        ]

    def x_first_pair(l, copies):
        start, stop = columns[l]
        ZF, ZS, ZR, HS, HR = xbufs[l][3:]
        eight = halves * share
        for copy in copies:
            copy.wait_recv()
        total = ZF[z]
        for d in range(ZRUN - 1):
            total = total + ZR[d].astype(F32)
        fold = total.shape[1]
        for h in range(halves):
            HS[h, :, :fold] = total[h * share : (h + 1) * share, :]
            rest = stop - start - fold
            HS[h, :, fold:] = total[eight + h * share : eight + (h + 1) * share, :rest]
        return [
            send(
                HS.at[lax.rem(hi + d, halves)], HR.at[d - 1],
                hs.at[l, d - 1], hr.at[l, d - 1], hi_at(d),
            )
            for d in range(1, halves)
        ]

    def x_first_last(l, copies, out_ref):
        start, stop = columns[l]
        HS, HR = xbufs[l][6:]
        for copy in copies:
            copy.wait_recv()
        total = HS[hi]
        for d in range(halves - 1):
            total = total + HR[d]
        by_tap(total, start, out_ref)

    loads[0].wait()
    for x, v in enumerate(planes_of(og_ref)):
        field[0, 1, x // step, :, at_x(x % step)] = v.astype(BF)

    @pl.when(k == 0)
    def _():
        for l in range(2):
            field[l, 0] = jnp.zeros(field.shape[2:], BF)

    @pl.when(k == slabs - 1)
    def _():
        for l in range(2):
            field[l, 2] = jnp.zeros(field.shape[2:], BF)

    pl.semaphore_wait(barrier, len(peers))
    for q in range(PIECES):
        halo_send(0, q)
    loads[1].wait()
    for x, v in enumerate(planes_of(pre_ref)):
        slope[x // step, :, at_x(x % step)] = jnp.where(v > 0, jnp.float32(1.0), jnp.float32(0.3))
        U[0, me, :, at_x(x)] = jnp.where(v > 0, v, 0.3 * v).astype(BF)
    gather_act = gather_copies(0, 0, own)
    start_when(jnp.logical_not(ends), gather_act)
    near_act = gather_sibling(0)
    loads[3].wait()
    for x, v in enumerate(planes_of(in_ref)):
        U[1, me, :, at_x(x)] = v.astype(BF)
    gather_in = gather_copies(1, 0, own // 2)
    start_when(inland, gather_in)

    none = jnp.zeros((own, ACROSS), BF)
    for a in (-1, 0, 1):
        for c in (-1, 0, 1):
            G[tap_rows(number(a, 1, c)), at_x(1)] = none
            G[tap_rows(number(a, -1, c)), at_x(height)] = none
    if wide > filled:
        G[filled:, :] = jnp.zeros((wide - filled, G.shape[1]), BF)

    def finish_taps(l):
        for q in range(PIECES):
            halo_wait(l, q)
            build(l, 0, q)
            build(l, 2, q)

    for q in range(PIECES):
        build(0, 1, q)
    loads[2].wait()
    turn(0, w2_ref)
    finish_taps(0)
    start_when(border, gather_in)
    pair = grad_first(0)
    grad_own(0)
    parts = [grad_second(0, q, pair[q]) for q in range(PIECES)]
    start_when(ends, gather_act + gather_in)
    onward = gather_forward(0, gather_act)
    loads[4].wait()
    turn(1, w1_ref)
    gather_finish(onward + [near_act])
    two = x_first(0)
    for q in range(PIECES):
        field[1, 1, q] = (grad_last(0, q, parts[q]) * slope[q]).astype(BF)
        halo_send(1, q)
    gather_rest = gather_copies(1, own // 2, own)
    for copy in gather_rest:
        copy.start()
    near_in = gather_sibling(1)
    for q in range(PIECES):
        build(1, 1, q)
    onward = gather_forward(1, gather_in, gather_rest)
    finish_taps(1)
    pair = grad_first(1)
    gather_finish(onward + [near_in])
    one_x = x_first(1)
    reorder(1)
    one_z = z_first()
    grad_own(1)
    parts = [grad_second(1, q, pair[q]) for q in range(PIECES)]
    two = x_first_then(0, two)
    one_x = x_first_then(1, one_x)
    one_z = z_first_then(one_z)
    two = x_first_pair(0, two)
    for q in range(PIECES):
        total = grad_last(1, q, parts[q])
        for x in range(step):
            rel[pl.ds(q * step + x, own, stride=height), :] = total[:, at_x(x)]
    ig_ref[...] = rel[...].reshape(own, height, ACROSS).astype(BF)
    one_x = x_first_pair(1, one_x)
    x_first_last(0, two, f2_ref)
    z_first_last(one_z, f1_ref)
    for l in range(2):
        for q in range(PIECES):
            halo_done(l, q)
    for copy in started:
        copy.wait_send()
    x_first_last(1, one_x, f1_ref)


def body(slabs, groups, inputs, pre_acts, out_grad, weight_one, weight_two):
    own, planes, height, across = out_grad.shape
    channels = weight_one.shape[2]
    cells = height * across
    chips = groups // 2
    runs = slabs // ZRUN
    halves = runs // XRUN
    share = channels // slabs
    wide = -(-TAPS * own // 128) * 128
    cut = CUT
    flat = lambda v: v.reshape(own, height, across)
    taps = lambda w: jnp.transpose(w, (1, 0, 2)).reshape(TAPS * own, channels)
    results = [
        jax.ShapeDtypeStruct((own, height, across), BF),
        jax.ShapeDtypeStruct((TAPS, share, own), F32),
        jax.ShapeDtypeStruct((TAPS, share, own), F32),
    ]
    piece = cells // PIECES
    fold = lambda width: -(-width // 256) * 128
    scratch = [pltpu.VMEM((own, height, across), BF)] * 3
    scratch += [pltpu.VMEM((TAPS * own, channels), BF)] * 2
    scratch += [
        pltpu.VMEM((own * height, across), F32),
        pltpu.VMEM((PIECES, own, piece), F32),
        pltpu.VMEM((2, 3, PIECES, own, piece), BF),
        pltpu.VMEM((wide, cells + 2 * across), BF),
        pltpu.VMEM((2, 2, chips * own, wide), BF),
        pltpu.VMEM((2, groups, own, cells), BF),
        pltpu.VMEM((channels, cells), BF),
        pltpu.VMEM((2, 2, PIECES, chips * own, piece), F32),
        pltpu.VMEM((2, PIECES, chips * own, piece), F32),
        pltpu.VMEM((2, PIECES, chips, own, piece), BF),
        pltpu.VMEM((2, PIECES, chips - 1, own, piece), BF),
    ]
    scratch += [
        pltpu.VMEM((ZRUN, runs * share, cut), F32),
        pltpu.VMEM((ZRUN, runs * share, cut), BF),
        pltpu.VMEM((ZRUN - 1, runs * share, cut), BF),
        pltpu.VMEM((runs, share, cut), F32),
        pltpu.VMEM((runs - 1, share, cut), F32),
    ]
    for width in (wide, wide - cut):
        scratch += [
            pltpu.VMEM((XRUN, halves, ZRUN * share, width), F32),
            pltpu.VMEM((XRUN, halves, ZRUN * share, width), BF),
            pltpu.VMEM((XRUN - 1, halves, ZRUN * share, width), BF),
            pltpu.VMEM((ZRUN, 2 * halves * share, fold(width)), F32),
            pltpu.VMEM((ZRUN, 2 * halves * share, fold(width)), BF),
            pltpu.VMEM((ZRUN - 1, 2 * halves * share, fold(width)), BF),
            pltpu.VMEM((halves, share, width), F32),
            pltpu.VMEM((halves - 1, share, width), F32),
        ]
    scratch.append(pltpu.SemaphoreType.DMA((5,)))
    for shape in (
        (2, PIECES, 2), (3, 2 * chips - 1), (2, PIECES), (2, PIECES, chips - 1), (ZRUN - 1,), (runs - 1,),
        (2, XRUN - 1), (2, ZRUN - 1), (2, halves - 1),
    ):
        scratch += [pltpu.SemaphoreType.DMA(shape), pltpu.SemaphoreType.DMA(shape)]
    arrays = (flat(inputs), flat(pre_acts), flat(out_grad), taps(weight_one), taps(weight_two))
    input_grad, one, two = pl.pallas_call(
        functools.partial(kernel, slabs, groups, own, height, cut),
        out_shape=results,
        in_specs=[pl.BlockSpec(memory_space=pltpu.HBM)] * 5,
        out_specs=[pl.BlockSpec(memory_space=pltpu.VMEM)] * 3,
        scratch_shapes=scratch,
        compiler_params=pltpu.CompilerParams(
            collective_id=0, has_side_effects=True, vmem_limit_bytes=48 * 1024 * 1024
        ),
        name="conv_back",
    )(*[pltpu.with_memory_space_constraint(v, pltpu.HBM) for v in arrays])
    return input_grad.reshape(own, planes, height, across), one, two


def solution(mesh):
    in_specs = (
        P("af", "gz", None, None),
        P("af", "gz", None, None),
        P("af", "gz", None, None),
        P("af", None, None),
        P("af", None, None),
    )
    out_specs = (P("af", "gz", None, None), P(None, "gz", "af"), P(None, "gz", "af"))
    return jax.shard_map(
        functools.partial(body, mesh.shape["gz"], mesh.shape["af"]),
        mesh=mesh, in_specs=in_specs, out_specs=out_specs, check_vma=False,
    )
```

```python
import functools

import jax
import jax.numpy as jnp
from jax import lax
from jax.experimental import pallas as pl
from jax.experimental.pallas import tpu as pltpu
from jax.sharding import PartitionSpec as P

MESH = pl.DeviceIdType.MESH
BF = jnp.bfloat16
F32 = jnp.float32
ZRUN = 8
XRUN = 4
CUT = 384
PIECES = 2
ORDER = (0, -1, 1)
TAPS = 27
ACROSS = 128
last_dims = (((1,), (1,)), ((), ()))


def kernel(
    slabs, groups, own, height, cut,
    in_hbm, pre_hbm, og_hbm, w1_hbm, w2_hbm,
    ig_ref, f1_ref, f2_ref,
    in_ref, pre_ref, og_ref, w1_ref, w2_ref,
    rel, slope, field, G, WT, U, UP, PB, PS, PR, SB, SR,
    KF, KS, KR, QS, QR,
    XF0, XS0, XR0, ZF0, ZS0, ZR0, HS0, HR0,
    XF1, XS1, XR1, ZF1, ZS1, ZR1, HS1, HR1,
    load_s, halo_s, halo_r, ag_s, ag_r, px_s, px_r, y_s, y_r, k_s, k_r, q_s, q_r,
    xs, xr, zs, zr, hs, hr,
):
    cells = height * ACROSS
    chips = groups // 2
    runs = slabs // ZRUN
    halves = runs // XRUN
    rows = groups * own
    share = rows // slabs
    k = lax.axis_index("gz")
    me = lax.axis_index("af")
    chip, core = me // 2, me % 2
    run, z = k // ZRUN, k % ZRUN
    hi, xi = run // XRUN, run % XRUN
    place = k % (ZRUN * XRUN)
    ends = (k == 0) | (k == slabs - 1)
    border = ((place == 0) | (place == ZRUN * XRUN - 1)) & jnp.logical_not(ends)
    inland = jnp.logical_not(ends | border)
    sibling = {"af": chip * 2 + (1 - core)}
    chip_at = lambda d: {"af": lax.rem(chip + d, chips) * 2 + core}
    z_at = lambda d: {"gz": run * ZRUN + lax.rem(z + d, ZRUN)}
    run_at = lambda d: {"gz": lax.rem(run + d, runs) * ZRUN + z}
    x_at = lambda d: {"gz": (hi * XRUN + lax.rem(xi + d, XRUN)) * ZRUN + z}
    hi_at = lambda d: {"gz": (lax.rem(hi + d, halves) * XRUN + xi) * ZRUN + z}
    above = {"gz": lax.rem(k + 1, slabs)}
    below = {"gz": lax.rem(k + slabs - 1, slabs)}
    filled = TAPS * own
    wide = G.shape[0]
    inner = slice(ACROSS, ACROSS + cells)
    part = cells // PIECES
    step = height // PIECES
    columns = ((0, wide), (cut, wide))
    xbufs = ((XF0, XS0, XR0, ZF0, ZS0, ZR0, HS0, HR0), (XF1, XS1, XR1, ZF1, ZS1, ZR1, HS1, HR1))

    loads = []
    for i, (src, dst) in enumerate(
        ((og_hbm, og_ref), (pre_hbm, pre_ref), (w2_hbm, w2_ref), (in_hbm, in_ref), (w1_hbm, w1_ref))
    ):
        loads.append(pltpu.make_async_copy(src, dst, load_s.at[i]))
        loads[-1].start()

    peers = [sibling, above, below]
    peers += [chip_at(d) for d in range(1, chips)]
    peers += [z_at(d) for d in range(1, ZRUN)]
    peers += [run_at(d) for d in range(1, runs)]
    barrier = pltpu.get_barrier_semaphore()
    for peer in peers:
        pl.semaphore_signal(barrier, inc=1, device_id=peer, device_id_type=MESH)

    started = []

    def remote(src, dst, s, r, to):
        return pltpu.make_async_remote_copy(
            src_ref=src, dst_ref=dst, send_sem=s, recv_sem=r, device_id=to, device_id_type=MESH
        )

    def send(src, dst, s, r, to):
        copy = remote(src, dst, s, r, to)
        copy.start()
        started.append(copy)
        return copy

    def planes_of(ref):
        rel[...] = ref[...].astype(F32).reshape(own * height, ACROSS)
        return [rel[pl.ds(x, own, stride=height), :] for x in range(height)]

    def at_x(x):
        return slice(x * ACROSS, (x + 1) * ACROSS)

    def halo_copies(l, q):
        own_plane, low, high = (field.at[l, p, q] for p in (1, 0, 2))
        up = remote(own_plane, low, halo_s.at[l, q, 0], halo_r.at[l, q, 0], above)
        down = remote(own_plane, high, halo_s.at[l, q, 1], halo_r.at[l, q, 1], below)
        return up, down

    def halo_send(l, q):
        up, down = halo_copies(l, q)
        pl.when(k < slabs - 1)(up.start)
        pl.when(k > 0)(down.start)

    def halo_wait(l, q):
        up, down = halo_copies(l, q)
        pl.when(k > 0)(up.wait_recv)
        pl.when(k < slabs - 1)(down.wait_recv)

    def halo_done(l, q):
        up, down = halo_copies(l, q)
        pl.when(k < slabs - 1)(up.wait_send)
        pl.when(k > 0)(down.wait_send)

    def gather_copies(l, low, high):
        mine = U.at[l, me, pl.ds(low, high - low)]
        i = l if low == 0 else 2
        found = [
            remote(mine, mine, ag_s.at[i, d], ag_r.at[i, d], chip_at(d)) for d in range(1, chips)
        ]
        started.extend(found)
        return found

    def start_when(when, copies):
        @pl.when(when)
        def _():
            for copy in copies:
                copy.start()

    def gather_sibling(l):
        mine = U.at[l, me]
        return send(mine, mine, ag_s.at[l, 0], ag_r.at[l, 0], sibling)

    def gather_forward(l, *found):
        onward = []
        for d in range(1, chips):
            for copies in found:
                copies[d - 1].wait_recv()
            block = U.at[l, lax.rem(chip + chips - d, chips) * 2 + core]
            onward.append(
                send(block, block, ag_s.at[l, chips - 1 + d], ag_r.at[l, chips - 1 + d], sibling)
            )
        return onward

    def gather_finish(onward):
        for copy in onward:
            copy.wait_recv()

    def reorder(l):
        low, mid, top = share.bit_length() - 1, runs.bit_length() - 1, ZRUN.bit_length() - 1
        to_row = lax.broadcasted_iota(jnp.int32, (rows, rows), 0)
        from_row = lax.broadcasted_iota(jnp.int32, (rows, rows), 1)
        wanted = (
            (((to_row >> low) & (runs - 1)) << (low + top))
            | ((to_row >> (low + mid)) << low)
            | (to_row & (share - 1))
        )
        move = jnp.where(from_row == wanted, 1.0, 0.0).astype(BF)
        for n in range(0, cells, 256):
            block = U[l, :, :, n : n + 256].reshape(rows, 256)
            UP[:, n : n + 256] = jnp.dot(move, block, preferred_element_type=F32).astype(BF)

    def turn(l, w_ref):
        third = filled // 3
        blocks = [w_ref[(a + 1) * third : (a + 2) * third, :] for a in ORDER]
        full = jnp.concatenate(blocks + [jnp.zeros((wide - filled, rows), BF)], axis=0).T
        for g in range(groups):
            WT[l, g % 2, (g // 2) * own : (g // 2 + 1) * own, :] = full[g * own : (g + 1) * own, :]

    lane = lax.broadcasted_iota(jnp.int32, (own, ACROSS), 1)
    number = lambda a, b, c: 9 * ORDER.index(a) + 3 * (b + 1) + (c + 1)
    tap_rows = lambda t: slice(t * own, (t + 1) * own)

    def build(l, p, q):
        a = 1 - p
        for x in range(q * step, (q + 1) * step):
            v = field[l, p, q, :, at_x(x - q * step)].astype(F32)
            for c in (-1, 0, 1):
                if c == 0:
                    s = v
                else:
                    edge = 0 if c == 1 else ACROSS - 1
                    s = jnp.where(lane == edge, 0.0, pltpu.roll(v, c % ACROSS, 1))
                s = s.astype(BF)
                for b in (-1, 0, 1):
                    if 0 <= x + b < height:
                        G[tap_rows(number(a, b, c)), at_x(x + b + 1)] = s

    def grad_product(l, which, q, to):
        for n in range(0, part, 256):
            at = slice(ACROSS + q * part + n, ACROSS + q * part + n + 256)
            block = jnp.dot(WT[l, which], G[:, at], preferred_element_type=F32)
            to[l, q, :, n : n + 256] = block.astype(to.dtype)

    def grad_first(l):
        copies = []
        for q in range(PIECES):
            grad_product(l, 1 - core, q, PB)
            copies.append(send(PB.at[l, q], PR.at[l, q], px_s.at[l, q], px_r.at[l, q], sibling))
        return copies

    def grad_own(l):
        for q in range(PIECES):
            grad_product(l, core, q, PS)

    def grad_second(l, q, copy):
        copy.wait_recv()
        for j in range(chips):
            at = slice(j * own, (j + 1) * own)
            total = PS[l, q, at, :] + PR[l, q, at, :].astype(F32)
            PS[l, q, at, :] = total
            SB[l, q, j] = total.astype(BF)
        return [
            send(
                SB.at[l, q, lax.rem(chip + d, chips)], SR.at[l, q, d - 1],
                y_s.at[l, q, d - 1], y_r.at[l, q, d - 1], chip_at(d),
            )
            for d in range(1, chips)
        ]

    def grad_last(l, q, found):
        for copy in found:
            copy.wait_recv()
        mine = pl.ds(pl.multiple_of(chip * own, own), own)
        total = PS[l, q, mine, :]
        for d in range(chips - 1):
            total = total + SR[l, q, d].astype(F32)
        return total

    def by_tap(total, start, out_ref):
        for i in range(total.shape[1] // own):
            block = start // own + i
            if block < TAPS:
                out_ref[9 * (ORDER[block // 9] + 1) + block % 9] = total[:, i * own : (i + 1) * own]

    def z_first():
        for n in range(0, cut, 256):
            size = min(256, cut - n)
            at = slice(n, n + size)
            block = lax.dot_general(
                UP[...], G[n : n + size, inner], last_dims, preferred_element_type=F32
            ).reshape(ZRUN, runs * share, size)
            KF[:, :, at] = block
            KS[:, :, at] = block.astype(BF)
        return [
            send(
                KS.at[lax.rem(z + d, ZRUN)], KR.at[d - 1],
                k_s.at[d - 1], k_r.at[d - 1], z_at(d),
            )
            for d in range(1, ZRUN)
        ]

    def z_first_then(copies):
        for copy in copies:
            copy.wait_recv()
        for n in range(0, KF.shape[2], 128):
            at = slice(n, n + 128)
            total = KF[z, :, at]
            for d in range(ZRUN - 1):
                total = total + KR[d, :, at].astype(F32)
            for j in range(runs):
                QS[j, :, at] = total[j * share : (j + 1) * share, :]
        return [
            send(
                QS.at[lax.rem(run + d, runs)], QR.at[d - 1],
                q_s.at[d - 1], q_r.at[d - 1], run_at(d),
            )
            for d in range(1, runs)
        ]

    def z_first_last(copies, out_ref):
        for copy in copies:
            copy.wait_recv()
        total = QS[run]
        for d in range(runs - 1):
            total = total + QR[d]
        by_tap(total, 0, out_ref)

    def x_first(l):
        start, stop = columns[l]
        XF, XS, XR = xbufs[l][:3]
        for n in range(start, stop, 256):
            size = min(256, stop - n)
            at = slice(n - start, n - start + size)
            block = lax.dot_general(
                U[l].reshape(rows, cells), G[n : n + size, inner], last_dims,
                preferred_element_type=F32,
            )
            for h in range(halves):
                for x in range(XRUN):
                    j = (h * XRUN + x) * ZRUN * share
                    part = block[j : j + ZRUN * share, :]
                    XF[x, h, :, at] = part
                    XS[x, h, :, at] = part.astype(BF)
        return [
            send(
                XS.at[lax.rem(xi + d, XRUN)], XR.at[d - 1],
                xs.at[l, d - 1], xr.at[l, d - 1], x_at(d),
            )
            for d in range(1, XRUN)
        ]

    def x_first_then(l, copies):
        start, stop = columns[l]
        XF, XS, XR, ZF, ZS, ZR = xbufs[l][:6]
        eight = halves * share
        for copy in copies:
            copy.wait_recv()
        for n in range(0, stop - start, 128):
            at = slice(n, n + 128)
            fold, to = divmod(n, ZS.shape[2])
            to = slice(to, to + 128)
            for h in range(halves):
                total = XF[xi, h, :, at]
                for d in range(XRUN - 1):
                    total = total + XR[d, h, :, at].astype(F32)
                first = fold * eight + h * share
                for j in range(ZRUN):
                    ZF[j, first : first + share, to] = total[j * share : (j + 1) * share, :]
        for j in range(ZRUN):
            ZS[j] = ZF[j].astype(BF)
        return [
            send(
                ZS.at[lax.rem(z + d, ZRUN)], ZR.at[d - 1],
                zs.at[l, d - 1], zr.at[l, d - 1], z_at(d),
            )
            for d in range(1, ZRUN)
        ]

    def x_first_pair(l, copies):
        start, stop = columns[l]
        ZF, ZS, ZR, HS, HR = xbufs[l][3:]
        eight = halves * share
        for copy in copies:
            copy.wait_recv()
        total = ZF[z]
        for d in range(ZRUN - 1):
            total = total + ZR[d].astype(F32)
        fold = total.shape[1]
        for h in range(halves):
            HS[h, :, :fold] = total[h * share : (h + 1) * share, :]
            rest = stop - start - fold
            HS[h, :, fold:] = total[eight + h * share : eight + (h + 1) * share, :rest]
        return [
            send(
                HS.at[lax.rem(hi + d, halves)], HR.at[d - 1],
                hs.at[l, d - 1], hr.at[l, d - 1], hi_at(d),
            )
            for d in range(1, halves)
        ]

    def x_first_last(l, copies, out_ref):
        start, stop = columns[l]
        HS, HR = xbufs[l][6:]
        for copy in copies:
            copy.wait_recv()
        total = HS[hi]
        for d in range(halves - 1):
            total = total + HR[d]
        by_tap(total, start, out_ref)

    loads[0].wait()
    for x, v in enumerate(planes_of(og_ref)):
        field[0, 1, x // step, :, at_x(x % step)] = v.astype(BF)

    @pl.when(k == 0)
    def _():
        for l in range(2):
            field[l, 0] = jnp.zeros(field.shape[2:], BF)

    @pl.when(k == slabs - 1)
    def _():
        for l in range(2):
            field[l, 2] = jnp.zeros(field.shape[2:], BF)

    pl.semaphore_wait(barrier, len(peers))
    for q in range(PIECES):
        halo_send(0, q)
    loads[1].wait()
    for x, v in enumerate(planes_of(pre_ref)):
        slope[x // step, :, at_x(x % step)] = jnp.where(v > 0, jnp.float32(1.0), jnp.float32(0.3))
        U[0, me, :, at_x(x)] = jnp.where(v > 0, v, 0.3 * v).astype(BF)
    gather_act = gather_copies(0, 0, own)
    start_when(jnp.logical_not(ends), gather_act)
    near_act = gather_sibling(0)
    loads[3].wait()
    for x, v in enumerate(planes_of(in_ref)):
        U[1, me, :, at_x(x)] = v.astype(BF)
    gather_in = gather_copies(1, 0, own // 2)
    start_when(inland, gather_in)

    none = jnp.zeros((own, ACROSS), BF)
    for a in (-1, 0, 1):
        for c in (-1, 0, 1):
            G[tap_rows(number(a, 1, c)), at_x(1)] = none
            G[tap_rows(number(a, -1, c)), at_x(height)] = none
    if wide > filled:
        G[filled:, :] = jnp.zeros((wide - filled, G.shape[1]), BF)

    def finish_taps(l):
        for q in range(PIECES):
            halo_wait(l, q)
            build(l, 0, q)
            build(l, 2, q)

    for q in range(PIECES):
        build(0, 1, q)
    loads[2].wait()
    turn(0, w2_ref)
    finish_taps(0)
    start_when(border, gather_in)
    pair = grad_first(0)
    grad_own(0)
    parts = [grad_second(0, q, pair[q]) for q in range(PIECES)]
    start_when(ends, gather_act + gather_in)
    onward = gather_forward(0, gather_act)
    loads[4].wait()
    turn(1, w1_ref)
    gather_finish(onward + [near_act])
    two = x_first(0)
    for q in range(PIECES):
        field[1, 1, q] = (grad_last(0, q, parts[q]) * slope[q]).astype(BF)
        halo_send(1, q)
    gather_rest = gather_copies(1, own // 2, own)
    for copy in gather_rest:
        copy.start()
    near_in = gather_sibling(1)
    for q in range(PIECES):
        build(1, 1, q)
    onward = gather_forward(1, gather_in, gather_rest)
    finish_taps(1)
    pair = grad_first(1)
    two = x_first_then(0, two)
    gather_finish(onward + [near_in])
    one_x = x_first(1)
    reorder(1)
    one_z = z_first()
    grad_own(1)
    parts = [grad_second(1, q, pair[q]) for q in range(PIECES)]
    one_x = x_first_then(1, one_x)
    one_z = z_first_then(one_z)
    two = x_first_pair(0, two)
    for q in range(PIECES):
        total = grad_last(1, q, parts[q])
        for x in range(step):
            rel[pl.ds(q * step + x, own, stride=height), :] = total[:, at_x(x)]
    ig_ref[...] = rel[...].reshape(own, height, ACROSS).astype(BF)
    one_x = x_first_pair(1, one_x)
    x_first_last(0, two, f2_ref)
    z_first_last(one_z, f1_ref)
    for l in range(2):
        for q in range(PIECES):
            halo_done(l, q)
    for copy in started:
        copy.wait_send()
    x_first_last(1, one_x, f1_ref)


def body(slabs, groups, inputs, pre_acts, out_grad, weight_one, weight_two):
    own, planes, height, across = out_grad.shape
    channels = weight_one.shape[2]
    cells = height * across
    chips = groups // 2
    runs = slabs // ZRUN
    halves = runs // XRUN
    share = channels // slabs
    wide = -(-TAPS * own // 128) * 128
    cut = CUT
    flat = lambda v: v.reshape(own, height, across)
    taps = lambda w: jnp.transpose(w, (1, 0, 2)).reshape(TAPS * own, channels)
    results = [
        jax.ShapeDtypeStruct((own, height, across), BF),
        jax.ShapeDtypeStruct((TAPS, share, own), F32),
        jax.ShapeDtypeStruct((TAPS, share, own), F32),
    ]
    piece = cells // PIECES
    fold = lambda width: -(-width // 256) * 128
    scratch = [pltpu.VMEM((own, height, across), BF)] * 3
    scratch += [pltpu.VMEM((TAPS * own, channels), BF)] * 2
    scratch += [
        pltpu.VMEM((own * height, across), F32),
        pltpu.VMEM((PIECES, own, piece), F32),
        pltpu.VMEM((2, 3, PIECES, own, piece), BF),
        pltpu.VMEM((wide, cells + 2 * across), BF),
        pltpu.VMEM((2, 2, chips * own, wide), BF),
        pltpu.VMEM((2, groups, own, cells), BF),
        pltpu.VMEM((channels, cells), BF),
        pltpu.VMEM((2, PIECES, chips * own, piece), BF),
        pltpu.VMEM((2, PIECES, chips * own, piece), F32),
        pltpu.VMEM((2, PIECES, chips * own, piece), BF),
        pltpu.VMEM((2, PIECES, chips, own, piece), BF),
        pltpu.VMEM((2, PIECES, chips - 1, own, piece), BF),
    ]
    scratch += [
        pltpu.VMEM((ZRUN, runs * share, cut), F32),
        pltpu.VMEM((ZRUN, runs * share, cut), BF),
        pltpu.VMEM((ZRUN - 1, runs * share, cut), BF),
        pltpu.VMEM((runs, share, cut), F32),
        pltpu.VMEM((runs - 1, share, cut), F32),
    ]
    for width in (wide, wide - cut):
        scratch += [
            pltpu.VMEM((XRUN, halves, ZRUN * share, width), F32),
            pltpu.VMEM((XRUN, halves, ZRUN * share, width), BF),
            pltpu.VMEM((XRUN - 1, halves, ZRUN * share, width), BF),
            pltpu.VMEM((ZRUN, 2 * halves * share, fold(width)), F32),
            pltpu.VMEM((ZRUN, 2 * halves * share, fold(width)), BF),
            pltpu.VMEM((ZRUN - 1, 2 * halves * share, fold(width)), BF),
            pltpu.VMEM((halves, share, width), F32),
            pltpu.VMEM((halves - 1, share, width), F32),
        ]
    scratch.append(pltpu.SemaphoreType.DMA((5,)))
    for shape in (
        (2, PIECES, 2), (3, 2 * chips - 1), (2, PIECES), (2, PIECES, chips - 1), (ZRUN - 1,), (runs - 1,),
        (2, XRUN - 1), (2, ZRUN - 1), (2, halves - 1),
    ):
        scratch += [pltpu.SemaphoreType.DMA(shape), pltpu.SemaphoreType.DMA(shape)]
    arrays = (flat(inputs), flat(pre_acts), flat(out_grad), taps(weight_one), taps(weight_two))
    input_grad, one, two = pl.pallas_call(
        functools.partial(kernel, slabs, groups, own, height, cut),
        out_shape=results,
        in_specs=[pl.BlockSpec(memory_space=pltpu.HBM)] * 5,
        out_specs=[pl.BlockSpec(memory_space=pltpu.VMEM)] * 3,
        scratch_shapes=scratch,
        compiler_params=pltpu.CompilerParams(
            collective_id=0, has_side_effects=True, vmem_limit_bytes=48 * 1024 * 1024
        ),
        name="conv_back",
    )(*[pltpu.with_memory_space_constraint(v, pltpu.HBM) for v in arrays])
    return input_grad.reshape(own, planes, height, across), one, two


def solution(mesh):
    in_specs = (
        P("af", "gz", None, None),
        P("af", "gz", None, None),
        P("af", "gz", None, None),
        P("af", None, None),
        P("af", None, None),
    )
    out_specs = (P("af", "gz", None, None), P(None, "gz", "af"), P(None, "gz", "af"))
    return jax.shard_map(
        functools.partial(body, mesh.shape["gz"], mesh.shape["af"]),
        mesh=mesh, in_specs=in_specs, out_specs=out_specs, check_vma=False,
    )
```

```python
import functools

import jax
import jax.numpy as jnp
from jax import lax
from jax.experimental import pallas as pl
from jax.experimental.pallas import tpu as pltpu
from jax.sharding import PartitionSpec as P

MESH = pl.DeviceIdType.MESH
BF = jnp.bfloat16
F32 = jnp.float32
ZRUN = 8
XRUN = 4
CUT = 384
PIECES = 2
ORDER = (0, -1, 1)
TAPS = 27
ACROSS = 128
last_dims = (((1,), (1,)), ((), ()))


def kernel(
    slabs, groups, own, height, cut,
    in_hbm, pre_hbm, og_hbm, w1_hbm, w2_hbm,
    ig_ref, f1_ref, f2_ref,
    in_ref, pre_ref, og_ref, w1_ref, w2_ref,
    rel, slope, field, G, WT, U, UP, PB, PS, PR, SB, SR,
    KF, KS, KR, QS, QR,
    XF0, XS0, XR0, ZF0, ZS0, ZR0, HS0, HR0,
    XF1, XS1, XR1, ZF1, ZS1, ZR1, HS1, HR1,
    load_s, halo_s, halo_r, ag_s, ag_r, px_s, px_r, y_s, y_r, k_s, k_r, q_s, q_r,
    xs, xr, zs, zr, hs, hr,
):
    cells = height * ACROSS
    chips = groups // 2
    runs = slabs // ZRUN
    halves = runs // XRUN
    rows = groups * own
    share = rows // slabs
    k = lax.axis_index("gz")
    me = lax.axis_index("af")
    chip, core = me // 2, me % 2
    run, z = k // ZRUN, k % ZRUN
    hi, xi = run // XRUN, run % XRUN
    place = k % (ZRUN * XRUN)
    ends = (k == 0) | (k == slabs - 1)
    border = ((place == 0) | (place == ZRUN * XRUN - 1)) & jnp.logical_not(ends)
    inland = jnp.logical_not(ends | border)
    sibling = {"af": chip * 2 + (1 - core)}
    chip_at = lambda d: {"af": lax.rem(chip + d, chips) * 2 + core}
    z_at = lambda d: {"gz": run * ZRUN + lax.rem(z + d, ZRUN)}
    x_at = lambda d: {"gz": (hi * XRUN + lax.rem(xi + d, XRUN)) * ZRUN + z}
    hi_at = lambda d: {"gz": (lax.rem(hi + d, halves) * XRUN + xi) * ZRUN + z}
    above = {"gz": lax.rem(k + 1, slabs)}
    below = {"gz": lax.rem(k + slabs - 1, slabs)}
    filled = TAPS * own
    wide = G.shape[0]
    inner = slice(ACROSS, ACROSS + cells)
    part = cells // PIECES
    step = height // PIECES
    columns = ((0, wide), (cut, wide))
    xbufs = ((XF0, XS0, XR0, ZF0, ZS0, ZR0, HS0, HR0), (XF1, XS1, XR1, ZF1, ZS1, ZR1, HS1, HR1))

    loads = []
    for i, (src, dst) in enumerate(
        ((og_hbm, og_ref), (pre_hbm, pre_ref), (w2_hbm, w2_ref), (in_hbm, in_ref), (w1_hbm, w1_ref))
    ):
        loads.append(pltpu.make_async_copy(src, dst, load_s.at[i]))
        loads[-1].start()

    peers = [sibling, above, below]
    peers += [chip_at(d) for d in range(1, chips)]
    peers += [z_at(d) for d in range(1, ZRUN)]
    peers += [x_at(d) for d in range(1, XRUN)]
    peers += [hi_at(d) for d in range(1, halves)]
    barrier = pltpu.get_barrier_semaphore()
    for peer in peers:
        pl.semaphore_signal(barrier, inc=1, device_id=peer, device_id_type=MESH)

    started = []

    def remote(src, dst, s, r, to):
        return pltpu.make_async_remote_copy(
            src_ref=src, dst_ref=dst, send_sem=s, recv_sem=r, device_id=to, device_id_type=MESH
        )

    def send(src, dst, s, r, to):
        copy = remote(src, dst, s, r, to)
        copy.start()
        started.append(copy)
        return copy

    def planes_of(ref):
        rel[...] = ref[...].astype(F32).reshape(own * height, ACROSS)
        return [rel[pl.ds(x, own, stride=height), :] for x in range(height)]

    def at_x(x):
        return slice(x * ACROSS, (x + 1) * ACROSS)

    def halo_copies(l, q):
        own_plane, low, high = (field.at[l, p, q] for p in (1, 0, 2))
        up = remote(own_plane, low, halo_s.at[l, q, 0], halo_r.at[l, q, 0], above)
        down = remote(own_plane, high, halo_s.at[l, q, 1], halo_r.at[l, q, 1], below)
        return up, down

    def halo_send(l, q):
        up, down = halo_copies(l, q)
        pl.when(k < slabs - 1)(up.start)
        pl.when(k > 0)(down.start)

    def halo_wait(l, q):
        up, down = halo_copies(l, q)
        pl.when(k > 0)(up.wait_recv)
        pl.when(k < slabs - 1)(down.wait_recv)

    def halo_done(l, q):
        up, down = halo_copies(l, q)
        pl.when(k < slabs - 1)(up.wait_send)
        pl.when(k > 0)(down.wait_send)

    def gather_copies(l, low, high):
        mine = U.at[l, me, pl.ds(low, high - low)]
        i = l if low == 0 else 2
        found = [
            remote(mine, mine, ag_s.at[i, d], ag_r.at[i, d], chip_at(d)) for d in range(1, chips)
        ]
        started.extend(found)
        return found

    def start_when(when, copies):
        @pl.when(when)
        def _():
            for copy in copies:
                copy.start()

    def gather_sibling(l):
        mine = U.at[l, me]
        return send(mine, mine, ag_s.at[l, 0], ag_r.at[l, 0], sibling)

    def gather_forward(l, *found):
        onward = []
        for d in range(1, chips):
            for copies in found:
                copies[d - 1].wait_recv()
            block = U.at[l, lax.rem(chip + chips - d, chips) * 2 + core]
            onward.append(
                send(block, block, ag_s.at[l, chips - 1 + d], ag_r.at[l, chips - 1 + d], sibling)
            )
        return onward

    def gather_finish(onward):
        for copy in onward:
            copy.wait_recv()

    def reorder(l):
        low, mid, top = share.bit_length() - 1, runs.bit_length() - 1, ZRUN.bit_length() - 1
        to_row = lax.broadcasted_iota(jnp.int32, (rows, rows), 0)
        from_row = lax.broadcasted_iota(jnp.int32, (rows, rows), 1)
        wanted = (
            (((to_row >> low) & (runs - 1)) << (low + top))
            | ((to_row >> (low + mid)) << low)
            | (to_row & (share - 1))
        )
        move = jnp.where(from_row == wanted, 1.0, 0.0).astype(BF)
        for n in range(0, cells, 256):
            block = U[l, :, :, n : n + 256].reshape(rows, 256)
            UP[:, n : n + 256] = jnp.dot(move, block, preferred_element_type=F32).astype(BF)

    def turn(l, w_ref):
        third = filled // 3
        blocks = [w_ref[(a + 1) * third : (a + 2) * third, :] for a in ORDER]
        full = jnp.concatenate(blocks + [jnp.zeros((wide - filled, rows), BF)], axis=0).T
        for g in range(groups):
            WT[l, g % 2, (g // 2) * own : (g // 2 + 1) * own, :] = full[g * own : (g + 1) * own, :]

    lane = lax.broadcasted_iota(jnp.int32, (own, ACROSS), 1)
    number = lambda a, b, c: 9 * ORDER.index(a) + 3 * (b + 1) + (c + 1)
    tap_rows = lambda t: slice(t * own, (t + 1) * own)

    def build(l, p, q):
        a = 1 - p
        for x in range(q * step, (q + 1) * step):
            v = field[l, p, q, :, at_x(x - q * step)].astype(F32)
            for c in (-1, 0, 1):
                if c == 0:
                    s = v
                else:
                    edge = 0 if c == 1 else ACROSS - 1
                    s = jnp.where(lane == edge, 0.0, pltpu.roll(v, c % ACROSS, 1))
                s = s.astype(BF)
                for b in (-1, 0, 1):
                    if 0 <= x + b < height:
                        G[tap_rows(number(a, b, c)), at_x(x + b + 1)] = s

    def grad_product(l, which, q, to):
        for n in range(0, part, 256):
            at = slice(ACROSS + q * part + n, ACROSS + q * part + n + 256)
            to[l, q, :, n : n + 256] = jnp.dot(
                WT[l, which], G[:, at], preferred_element_type=F32
            )

    def grad_first(l):
        copies = []
        for q in range(PIECES):
            grad_product(l, 1 - core, q, PB)
            copies.append(send(PB.at[l, q], PR.at[l, q], px_s.at[l, q], px_r.at[l, q], sibling))
        return copies

    def grad_own(l):
        for q in range(PIECES):
            grad_product(l, core, q, PS)

    def grad_second(l, q, copy):
        copy.wait_recv()
        for j in range(chips):
            at = slice(j * own, (j + 1) * own)
            total = PS[l, q, at, :] + PR[l, q, at, :]
            PS[l, q, at, :] = total
            SB[l, q, j] = total.astype(BF)
        return [
            send(
                SB.at[l, q, lax.rem(chip + d, chips)], SR.at[l, q, d - 1],
                y_s.at[l, q, d - 1], y_r.at[l, q, d - 1], chip_at(d),
            )
            for d in range(1, chips)
        ]

    def grad_last(l, q, found):
        for copy in found:
            copy.wait_recv()
        mine = pl.ds(pl.multiple_of(chip * own, own), own)
        total = PS[l, q, mine, :]
        for d in range(chips - 1):
            total = total + SR[l, q, d].astype(F32)
        return total

    def by_tap(total, out_ref):
        for block in range(TAPS):
            at = slice(block * own, (block + 1) * own)
            out_ref[9 * (ORDER[block // 9] + 1) + block % 9] = total[:, at]

    def z_first():
        for n in range(0, cut, 256):
            size = min(256, cut - n)
            at = slice(n, n + size)
            block = lax.dot_general(
                UP[...], G[n : n + size, inner], last_dims, preferred_element_type=F32
            ).reshape(ZRUN, runs * share, size)
            KF[:, :, at] = block
            KS[:, :, at] = block.astype(BF)
        return [
            send(
                KS.at[lax.rem(z + d, ZRUN)], KR.at[d - 1],
                k_s.at[d - 1], k_r.at[d - 1], z_at(d),
            )
            for d in range(1, ZRUN)
        ]

    def z_first_then(copies):
        for copy in copies:
            copy.wait_recv()
        for n in range(0, KF.shape[2], 128):
            at = slice(n, n + 128)
            total = KF[z, :, at]
            for d in range(ZRUN - 1):
                total = total + KR[d, :, at].astype(F32)
            for j in range(runs):
                h, x = divmod(j, XRUN)
                part_rows = total[j * share : (j + 1) * share, :]
                QS[x, h * share : (h + 1) * share, at] = part_rows
        return [
            send(
                QS.at[lax.rem(xi + d, XRUN)], QR.at[d - 1],
                q_s.at[d - 1], q_r.at[d - 1], x_at(d),
            )
            for d in range(1, XRUN)
        ]

    def z_first_pair(copies):
        for copy in copies:
            copy.wait_recv()
        total = QS[xi]
        for d in range(XRUN - 1):
            total = total + QR[d]
        for h in range(halves):
            HS1[h, :, :cut] = total[h * share : (h + 1) * share, :]

    def x_first(l):
        start, stop = columns[l]
        XF, XS, XR = xbufs[l][:3]
        for n in range(start, stop, 256):
            size = min(256, stop - n)
            at = slice(n - start, n - start + size)
            block = lax.dot_general(
                U[l].reshape(rows, cells), G[n : n + size, inner], last_dims,
                preferred_element_type=F32,
            )
            for h in range(halves):
                for x in range(XRUN):
                    j = (h * XRUN + x) * ZRUN * share
                    part = block[j : j + ZRUN * share, :]
                    XF[x, h, :, at] = part
                    XS[x, h, :, at] = part.astype(BF)
        return [
            send(
                XS.at[lax.rem(xi + d, XRUN)], XR.at[d - 1],
                xs.at[l, d - 1], xr.at[l, d - 1], x_at(d),
            )
            for d in range(1, XRUN)
        ]

    def x_first_then(l, copies):
        start, stop = columns[l]
        XF, XS, XR, ZF, ZS, ZR = xbufs[l][:6]
        eight = halves * share
        for copy in copies:
            copy.wait_recv()
        for n in range(0, stop - start, 128):
            at = slice(n, n + 128)
            fold, to = divmod(n, ZS.shape[2])
            to = slice(to, to + 128)
            for h in range(halves):
                total = XF[xi, h, :, at]
                for d in range(XRUN - 1):
                    total = total + XR[d, h, :, at].astype(F32)
                first = fold * eight + h * share
                for j in range(ZRUN):
                    ZF[j, first : first + share, to] = total[j * share : (j + 1) * share, :]
        for j in range(ZRUN):
            ZS[j] = ZF[j].astype(BF)
        return [
            send(
                ZS.at[lax.rem(z + d, ZRUN)], ZR.at[d - 1],
                zs.at[l, d - 1], zr.at[l, d - 1], z_at(d),
            )
            for d in range(1, ZRUN)
        ]

    def x_first_pair(l, copies):
        start, stop = columns[l]
        ZF, ZS, ZR, HS, HR = xbufs[l][3:]
        eight = halves * share
        for copy in copies:
            copy.wait_recv()
        total = ZF[z]
        for d in range(ZRUN - 1):
            total = total + ZR[d].astype(F32)
        fold = total.shape[1]
        for h in range(halves):
            HS[h, :, start : start + fold] = total[h * share : (h + 1) * share, :]
            rest = stop - start - fold
            HS[h, :, start + fold :] = total[eight + h * share : eight + (h + 1) * share, :rest]

    def last_start(l):
        HS, HR = xbufs[l][6:]
        return [
            send(
                HS.at[lax.rem(hi + d, halves)], HR.at[d - 1],
                hs.at[l, d - 1], hr.at[l, d - 1], hi_at(d),
            )
            for d in range(1, halves)
        ]

    def last_finish(l, copies, out_ref):
        HS, HR = xbufs[l][6:]
        for copy in copies:
            copy.wait_recv()
        total = HS[hi]
        for d in range(halves - 1):
            total = total + HR[d]
        by_tap(total, out_ref)

    loads[0].wait()
    for x, v in enumerate(planes_of(og_ref)):
        field[0, 1, x // step, :, at_x(x % step)] = v.astype(BF)

    @pl.when(k == 0)
    def _():
        for l in range(2):
            field[l, 0] = jnp.zeros(field.shape[2:], BF)

    @pl.when(k == slabs - 1)
    def _():
        for l in range(2):
            field[l, 2] = jnp.zeros(field.shape[2:], BF)

    pl.semaphore_wait(barrier, len(peers))
    for q in range(PIECES):
        halo_send(0, q)
    loads[1].wait()
    for x, v in enumerate(planes_of(pre_ref)):
        slope[x // step, :, at_x(x % step)] = jnp.where(v > 0, jnp.float32(1.0), jnp.float32(0.3))
        U[0, me, :, at_x(x)] = jnp.where(v > 0, v, 0.3 * v).astype(BF)
    gather_act = gather_copies(0, 0, own)
    start_when(jnp.logical_not(ends), gather_act)
    near_act = gather_sibling(0)
    loads[3].wait()
    for x, v in enumerate(planes_of(in_ref)):
        U[1, me, :, at_x(x)] = v.astype(BF)
    gather_in = gather_copies(1, 0, own // 2)
    start_when(inland, gather_in)

    none = jnp.zeros((own, ACROSS), BF)
    for a in (-1, 0, 1):
        for c in (-1, 0, 1):
            G[tap_rows(number(a, 1, c)), at_x(1)] = none
            G[tap_rows(number(a, -1, c)), at_x(height)] = none
    if wide > filled:
        G[filled:, :] = jnp.zeros((wide - filled, G.shape[1]), BF)

    def finish_taps(l):
        for q in range(PIECES):
            halo_wait(l, q)
            build(l, 0, q)
            build(l, 2, q)

    for q in range(PIECES):
        build(0, 1, q)
    loads[2].wait()
    turn(0, w2_ref)
    finish_taps(0)
    start_when(border, gather_in)
    pair = grad_first(0)
    grad_own(0)
    parts = [grad_second(0, q, pair[q]) for q in range(PIECES)]
    start_when(ends, gather_act + gather_in)
    onward = gather_forward(0, gather_act)
    loads[4].wait()
    turn(1, w1_ref)
    gather_finish(onward + [near_act])
    two = x_first(0)
    for q in range(PIECES):
        field[1, 1, q] = (grad_last(0, q, parts[q]) * slope[q]).astype(BF)
        halo_send(1, q)
    gather_rest = gather_copies(1, own // 2, own)
    for copy in gather_rest:
        copy.start()
    near_in = gather_sibling(1)
    for q in range(PIECES):
        build(1, 1, q)
    onward = gather_forward(1, gather_in, gather_rest)
    finish_taps(1)
    pair = grad_first(1)
    two = x_first_then(0, two)
    gather_finish(onward + [near_in])
    reorder(1)
    one_z = z_first()
    one_x = x_first(1)
    grad_own(1)
    parts = [grad_second(1, q, pair[q]) for q in range(PIECES)]
    x_first_pair(0, two)
    two = last_start(0)
    one_x = x_first_then(1, one_x)
    one_z = z_first_then(one_z)
    for q in range(PIECES):
        total = grad_last(1, q, parts[q])
        for x in range(step):
            rel[pl.ds(q * step + x, own, stride=height), :] = total[:, at_x(x)]
    ig_ref[...] = rel[...].reshape(own, height, ACROSS).astype(BF)
    last_finish(0, two, f2_ref)
    z_first_pair(one_z)
    x_first_pair(1, one_x)
    one = last_start(1)
    for l in range(2):
        for q in range(PIECES):
            halo_done(l, q)
    for copy in started:
        copy.wait_send()
    last_finish(1, one, f1_ref)


def body(slabs, groups, inputs, pre_acts, out_grad, weight_one, weight_two):
    own, planes, height, across = out_grad.shape
    channels = weight_one.shape[2]
    cells = height * across
    chips = groups // 2
    runs = slabs // ZRUN
    halves = runs // XRUN
    share = channels // slabs
    wide = -(-TAPS * own // 128) * 128
    cut = CUT
    flat = lambda v: v.reshape(own, height, across)
    taps = lambda w: jnp.transpose(w, (1, 0, 2)).reshape(TAPS * own, channels)
    results = [
        jax.ShapeDtypeStruct((own, height, across), BF),
        jax.ShapeDtypeStruct((TAPS, share, own), F32),
        jax.ShapeDtypeStruct((TAPS, share, own), F32),
    ]
    piece = cells // PIECES
    fold = lambda width: -(-width // 256) * 128
    scratch = [pltpu.VMEM((own, height, across), BF)] * 3
    scratch += [pltpu.VMEM((TAPS * own, channels), BF)] * 2
    scratch += [
        pltpu.VMEM((own * height, across), F32),
        pltpu.VMEM((PIECES, own, piece), F32),
        pltpu.VMEM((2, 3, PIECES, own, piece), BF),
        pltpu.VMEM((wide, cells + 2 * across), BF),
        pltpu.VMEM((2, 2, chips * own, wide), BF),
        pltpu.VMEM((2, groups, own, cells), BF),
        pltpu.VMEM((channels, cells), BF),
        pltpu.VMEM((2, PIECES, chips * own, piece), F32),
        pltpu.VMEM((2, PIECES, chips * own, piece), F32),
        pltpu.VMEM((2, PIECES, chips * own, piece), F32),
        pltpu.VMEM((2, PIECES, chips, own, piece), BF),
        pltpu.VMEM((2, PIECES, chips - 1, own, piece), BF),
    ]
    scratch += [
        pltpu.VMEM((ZRUN, runs * share, cut), F32),
        pltpu.VMEM((ZRUN, runs * share, cut), BF),
        pltpu.VMEM((ZRUN - 1, runs * share, cut), BF),
        pltpu.VMEM((XRUN, halves * share, cut), F32),
        pltpu.VMEM((XRUN - 1, halves * share, cut), F32),
    ]
    for width in (wide, wide - cut):
        scratch += [
            pltpu.VMEM((XRUN, halves, ZRUN * share, width), F32),
            pltpu.VMEM((XRUN, halves, ZRUN * share, width), BF),
            pltpu.VMEM((XRUN - 1, halves, ZRUN * share, width), BF),
            pltpu.VMEM((ZRUN, 2 * halves * share, fold(width)), F32),
            pltpu.VMEM((ZRUN, 2 * halves * share, fold(width)), BF),
            pltpu.VMEM((ZRUN - 1, 2 * halves * share, fold(width)), BF),
            pltpu.VMEM((halves, share, wide), F32),
            pltpu.VMEM((halves - 1, share, wide), F32),
        ]
    scratch.append(pltpu.SemaphoreType.DMA((5,)))
    for shape in (
        (2, PIECES, 2), (3, 2 * chips - 1), (2, PIECES), (2, PIECES, chips - 1), (ZRUN - 1,), (XRUN - 1,),
        (2, XRUN - 1), (2, ZRUN - 1), (2, halves - 1),
    ):
        scratch += [pltpu.SemaphoreType.DMA(shape), pltpu.SemaphoreType.DMA(shape)]
    arrays = (flat(inputs), flat(pre_acts), flat(out_grad), taps(weight_one), taps(weight_two))
    input_grad, one, two = pl.pallas_call(
        functools.partial(kernel, slabs, groups, own, height, cut),
        out_shape=results,
        in_specs=[pl.BlockSpec(memory_space=pltpu.HBM)] * 5,
        out_specs=[pl.BlockSpec(memory_space=pltpu.VMEM)] * 3,
        scratch_shapes=scratch,
        compiler_params=pltpu.CompilerParams(
            collective_id=0, has_side_effects=True, vmem_limit_bytes=48 * 1024 * 1024
        ),
        name="conv_back",
    )(*[pltpu.with_memory_space_constraint(v, pltpu.HBM) for v in arrays])
    return input_grad.reshape(own, planes, height, across), one, two


def solution(mesh):
    in_specs = (
        P("af", "gz", None, None),
        P("af", "gz", None, None),
        P("af", "gz", None, None),
        P("af", None, None),
        P("af", None, None),
    )
    out_specs = (P("af", "gz", None, None), P(None, "gz", "af"), P(None, "gz", "af"))
    return jax.shard_map(
        functools.partial(body, mesh.shape["gz"], mesh.shape["af"]),
        mesh=mesh, in_specs=in_specs, out_specs=out_specs, check_vma=False,
    )
```

```python
import functools

import jax
import jax.numpy as jnp
from jax import lax
from jax.experimental import pallas as pl
from jax.experimental.pallas import tpu as pltpu
from jax.sharding import PartitionSpec as P

MESH = pl.DeviceIdType.MESH
BF = jnp.bfloat16
F32 = jnp.float32
ZRUN = 8
XRUN = 4
CUT = 384
PIECES = 2
ORDER = (0, -1, 1)
TAPS = 27
ACROSS = 128
last_dims = (((1,), (1,)), ((), ()))


def kernel(
    slabs, groups, own, height, cut,
    in_hbm, pre_hbm, og_hbm, w1_hbm, w2_hbm,
    ig_ref, f1_ref, f2_ref,
    in_ref, pre_ref, og_ref, w1_ref, w2_ref,
    rel, slope, field, G, WT, U, UP, PB, PS, PR, SB, SR,
    KF, KS, KR, QS, QR,
    XF0, XS0, XR0, ZF0, ZS0, ZR0, HS0, HR0,
    XF1, XS1, XR1, ZF1, ZS1, ZR1, HS1, HR1,
    load_s, halo_s, halo_r, ag_s, ag_r, px_s, px_r, y_s, y_r, k_s, k_r, q_s, q_r,
    xs, xr, zs, zr, hs, hr,
):
    cells = height * ACROSS
    chips = groups // 2
    runs = slabs // ZRUN
    halves = runs // XRUN
    rows = groups * own
    share = rows // slabs
    k = lax.axis_index("gz")
    me = lax.axis_index("af")
    chip, core = me // 2, me % 2
    run, z = k // ZRUN, k % ZRUN
    hi, xi = run // XRUN, run % XRUN
    place = k % (ZRUN * XRUN)
    ends = (k == 0) | (k == slabs - 1)
    border = ((place == 0) | (place == ZRUN * XRUN - 1)) & jnp.logical_not(ends)
    inland = jnp.logical_not(ends | border)
    sibling = {"af": chip * 2 + (1 - core)}
    chip_at = lambda d: {"af": lax.rem(chip + d, chips) * 2 + core}
    z_at = lambda d: {"gz": run * ZRUN + lax.rem(z + d, ZRUN)}
    run_at = lambda d: {"gz": lax.rem(run + d, runs) * ZRUN + z}
    x_at = lambda d: {"gz": (hi * XRUN + lax.rem(xi + d, XRUN)) * ZRUN + z}
    hi_at = lambda d: {"gz": (lax.rem(hi + d, halves) * XRUN + xi) * ZRUN + z}
    above = {"gz": lax.rem(k + 1, slabs)}
    below = {"gz": lax.rem(k + slabs - 1, slabs)}
    filled = TAPS * own
    wide = G.shape[0]
    inner = slice(ACROSS, ACROSS + cells)
    part = cells // PIECES
    step = height // PIECES
    columns = ((0, wide), (cut, wide))
    xbufs = ((XF0, XS0, XR0, ZF0, ZS0, ZR0, HS0, HR0), (XF1, XS1, XR1, ZF1, ZS1, ZR1, HS1, HR1))

    loads = []
    for i, (src, dst) in enumerate(
        ((og_hbm, og_ref), (pre_hbm, pre_ref), (w2_hbm, w2_ref), (in_hbm, in_ref), (w1_hbm, w1_ref))
    ):
        loads.append(pltpu.make_async_copy(src, dst, load_s.at[i]))
        loads[-1].start()

    peers = [sibling, above, below]
    peers += [chip_at(d) for d in range(1, chips)]
    peers += [z_at(d) for d in range(1, ZRUN)]
    peers += [run_at(d) for d in range(1, runs)]
    barrier = pltpu.get_barrier_semaphore()
    for peer in peers:
        pl.semaphore_signal(barrier, inc=1, device_id=peer, device_id_type=MESH)

    started = []

    def remote(src, dst, s, r, to):
        return pltpu.make_async_remote_copy(
            src_ref=src, dst_ref=dst, send_sem=s, recv_sem=r, device_id=to, device_id_type=MESH
        )

    def send(src, dst, s, r, to):
        copy = remote(src, dst, s, r, to)
        copy.start()
        started.append(copy)
        return copy

    def planes_of(ref):
        rel[...] = ref[...].astype(F32).reshape(own * height, ACROSS)
        return [rel[pl.ds(x, own, stride=height), :] for x in range(height)]

    def at_x(x):
        return slice(x * ACROSS, (x + 1) * ACROSS)

    def halo_copies(l, q):
        own_plane, low, high = (field.at[l, p, q] for p in (1, 0, 2))
        up = remote(own_plane, low, halo_s.at[l, q, 0], halo_r.at[l, q, 0], above)
        down = remote(own_plane, high, halo_s.at[l, q, 1], halo_r.at[l, q, 1], below)
        return up, down

    def halo_send(l, q):
        up, down = halo_copies(l, q)
        pl.when(k < slabs - 1)(up.start)
        pl.when(k > 0)(down.start)

    def halo_wait(l, q):
        up, down = halo_copies(l, q)
        pl.when(k > 0)(up.wait_recv)
        pl.when(k < slabs - 1)(down.wait_recv)

    def halo_done(l, q):
        up, down = halo_copies(l, q)
        pl.when(k < slabs - 1)(up.wait_send)
        pl.when(k > 0)(down.wait_send)

    def gather_copies(l, low, high):
        mine = U.at[l, me, pl.ds(low, high - low)]
        i = l if low == 0 else 2
        found = [
            remote(mine, mine, ag_s.at[i, d], ag_r.at[i, d], chip_at(d)) for d in range(1, chips)
        ]
        started.extend(found)
        return found

    def start_when(when, copies):
        @pl.when(when)
        def _():
            for copy in copies:
                copy.start()

    def gather_sibling(l):
        mine = U.at[l, me]
        return send(mine, mine, ag_s.at[l, 0], ag_r.at[l, 0], sibling)

    def gather_forward(l, *found):
        onward = []
        for d in range(1, chips):
            for copies in found:
                copies[d - 1].wait_recv()
            block = U.at[l, lax.rem(chip + chips - d, chips) * 2 + core]
            onward.append(
                send(block, block, ag_s.at[l, chips - 1 + d], ag_r.at[l, chips - 1 + d], sibling)
            )
        return onward

    def gather_finish(onward):
        for copy in onward:
            copy.wait_recv()

    def reorder(l):
        low, mid, top = share.bit_length() - 1, runs.bit_length() - 1, ZRUN.bit_length() - 1
        to_row = lax.broadcasted_iota(jnp.int32, (rows, rows), 0)
        from_row = lax.broadcasted_iota(jnp.int32, (rows, rows), 1)
        wanted = (
            (((to_row >> low) & (runs - 1)) << (low + top))
            | ((to_row >> (low + mid)) << low)
            | (to_row & (share - 1))
        )
        move = jnp.where(from_row == wanted, 1.0, 0.0).astype(BF)
        for n in range(0, cells, 256):
            block = U[l, :, :, n : n + 256].reshape(rows, 256)
            UP[:, n : n + 256] = jnp.dot(move, block, preferred_element_type=F32).astype(BF)

    def turn(l, w_ref):
        third = filled // 3
        blocks = [w_ref[(a + 1) * third : (a + 2) * third, :] for a in ORDER]
        full = jnp.concatenate(blocks + [jnp.zeros((wide - filled, rows), BF)], axis=0).T
        for g in range(groups):
            WT[l, g % 2, (g // 2) * own : (g // 2 + 1) * own, :] = full[g * own : (g + 1) * own, :]

    lane = lax.broadcasted_iota(jnp.int32, (own, ACROSS), 1)
    number = lambda a, b, c: 9 * ORDER.index(a) + 3 * (b + 1) + (c + 1)
    tap_rows = lambda t: slice(t * own, (t + 1) * own)

    def build(l, p, q):
        a = 1 - p
        for x in range(q * step, (q + 1) * step):
            v = field[l, p, q, :, at_x(x - q * step)].astype(F32)
            for c in (-1, 0, 1):
                if c == 0:
                    s = v
                else:
                    edge = 0 if c == 1 else ACROSS - 1
                    s = jnp.where(lane == edge, 0.0, pltpu.roll(v, c % ACROSS, 1))
                s = s.astype(BF)
                for b in (-1, 0, 1):
                    if 0 <= x + b < height:
                        G[tap_rows(number(a, b, c)), at_x(x + b + 1)] = s

    def grad_product(l, which, q, to):
        for n in range(0, part, 256):
            at = slice(ACROSS + q * part + n, ACROSS + q * part + n + 256)
            block = jnp.dot(WT[l, which], G[:, at], preferred_element_type=F32)
            to[l, q, :, n : n + 256] = block.astype(to.dtype)

    def grad_first(l):
        copies = []
        for q in range(PIECES):
            grad_product(l, 1 - core, q, PB)
            copies.append(send(PB.at[l, q], PR.at[l, q], px_s.at[l, q], px_r.at[l, q], sibling))
        return copies

    def grad_own(l):
        for q in range(PIECES):
            grad_product(l, core, q, PS)

    def grad_second(l, q, copy):
        copy.wait_recv()
        for j in range(chips):
            at = slice(j * own, (j + 1) * own)
            total = PS[l, q, at, :] + PR[l, q, at, :].astype(F32)
            PS[l, q, at, :] = total
            SB[l, q, j] = total.astype(BF)
        return [
            send(
                SB.at[l, q, lax.rem(chip + d, chips)], SR.at[l, q, d - 1],
                y_s.at[l, q, d - 1], y_r.at[l, q, d - 1], chip_at(d),
            )
            for d in range(1, chips)
        ]

    def grad_last(l, q, found):
        for copy in found:
            copy.wait_recv()
        mine = pl.ds(pl.multiple_of(chip * own, own), own)
        total = PS[l, q, mine, :]
        for d in range(chips - 1):
            total = total + SR[l, q, d].astype(F32)
        return total

    def by_tap(total, start, out_ref):
        for i in range(total.shape[1] // own):
            block = start // own + i
            if block < TAPS:
                out_ref[9 * (ORDER[block // 9] + 1) + block % 9] = total[:, i * own : (i + 1) * own]

    def z_first():
        for n in range(0, cut, 256):
            size = min(256, cut - n)
            at = slice(n, n + size)
            block = lax.dot_general(
                UP[...], G[n : n + size, inner], last_dims, preferred_element_type=F32
            ).reshape(ZRUN, runs * share, size)
            KF[:, :, at] = block
            KS[:, :, at] = block.astype(BF)
        return [
            send(
                KS.at[lax.rem(z + d, ZRUN)], KR.at[d - 1],
                k_s.at[d - 1], k_r.at[d - 1], z_at(d),
            )
            for d in range(1, ZRUN)
        ]

    def z_first_then(copies):
        for copy in copies:
            copy.wait_recv()
        for n in range(0, KF.shape[2], 128):
            at = slice(n, n + 128)
            total = KF[z, :, at]
            for d in range(ZRUN - 1):
                total = total + KR[d, :, at].astype(F32)
            for j in range(runs):
                QS[j, :, at] = total[j * share : (j + 1) * share, :]
        return [
            send(
                QS.at[lax.rem(run + d, runs)], QR.at[d - 1],
                q_s.at[d - 1], q_r.at[d - 1], run_at(d),
            )
            for d in range(1, runs)
        ]

    def z_first_last(copies, out_ref):
        for copy in copies:
            copy.wait_recv()
        total = QS[run]
        for d in range(runs - 1):
            total = total + QR[d]
        by_tap(total, 0, out_ref)

    def x_first(l):
        start, stop = columns[l]
        XF, XS, XR = xbufs[l][:3]
        for n in range(start, stop, 256):
            size = min(256, stop - n)
            at = slice(n - start, n - start + size)
            block = lax.dot_general(
                U[l].reshape(rows, cells), G[n : n + size, inner], last_dims,
                preferred_element_type=F32,
            )
            for h in range(halves):
                for x in range(XRUN):
                    j = (h * XRUN + x) * ZRUN * share
                    part = block[j : j + ZRUN * share, :]
                    XF[x, h, :, at] = part
                    XS[x, h, :, at] = part.astype(BF)
        return [
            send(
                XS.at[lax.rem(xi + d, XRUN)], XR.at[d - 1],
                xs.at[l, d - 1], xr.at[l, d - 1], x_at(d),
            )
            for d in range(1, XRUN)
        ]

    def x_first_then(l, copies):
        start, stop = columns[l]
        XF, XS, XR, ZF, ZS, ZR = xbufs[l][:6]
        eight = halves * share
        for copy in copies:
            copy.wait_recv()
        for n in range(0, stop - start, 128):
            at = slice(n, n + 128)
            fold, to = divmod(n, ZS.shape[2])
            to = slice(to, to + 128)
            for h in range(halves):
                total = XF[xi, h, :, at]
                for d in range(XRUN - 1):
                    total = total + XR[d, h, :, at].astype(F32)
                first = fold * eight + h * share
                for j in range(ZRUN):
                    ZF[j, first : first + share, to] = total[j * share : (j + 1) * share, :]
        for j in range(ZRUN):
            ZS[j] = ZF[j].astype(BF)
        return [
            send(
                ZS.at[lax.rem(z + d, ZRUN)], ZR.at[d - 1],
                zs.at[l, d - 1], zr.at[l, d - 1], z_at(d),
            )
            for d in range(1, ZRUN)
        ]

    def x_first_pair(l, copies):
        start, stop = columns[l]
        ZF, ZS, ZR, HS, HR = xbufs[l][3:]
        eight = halves * share
        for copy in copies:
            copy.wait_recv()
        total = ZF[z]
        for d in range(ZRUN - 1):
            total = total + ZR[d].astype(F32)
        fold = total.shape[1]
        for h in range(halves):
            HS[h, :, :fold] = total[h * share : (h + 1) * share, :]
            rest = stop - start - fold
            HS[h, :, fold:] = total[eight + h * share : eight + (h + 1) * share, :rest]
        return [
            send(
                HS.at[lax.rem(hi + d, halves)], HR.at[d - 1],
                hs.at[l, d - 1], hr.at[l, d - 1], hi_at(d),
            )
            for d in range(1, halves)
        ]

    def x_first_last(l, copies, out_ref):
        start, stop = columns[l]
        HS, HR = xbufs[l][6:]
        for copy in copies:
            copy.wait_recv()
        total = HS[hi]
        for d in range(halves - 1):
            total = total + HR[d]
        by_tap(total, start, out_ref)

    loads[0].wait()
    for x, v in enumerate(planes_of(og_ref)):
        field[0, 1, x // step, :, at_x(x % step)] = v.astype(BF)

    @pl.when(k == 0)
    def _():
        for l in range(2):
            field[l, 0] = jnp.zeros(field.shape[2:], BF)

    @pl.when(k == slabs - 1)
    def _():
        for l in range(2):
            field[l, 2] = jnp.zeros(field.shape[2:], BF)

    pl.semaphore_wait(barrier, len(peers))
    for q in range(PIECES):
        halo_send(0, q)
    loads[1].wait()
    for x, v in enumerate(planes_of(pre_ref)):
        slope[x // step, :, at_x(x % step)] = jnp.where(v > 0, jnp.float32(1.0), jnp.float32(0.3))
        U[0, me, :, at_x(x)] = jnp.where(v > 0, v, 0.3 * v).astype(BF)
    gather_act = gather_copies(0, 0, own)
    start_when(jnp.logical_not(ends), gather_act)
    near_act = gather_sibling(0)
    loads[3].wait()
    for x, v in enumerate(planes_of(in_ref)):
        U[1, me, :, at_x(x)] = v.astype(BF)
    gather_in = gather_copies(1, 0, own // 2)
    start_when(inland, gather_in)

    none = jnp.zeros((own, ACROSS), BF)
    for a in (-1, 0, 1):
        for c in (-1, 0, 1):
            G[tap_rows(number(a, 1, c)), at_x(1)] = none
            G[tap_rows(number(a, -1, c)), at_x(height)] = none
    if wide > filled:
        G[filled:, :] = jnp.zeros((wide - filled, G.shape[1]), BF)

    def finish_taps(l):
        for q in range(PIECES):
            halo_wait(l, q)
            build(l, 0, q)
            build(l, 2, q)

    for q in range(PIECES):
        build(0, 1, q)
    loads[2].wait()
    turn(0, w2_ref)
    finish_taps(0)
    start_when(border, gather_in)
    pair = grad_first(0)
    grad_own(0)
    parts = [grad_second(0, q, pair[q]) for q in range(PIECES)]
    start_when(ends, gather_act + gather_in)
    onward = gather_forward(0, gather_act)
    loads[4].wait()
    turn(1, w1_ref)
    gather_finish(onward + [near_act])
    two = x_first(0)
    for q in range(PIECES):
        field[1, 1, q] = (grad_last(0, q, parts[q]) * slope[q]).astype(BF)
        halo_send(1, q)
    gather_rest = gather_copies(1, own // 2, own)
    for copy in gather_rest:
        copy.start()
    near_in = gather_sibling(1)
    for q in range(PIECES):
        build(1, 1, q)
    onward = gather_forward(1, gather_in, gather_rest)
    finish_taps(1)
    gather_finish(onward + [near_in])
    one_x = x_first(1)
    pair = grad_first(1)
    reorder(1)
    one_z = z_first()
    two = x_first_then(0, two)
    grad_own(1)
    parts = [grad_second(1, q, pair[q]) for q in range(PIECES)]
    one_x = x_first_then(1, one_x)
    one_z = z_first_then(one_z)
    two = x_first_pair(0, two)
    for q in range(PIECES):
        total = grad_last(1, q, parts[q])
        for x in range(step):
            rel[pl.ds(q * step + x, own, stride=height), :] = total[:, at_x(x)]
    ig_ref[...] = rel[...].reshape(own, height, ACROSS).astype(BF)
    one_x = x_first_pair(1, one_x)
    x_first_last(0, two, f2_ref)
    z_first_last(one_z, f1_ref)
    for l in range(2):
        for q in range(PIECES):
            halo_done(l, q)
    for copy in started:
        copy.wait_send()
    x_first_last(1, one_x, f1_ref)


def body(slabs, groups, inputs, pre_acts, out_grad, weight_one, weight_two):
    own, planes, height, across = out_grad.shape
    channels = weight_one.shape[2]
    cells = height * across
    chips = groups // 2
    runs = slabs // ZRUN
    halves = runs // XRUN
    share = channels // slabs
    wide = -(-TAPS * own // 128) * 128
    cut = CUT
    flat = lambda v: v.reshape(own, height, across)
    taps = lambda w: jnp.transpose(w, (1, 0, 2)).reshape(TAPS * own, channels)
    results = [
        jax.ShapeDtypeStruct((own, height, across), BF),
        jax.ShapeDtypeStruct((TAPS, share, own), F32),
        jax.ShapeDtypeStruct((TAPS, share, own), F32),
    ]
    piece = cells // PIECES
    fold = lambda width: -(-width // 256) * 128
    scratch = [pltpu.VMEM((own, height, across), BF)] * 3
    scratch += [pltpu.VMEM((TAPS * own, channels), BF)] * 2
    scratch += [
        pltpu.VMEM((own * height, across), F32),
        pltpu.VMEM((PIECES, own, piece), F32),
        pltpu.VMEM((2, 3, PIECES, own, piece), BF),
        pltpu.VMEM((wide, cells + 2 * across), BF),
        pltpu.VMEM((2, 2, chips * own, wide), BF),
        pltpu.VMEM((2, groups, own, cells), BF),
        pltpu.VMEM((channels, cells), BF),
        pltpu.VMEM((2, PIECES, chips * own, piece), BF),
        pltpu.VMEM((2, PIECES, chips * own, piece), F32),
        pltpu.VMEM((2, PIECES, chips * own, piece), BF),
        pltpu.VMEM((2, PIECES, chips, own, piece), BF),
        pltpu.VMEM((2, PIECES, chips - 1, own, piece), BF),
    ]
    scratch += [
        pltpu.VMEM((ZRUN, runs * share, cut), F32),
        pltpu.VMEM((ZRUN, runs * share, cut), BF),
        pltpu.VMEM((ZRUN - 1, runs * share, cut), BF),
        pltpu.VMEM((runs, share, cut), F32),
        pltpu.VMEM((runs - 1, share, cut), F32),
    ]
    for width in (wide, wide - cut):
        scratch += [
            pltpu.VMEM((XRUN, halves, ZRUN * share, width), F32),
            pltpu.VMEM((XRUN, halves, ZRUN * share, width), BF),
            pltpu.VMEM((XRUN - 1, halves, ZRUN * share, width), BF),
            pltpu.VMEM((ZRUN, 2 * halves * share, fold(width)), F32),
            pltpu.VMEM((ZRUN, 2 * halves * share, fold(width)), BF),
            pltpu.VMEM((ZRUN - 1, 2 * halves * share, fold(width)), BF),
            pltpu.VMEM((halves, share, width), F32),
            pltpu.VMEM((halves - 1, share, width), F32),
        ]
    scratch.append(pltpu.SemaphoreType.DMA((5,)))
    for shape in (
        (2, PIECES, 2), (3, 2 * chips - 1), (2, PIECES), (2, PIECES, chips - 1), (ZRUN - 1,), (runs - 1,),
        (2, XRUN - 1), (2, ZRUN - 1), (2, halves - 1),
    ):
        scratch += [pltpu.SemaphoreType.DMA(shape), pltpu.SemaphoreType.DMA(shape)]
    arrays = (flat(inputs), flat(pre_acts), flat(out_grad), taps(weight_one), taps(weight_two))
    input_grad, one, two = pl.pallas_call(
        functools.partial(kernel, slabs, groups, own, height, cut),
        out_shape=results,
        in_specs=[pl.BlockSpec(memory_space=pltpu.HBM)] * 5,
        out_specs=[pl.BlockSpec(memory_space=pltpu.VMEM)] * 3,
        scratch_shapes=scratch,
        compiler_params=pltpu.CompilerParams(
            collective_id=0, has_side_effects=True, vmem_limit_bytes=48 * 1024 * 1024
        ),
        name="conv_back",
    )(*[pltpu.with_memory_space_constraint(v, pltpu.HBM) for v in arrays])
    return input_grad.reshape(own, planes, height, across), one, two


def solution(mesh):
    in_specs = (
        P("af", "gz", None, None),
        P("af", "gz", None, None),
        P("af", "gz", None, None),
        P("af", None, None),
        P("af", None, None),
    )
    out_specs = (P("af", "gz", None, None), P(None, "gz", "af"), P(None, "gz", "af"))
    return jax.shard_map(
        functools.partial(body, mesh.shape["gz"], mesh.shape["af"]),
        mesh=mesh, in_specs=in_specs, out_specs=out_specs, check_vma=False,
    )
```

```python
import functools

import jax
import jax.numpy as jnp
from jax import lax
from jax.experimental import pallas as pl
from jax.experimental.pallas import tpu as pltpu
from jax.sharding import PartitionSpec as P

MESH = pl.DeviceIdType.MESH
BF = jnp.bfloat16
F32 = jnp.float32
ZRUN = 8
XRUN = 4
CUT = 256
PIECES = 2
ORDER = (0, -1, 1)
TAPS = 27
ACROSS = 128
last_dims = (((1,), (1,)), ((), ()))


def kernel(
    slabs, groups, own, height, cut,
    in_hbm, pre_hbm, og_hbm, w1_hbm, w2_hbm,
    ig_ref, f1_ref, f2_ref,
    in_ref, pre_ref, og_ref, w1_ref, w2_ref,
    rel, slope, field, G, WT, U, UP, PB, PS, PR, SB, SR,
    KF, KS, KR, QS, QR,
    XF0, XS0, XR0, ZF0, ZS0, ZR0, HS0, HR0,
    XF1, XS1, XR1, ZF1, ZS1, ZR1, HS1, HR1,
    load_s, halo_s, halo_r, ag_s, ag_r, px_s, px_r, y_s, y_r, k_s, k_r, q_s, q_r,
    xs, xr, zs, zr, hs, hr,
):
    cells = height * ACROSS
    chips = groups // 2
    runs = slabs // ZRUN
    halves = runs // XRUN
    rows = groups * own
    share = rows // slabs
    k = lax.axis_index("gz")
    me = lax.axis_index("af")
    chip, core = me // 2, me % 2
    run, z = k // ZRUN, k % ZRUN
    hi, xi = run // XRUN, run % XRUN
    place = k % (ZRUN * XRUN)
    ends = (k == 0) | (k == slabs - 1)
    border = ((place == 0) | (place == ZRUN * XRUN - 1)) & jnp.logical_not(ends)
    inland = jnp.logical_not(ends | border)
    sibling = {"af": chip * 2 + (1 - core)}
    chip_at = lambda d: {"af": lax.rem(chip + d, chips) * 2 + core}
    z_at = lambda d: {"gz": run * ZRUN + lax.rem(z + d, ZRUN)}
    run_at = lambda d: {"gz": lax.rem(run + d, runs) * ZRUN + z}
    x_at = lambda d: {"gz": (hi * XRUN + lax.rem(xi + d, XRUN)) * ZRUN + z}
    hi_at = lambda d: {"gz": (lax.rem(hi + d, halves) * XRUN + xi) * ZRUN + z}
    above = {"gz": lax.rem(k + 1, slabs)}
    below = {"gz": lax.rem(k + slabs - 1, slabs)}
    filled = TAPS * own
    wide = G.shape[0]
    inner = slice(ACROSS, ACROSS + cells)
    part = cells // PIECES
    step = height // PIECES
    columns = ((0, wide), (cut, wide))
    xbufs = ((XF0, XS0, XR0, ZF0, ZS0, ZR0, HS0, HR0), (XF1, XS1, XR1, ZF1, ZS1, ZR1, HS1, HR1))

    loads = []
    for i, (src, dst) in enumerate(
        ((og_hbm, og_ref), (pre_hbm, pre_ref), (w2_hbm, w2_ref), (in_hbm, in_ref), (w1_hbm, w1_ref))
    ):
        loads.append(pltpu.make_async_copy(src, dst, load_s.at[i]))
        loads[-1].start()

    peers = [sibling, above, below]
    peers += [chip_at(d) for d in range(1, chips)]
    peers += [z_at(d) for d in range(1, ZRUN)]
    peers += [run_at(d) for d in range(1, runs)]
    barrier = pltpu.get_barrier_semaphore()
    for peer in peers:
        pl.semaphore_signal(barrier, inc=1, device_id=peer, device_id_type=MESH)

    started = []

    def remote(src, dst, s, r, to):
        return pltpu.make_async_remote_copy(
            src_ref=src, dst_ref=dst, send_sem=s, recv_sem=r, device_id=to, device_id_type=MESH
        )

    def send(src, dst, s, r, to):
        copy = remote(src, dst, s, r, to)
        copy.start()
        started.append(copy)
        return copy

    def planes_of(ref):
        rel[...] = ref[...].astype(F32).reshape(own * height, ACROSS)
        return [rel[pl.ds(x, own, stride=height), :] for x in range(height)]

    def at_x(x):
        return slice(x * ACROSS, (x + 1) * ACROSS)

    def halo_copies(l, q):
        own_plane, low, high = (field.at[l, p, q] for p in (1, 0, 2))
        up = remote(own_plane, low, halo_s.at[l, q, 0], halo_r.at[l, q, 0], above)
        down = remote(own_plane, high, halo_s.at[l, q, 1], halo_r.at[l, q, 1], below)
        return up, down

    def halo_send(l, q):
        up, down = halo_copies(l, q)
        pl.when(k < slabs - 1)(up.start)
        pl.when(k > 0)(down.start)

    def halo_wait(l, q):
        up, down = halo_copies(l, q)
        pl.when(k > 0)(up.wait_recv)
        pl.when(k < slabs - 1)(down.wait_recv)

    def halo_done(l, q):
        up, down = halo_copies(l, q)
        pl.when(k < slabs - 1)(up.wait_send)
        pl.when(k > 0)(down.wait_send)

    def gather_copies(l, low, high):
        mine = U.at[l, me, pl.ds(low, high - low)]
        i = l if low == 0 else 2
        found = [
            remote(mine, mine, ag_s.at[i, d], ag_r.at[i, d], chip_at(d)) for d in range(1, chips)
        ]
        started.extend(found)
        return found

    def start_when(when, copies):
        @pl.when(when)
        def _():
            for copy in copies:
                copy.start()

    def gather_sibling(l):
        mine = U.at[l, me]
        return send(mine, mine, ag_s.at[l, 0], ag_r.at[l, 0], sibling)

    def gather_forward(l, *found):
        onward = []
        for d in range(1, chips):
            for copies in found:
                copies[d - 1].wait_recv()
            block = U.at[l, lax.rem(chip + chips - d, chips) * 2 + core]
            onward.append(
                send(block, block, ag_s.at[l, chips - 1 + d], ag_r.at[l, chips - 1 + d], sibling)
            )
        return onward

    def gather_finish(onward):
        for copy in onward:
            copy.wait_recv()

    def reorder(l):
        low, mid, top = share.bit_length() - 1, runs.bit_length() - 1, ZRUN.bit_length() - 1
        to_row = lax.broadcasted_iota(jnp.int32, (rows, rows), 0)
        from_row = lax.broadcasted_iota(jnp.int32, (rows, rows), 1)
        wanted = (
            (((to_row >> low) & (runs - 1)) << (low + top))
            | ((to_row >> (low + mid)) << low)
            | (to_row & (share - 1))
        )
        move = jnp.where(from_row == wanted, 1.0, 0.0).astype(BF)
        for n in range(0, cells, 256):
            block = U[l, :, :, n : n + 256].reshape(rows, 256)
            UP[:, n : n + 256] = jnp.dot(move, block, preferred_element_type=F32).astype(BF)

    def turn(l, w_ref):
        third = filled // 3
        blocks = [w_ref[(a + 1) * third : (a + 2) * third, :] for a in ORDER]
        full = jnp.concatenate(blocks + [jnp.zeros((wide - filled, rows), BF)], axis=0).T
        for g in range(groups):
            WT[l, g % 2, (g // 2) * own : (g // 2 + 1) * own, :] = full[g * own : (g + 1) * own, :]

    lane = lax.broadcasted_iota(jnp.int32, (own, ACROSS), 1)
    number = lambda a, b, c: 9 * ORDER.index(a) + 3 * (b + 1) + (c + 1)
    tap_rows = lambda t: slice(t * own, (t + 1) * own)

    def build(l, p, q):
        a = 1 - p
        for x in range(q * step, (q + 1) * step):
            v = field[l, p, q, :, at_x(x - q * step)].astype(F32)
            for c in (-1, 0, 1):
                if c == 0:
                    s = v
                else:
                    edge = 0 if c == 1 else ACROSS - 1
                    s = jnp.where(lane == edge, 0.0, pltpu.roll(v, c % ACROSS, 1))
                s = s.astype(BF)
                for b in (-1, 0, 1):
                    if 0 <= x + b < height:
                        G[tap_rows(number(a, b, c)), at_x(x + b + 1)] = s

    def grad_product(l, which, q, to):
        for n in range(0, part, 256):
            at = slice(ACROSS + q * part + n, ACROSS + q * part + n + 256)
            block = jnp.dot(WT[l, which], G[:, at], preferred_element_type=F32)
            to[l, q, :, n : n + 256] = block.astype(to.dtype)

    def grad_first(l):
        copies = []
        for q in range(PIECES):
            grad_product(l, 1 - core, q, PB)
            copies.append(send(PB.at[l, q], PR.at[l, q], px_s.at[l, q], px_r.at[l, q], sibling))
        return copies

    def grad_own(l):
        for q in range(PIECES):
            grad_product(l, core, q, PS)

    def grad_second(l, q, copy):
        copy.wait_recv()
        for j in range(chips):
            at = slice(j * own, (j + 1) * own)
            total = PS[l, q, at, :] + PR[l, q, at, :].astype(F32)
            PS[l, q, at, :] = total
            SB[l, q, j] = total.astype(BF)
        return [
            send(
                SB.at[l, q, lax.rem(chip + d, chips)], SR.at[l, q, d - 1],
                y_s.at[l, q, d - 1], y_r.at[l, q, d - 1], chip_at(d),
            )
            for d in range(1, chips)
        ]

    def grad_last(l, q, found):
        for copy in found:
            copy.wait_recv()
        mine = pl.ds(pl.multiple_of(chip * own, own), own)
        total = PS[l, q, mine, :]
        for d in range(chips - 1):
            total = total + SR[l, q, d].astype(F32)
        return total

    def by_tap(total, start, out_ref):
        for i in range(total.shape[1] // own):
            block = start // own + i
            if block < TAPS:
                out_ref[9 * (ORDER[block // 9] + 1) + block % 9] = total[:, i * own : (i + 1) * own]

    def z_first():
        for n in range(0, cut, 256):
            size = min(256, cut - n)
            at = slice(n, n + size)
            block = lax.dot_general(
                UP[...], G[n : n + size, inner], last_dims, preferred_element_type=F32
            ).reshape(ZRUN, runs * share, size)
            KF[:, :, at] = block
            KS[:, :, at] = block.astype(BF)
        return [
            send(
                KS.at[lax.rem(z + d, ZRUN)], KR.at[d - 1],
                k_s.at[d - 1], k_r.at[d - 1], z_at(d),
            )
            for d in range(1, ZRUN)
        ]

    def z_first_then(copies):
        for copy in copies:
            copy.wait_recv()
        for n in range(0, KF.shape[2], 128):
            at = slice(n, n + 128)
            total = KF[z, :, at]
            for d in range(ZRUN - 1):
                total = total + KR[d, :, at].astype(F32)
            for j in range(runs):
                QS[j, :, at] = total[j * share : (j + 1) * share, :]
        return [
            send(
                QS.at[lax.rem(run + d, runs)], QR.at[d - 1],
                q_s.at[d - 1], q_r.at[d - 1], run_at(d),
            )
            for d in range(1, runs)
        ]

    def z_first_last(copies, out_ref):
        for copy in copies:
            copy.wait_recv()
        total = QS[run]
        for d in range(runs - 1):
            total = total + QR[d]
        by_tap(total, 0, out_ref)

    def x_first(l):
        start, stop = columns[l]
        XF, XS, XR = xbufs[l][:3]
        for n in range(start, stop, 256):
            size = min(256, stop - n)
            at = slice(n - start, n - start + size)
            block = lax.dot_general(
                U[l].reshape(rows, cells), G[n : n + size, inner], last_dims,
                preferred_element_type=F32,
            )
            for h in range(halves):
                for x in range(XRUN):
                    j = (h * XRUN + x) * ZRUN * share
                    part = block[j : j + ZRUN * share, :]
                    XF[x, h, :, at] = part
                    XS[x, h, :, at] = part.astype(BF)
        return [
            send(
                XS.at[lax.rem(xi + d, XRUN)], XR.at[d - 1],
                xs.at[l, d - 1], xr.at[l, d - 1], x_at(d),
            )
            for d in range(1, XRUN)
        ]

    def x_first_then(l, copies):
        start, stop = columns[l]
        XF, XS, XR, ZF, ZS, ZR = xbufs[l][:6]
        eight = halves * share
        for copy in copies:
            copy.wait_recv()
        for n in range(0, stop - start, 128):
            at = slice(n, n + 128)
            fold, to = divmod(n, ZS.shape[2])
            to = slice(to, to + 128)
            for h in range(halves):
                total = XF[xi, h, :, at]
                for d in range(XRUN - 1):
                    total = total + XR[d, h, :, at].astype(F32)
                first = fold * eight + h * share
                for j in range(ZRUN):
                    ZF[j, first : first + share, to] = total[j * share : (j + 1) * share, :]
        for j in range(ZRUN):
            ZS[j] = ZF[j].astype(BF)
        return [
            send(
                ZS.at[lax.rem(z + d, ZRUN)], ZR.at[d - 1],
                zs.at[l, d - 1], zr.at[l, d - 1], z_at(d),
            )
            for d in range(1, ZRUN)
        ]

    def x_first_pair(l, copies):
        start, stop = columns[l]
        ZF, ZS, ZR, HS, HR = xbufs[l][3:]
        eight = halves * share
        for copy in copies:
            copy.wait_recv()
        total = ZF[z]
        for d in range(ZRUN - 1):
            total = total + ZR[d].astype(F32)
        fold = total.shape[1]
        for h in range(halves):
            HS[h, :, :fold] = total[h * share : (h + 1) * share, :]
            rest = stop - start - fold
            HS[h, :, fold:] = total[eight + h * share : eight + (h + 1) * share, :rest]
        return [
            send(
                HS.at[lax.rem(hi + d, halves)], HR.at[d - 1],
                hs.at[l, d - 1], hr.at[l, d - 1], hi_at(d),
            )
            for d in range(1, halves)
        ]

    def x_first_last(l, copies, out_ref):
        start, stop = columns[l]
        HS, HR = xbufs[l][6:]
        for copy in copies:
            copy.wait_recv()
        total = HS[hi]
        for d in range(halves - 1):
            total = total + HR[d]
        by_tap(total, start, out_ref)

    loads[0].wait()
    for x, v in enumerate(planes_of(og_ref)):
        field[0, 1, x // step, :, at_x(x % step)] = v.astype(BF)

    @pl.when(k == 0)
    def _():
        for l in range(2):
            field[l, 0] = jnp.zeros(field.shape[2:], BF)

    @pl.when(k == slabs - 1)
    def _():
        for l in range(2):
            field[l, 2] = jnp.zeros(field.shape[2:], BF)

    pl.semaphore_wait(barrier, len(peers))
    for q in range(PIECES):
        halo_send(0, q)
    loads[1].wait()
    for x, v in enumerate(planes_of(pre_ref)):
        slope[x // step, :, at_x(x % step)] = jnp.where(v > 0, jnp.float32(1.0), jnp.float32(0.3))
        U[0, me, :, at_x(x)] = jnp.where(v > 0, v, 0.3 * v).astype(BF)
    gather_act = gather_copies(0, 0, own)
    start_when(jnp.logical_not(ends), gather_act)
    near_act = gather_sibling(0)
    loads[3].wait()
    for x, v in enumerate(planes_of(in_ref)):
        U[1, me, :, at_x(x)] = v.astype(BF)
    gather_in = gather_copies(1, 0, own // 2)
    start_when(inland, gather_in)

    none = jnp.zeros((own, ACROSS), BF)
    for a in (-1, 0, 1):
        for c in (-1, 0, 1):
            G[tap_rows(number(a, 1, c)), at_x(1)] = none
            G[tap_rows(number(a, -1, c)), at_x(height)] = none
    if wide > filled:
        G[filled:, :] = jnp.zeros((wide - filled, G.shape[1]), BF)

    def finish_taps(l):
        for q in range(PIECES):
            halo_wait(l, q)
            build(l, 0, q)
            build(l, 2, q)

    for q in range(PIECES):
        build(0, 1, q)
    loads[2].wait()
    turn(0, w2_ref)
    finish_taps(0)
    start_when(border, gather_in)
    pair = grad_first(0)
    grad_own(0)
    parts = [grad_second(0, q, pair[q]) for q in range(PIECES)]
    start_when(ends, gather_act + gather_in)
    onward = gather_forward(0, gather_act)
    loads[4].wait()
    turn(1, w1_ref)
    gather_finish(onward + [near_act])
    two = x_first(0)
    for q in range(PIECES):
        field[1, 1, q] = (grad_last(0, q, parts[q]) * slope[q]).astype(BF)
        halo_send(1, q)
    gather_rest = gather_copies(1, own // 2, own)
    for copy in gather_rest:
        copy.start()
    near_in = gather_sibling(1)
    for q in range(PIECES):
        build(1, 1, q)
    onward = gather_forward(1, gather_in, gather_rest)
    finish_taps(1)
    pair = grad_first(1)
    two = x_first_then(0, two)
    gather_finish(onward + [near_in])
    one_x = x_first(1)
    reorder(1)
    one_z = z_first()
    grad_own(1)
    parts = [grad_second(1, q, pair[q]) for q in range(PIECES)]
    one_x = x_first_then(1, one_x)
    one_z = z_first_then(one_z)
    two = x_first_pair(0, two)
    for q in range(PIECES):
        total = grad_last(1, q, parts[q])
        for x in range(step):
            rel[pl.ds(q * step + x, own, stride=height), :] = total[:, at_x(x)]
    ig_ref[...] = rel[...].reshape(own, height, ACROSS).astype(BF)
    one_x = x_first_pair(1, one_x)
    x_first_last(0, two, f2_ref)
    z_first_last(one_z, f1_ref)
    for l in range(2):
        for q in range(PIECES):
            halo_done(l, q)
    for copy in started:
        copy.wait_send()
    x_first_last(1, one_x, f1_ref)


def body(slabs, groups, inputs, pre_acts, out_grad, weight_one, weight_two):
    own, planes, height, across = out_grad.shape
    channels = weight_one.shape[2]
    cells = height * across
    chips = groups // 2
    runs = slabs // ZRUN
    halves = runs // XRUN
    share = channels // slabs
    wide = -(-TAPS * own // 128) * 128
    cut = CUT
    flat = lambda v: v.reshape(own, height, across)
    taps = lambda w: jnp.transpose(w, (1, 0, 2)).reshape(TAPS * own, channels)
    results = [
        jax.ShapeDtypeStruct((own, height, across), BF),
        jax.ShapeDtypeStruct((TAPS, share, own), F32),
        jax.ShapeDtypeStruct((TAPS, share, own), F32),
    ]
    piece = cells // PIECES
    fold = lambda width: -(-width // 256) * 128
    scratch = [pltpu.VMEM((own, height, across), BF)] * 3
    scratch += [pltpu.VMEM((TAPS * own, channels), BF)] * 2
    scratch += [
        pltpu.VMEM((own * height, across), F32),
        pltpu.VMEM((PIECES, own, piece), F32),
        pltpu.VMEM((2, 3, PIECES, own, piece), BF),
        pltpu.VMEM((wide, cells + 2 * across), BF),
        pltpu.VMEM((2, 2, chips * own, wide), BF),
        pltpu.VMEM((2, groups, own, cells), BF),
        pltpu.VMEM((channels, cells), BF),
        pltpu.VMEM((2, PIECES, chips * own, piece), BF),
        pltpu.VMEM((2, PIECES, chips * own, piece), F32),
        pltpu.VMEM((2, PIECES, chips * own, piece), BF),
        pltpu.VMEM((2, PIECES, chips, own, piece), BF),
        pltpu.VMEM((2, PIECES, chips - 1, own, piece), BF),
    ]
    scratch += [
        pltpu.VMEM((ZRUN, runs * share, cut), F32),
        pltpu.VMEM((ZRUN, runs * share, cut), BF),
        pltpu.VMEM((ZRUN - 1, runs * share, cut), BF),
        pltpu.VMEM((runs, share, cut), F32),
        pltpu.VMEM((runs - 1, share, cut), F32),
    ]
    for width in (wide, wide - cut):
        scratch += [
            pltpu.VMEM((XRUN, halves, ZRUN * share, width), F32),
            pltpu.VMEM((XRUN, halves, ZRUN * share, width), BF),
            pltpu.VMEM((XRUN - 1, halves, ZRUN * share, width), BF),
            pltpu.VMEM((ZRUN, 2 * halves * share, fold(width)), F32),
            pltpu.VMEM((ZRUN, 2 * halves * share, fold(width)), BF),
            pltpu.VMEM((ZRUN - 1, 2 * halves * share, fold(width)), BF),
            pltpu.VMEM((halves, share, width), F32),
            pltpu.VMEM((halves - 1, share, width), F32),
        ]
    scratch.append(pltpu.SemaphoreType.DMA((5,)))
    for shape in (
        (2, PIECES, 2), (3, 2 * chips - 1), (2, PIECES), (2, PIECES, chips - 1), (ZRUN - 1,), (runs - 1,),
        (2, XRUN - 1), (2, ZRUN - 1), (2, halves - 1),
    ):
        scratch += [pltpu.SemaphoreType.DMA(shape), pltpu.SemaphoreType.DMA(shape)]
    arrays = (flat(inputs), flat(pre_acts), flat(out_grad), taps(weight_one), taps(weight_two))
    input_grad, one, two = pl.pallas_call(
        functools.partial(kernel, slabs, groups, own, height, cut),
        out_shape=results,
        in_specs=[pl.BlockSpec(memory_space=pltpu.HBM)] * 5,
        out_specs=[pl.BlockSpec(memory_space=pltpu.VMEM)] * 3,
        scratch_shapes=scratch,
        compiler_params=pltpu.CompilerParams(
            collective_id=0, has_side_effects=True, vmem_limit_bytes=48 * 1024 * 1024
        ),
        name="conv_back",
    )(*[pltpu.with_memory_space_constraint(v, pltpu.HBM) for v in arrays])
    return input_grad.reshape(own, planes, height, across), one, two


def solution(mesh):
    in_specs = (
        P("af", "gz", None, None),
        P("af", "gz", None, None),
        P("af", "gz", None, None),
        P("af", None, None),
        P("af", None, None),
    )
    out_specs = (P("af", "gz", None, None), P(None, "gz", "af"), P(None, "gz", "af"))
    return jax.shard_map(
        functools.partial(body, mesh.shape["gz"], mesh.shape["af"]),
        mesh=mesh, in_specs=in_specs, out_specs=out_specs, check_vma=False,
    )
```
